32 devices in a mesh: rep: 8 (over z, y), shard: 4 (over x, core).
Axes of the slice: x: 2, y: 2, z: 4, core: 2. Of those that a mesh axis runs over, the one named last changes fastest.
Arguments:
- tokens: bfloat16 [2048, 4096], P('rep'), may hold values from -6 to 6
- in_weight: bfloat16 [3, 4096, 2048], P(None, None, 'shard'), may hold values from -0.09375 to 0.09375
- kernel: float32 [7, 3, 2048], P(None, None, 'shard'), may hold values from -2.5 to 2.5
- out_grad: bfloat16 [2048, 2048], P('rep', 'shard'), may hold values from -6 to 6
Outputs:
- token_grad: bfloat16 [2048, 4096], P('rep', 'shard')
- weight_grad: float32 [12288, 2048], P('rep', 'shard')
- kernel_grad: float32 [7, 3, 2048], P(None, None, 'shard')
The draws below stay inside these ranges and needn't reach their ends.
All inputs are finite; a program needn't handle non-finite values.
Results may differ from the reference program's by a relative error of at most 0.0064.
Values sent between devices are 32-bit elements; how exact they have to be, the bound alone decides.
No kernel may reach another device: no remote copies, remote signals or barrier semaphores. Data moves between devices by JAX's collectives and lax.ppermute only.
A program may use at most 128 MiB of HBM per device.

```python
import jax
import jax.numpy as jnp
from jax import lax

D = 4096
CH = 2048
KER = 7
SEQ = 128
TOKENS = 2048


def shard_levels(key, dims, shards, least, largest):
    factor_of = 1.0
    for dim, shards_of in shards:
        draws = jax.random.uniform(jax.random.fold_in(jax.random.fold_in(key, 6), dim), (shards_of,), jnp.float32, least / len(shards), largest / len(shards))
        factor_of = factor_of * jnp.repeat(jnp.exp(draws), dims[dim] // shards_of).reshape((-1,) + (1,) * (len(dims) - 1 - dim))
    return factor_of


def bell_draw(key, extent, spread, most, cuts=(), kind=jnp.bfloat16):
    values = jax.random.normal(key, extent, jnp.float32) * spread
    if len(cuts) > 0:
        values = shard_levels(key, extent, cuts, -0.22, 0.18) * values
    return jnp.clip(values, min=-most, max=most).astype(kind)


def setup_inputs(seed: int = 0) -> dict:
    arg_keys = jax.random.split(jax.random.key(seed), 5)
    return {
        "tokens": bell_draw(arg_keys[0], (TOKENS, D), 1.0, 6.0, ((0, 8),)),
        "in_weight": bell_draw(arg_keys[1], (3, D, CH), D ** -0.5, 0.09375, ((2, 4),)),
        "kernel": bell_draw(arg_keys[2], (KER, 3, CH), 0.4, 2.5, ((2, 4),), jnp.float32),
        "out_grad": bell_draw(arg_keys[3], (TOKENS, CH), 1.0, 6.0, ((0, 8), (1, 4))),
    }


def causal_mix(values, kernel):
    width = kernel.shape[0]
    length = values.shape[1]
    padded = jnp.pad(values, ((0, 0), (width - 1, 0), (0, 0), (0, 0)))
    total = jnp.zeros_like(values)
    for offset in range(width):
        total = total + kernel[offset] * padded[:, width - 1 - offset:width - 1 - offset + length]
    return total

def causal_mix_back(grads, kernel):
    width = kernel.shape[0]
    length = grads.shape[1]
    padded = jnp.pad(grads, ((0, 0), (0, width - 1), (0, 0), (0, 0)))
    total = jnp.zeros_like(grads)
    for offset in range(width):
        total = total + kernel[offset] * padded[:, offset:offset + length]
    return total

def kernel_terms(values, grads, width):
    length = values.shape[1]
    padded = jnp.pad(values, ((0, 0), (width - 1, 0), (0, 0), (0, 0)))
    terms = []
    for offset in range(width):
        shifted = padded[:, width - 1 - offset:width - 1 - offset + length]
        terms.append(lax.optimization_barrier(jnp.sum(shifted * grads, axis=(0, 1))))
    return jnp.stack(terms, axis=0)

def reference(tokens, in_weight, kernel, out_grad):
    high = lax.Precision.HIGHEST
    tokens_wide = tokens.astype(jnp.float32)
    weight_wide = in_weight.astype(jnp.float32)
    mixed = jnp.einsum('td,sdc->tsc', tokens_wide, weight_wide, precision=high)
    stored = lax.optimization_barrier(mixed.astype(jnp.bfloat16))
    values = stored.astype(jnp.float32).reshape(TOKENS // SEQ, SEQ, 3, CH)
    conv = causal_mix(values, kernel)
    query = conv[:, :, 0]
    keyed = conv[:, :, 1]
    valued = conv[:, :, 2]
    upstream = out_grad.astype(jnp.float32).reshape(TOKENS // SEQ, SEQ, CH)
    conv_grad = jnp.stack([upstream * keyed * valued, upstream * query * valued, upstream * query * keyed], axis=2)
    mixed_grad = causal_mix_back(conv_grad, kernel).reshape(TOKENS, 3, CH).astype(jnp.bfloat16)
    scale = 1.0 / jnp.sqrt(jnp.float32(TOKENS))
    kernel_grad = kernel_terms(values, conv_grad, KER) * scale
    grad_wide = mixed_grad.astype(jnp.float32)
    token_grad = jnp.einsum('tsc,sdc->td', grad_wide, weight_wide, precision=high).astype(jnp.bfloat16)
    weight_grad = jnp.einsum('td,tsc->sdc', tokens_wide, grad_wide, precision=high) * scale
    return (token_grad, weight_grad.reshape(3 * D, CH), kernel_grad)
```

```python
import functools
import math

import jax
import jax.numpy as jnp
from jax import lax
from jax.experimental import pallas as pl
from jax.experimental.pallas import tpu as pltpu
from jax.sharding import PartitionSpec as P

SEQ = 128


def causal_mix(values, kernel):
    width = kernel.shape[0]
    length = values.shape[1]
    padded = jnp.pad(values, ((0, 0), (width - 1, 0), (0, 0), (0, 0)))
    total = jnp.zeros_like(values)
    for offset in range(width):
        total = total + kernel[offset] * padded[:, width - 1 - offset : width - 1 - offset + length]
    return total


def causal_mix_back(grads, kernel):
    width = kernel.shape[0]
    length = grads.shape[1]
    padded = jnp.pad(grads, ((0, 0), (0, width - 1), (0, 0), (0, 0)))
    total = jnp.zeros_like(grads)
    for offset in range(width):
        total = total + kernel[offset] * padded[:, offset : offset + length]
    return total


def kernel_terms(values, grads, width):
    length = values.shape[1]
    padded = jnp.pad(values, ((0, 0), (width - 1, 0), (0, 0), (0, 0)))
    terms = []
    for offset in range(width):
        shifted = padded[:, width - 1 - offset : width - 1 - offset + length]
        terms.append(jnp.sum(shifted * grads, axis=(0, 1)))
    return jnp.stack(terms, axis=0)


def gated_grads(tokens, in_weight, kernel, out_grad):
    rows = tokens.shape[0]
    chans = in_weight.shape[2]
    mixed = jnp.einsum("td,sdc->tsc", tokens, in_weight, preferred_element_type=jnp.float32)
    stored = lax.optimization_barrier(mixed.astype(jnp.bfloat16))
    values = stored.astype(jnp.float32).reshape(rows // SEQ, SEQ, 3, chans)
    conv = causal_mix(values, kernel)
    query = conv[:, :, 0]
    keyed = conv[:, :, 1]
    valued = conv[:, :, 2]
    upstream = out_grad.astype(jnp.float32).reshape(rows // SEQ, SEQ, chans)
    conv_grad = jnp.stack(
        [upstream * keyed * valued, upstream * query * valued, upstream * query * keyed], axis=2
    )
    mixed_grad = causal_mix_back(conv_grad, kernel).reshape(rows, 3, chans)
    return mixed_grad, kernel_terms(values, conv_grad, kernel.shape[0])


def plain(tokens, in_weight, kernel, out_grad):
    features = tokens.shape[1]
    chans = in_weight.shape[2]
    scale = 1.0 / math.sqrt(tokens.shape[0] * lax.axis_size("rep"))
    wide_grad, taps = gated_grads(tokens, in_weight, kernel, out_grad)
    mixed_grad = wide_grad.astype(jnp.bfloat16)
    partial_grad = jnp.einsum(
        "tsc,sdc->td", mixed_grad, in_weight, preferred_element_type=jnp.float32
    )
    token_grad = lax.psum_scatter(partial_grad, "shard", scatter_dimension=1, tiled=True).astype(
        jnp.bfloat16
    )
    local_grad = (
        jnp.einsum("td,tsc->sdc", tokens, mixed_grad, preferred_element_type=jnp.float32) * scale
    )
    weight_grad = lax.psum_scatter(
        local_grad.reshape(3 * features, chans), "rep", scatter_dimension=0, tiled=True
    )
    kernel_grad = lax.psum(taps * scale, "rep")
    return (token_grad, weight_grad, kernel_grad)


LEVELS = 4
BLOCK = 512


def along(array, levels, shift):
    perm = [(2 * z + y, 2 * (z + shift) + y) for z in levels for y in range(2)]
    return lax.ppermute(array, "rep", perm) if perm else None


def spread(array, needed):
    ups, downs = [], []
    for going, out in ((1, ups), (-1, downs)):
        now = array
        for step in range(LEVELS - 1):
            if going == 1:
                levels = [z for z in range(step, LEVELS - 1) if z + 1 <= max(needed)]
            else:
                levels = [z for z in range(1, LEVELS - step) if z - 1 >= min(needed)]
            now = along(now, levels, going) if levels else None
            if now is None:
                break
            out.append(now)
    return ups, downs


def source(level, slot):
    if slot == 1:
        return ("up", 1) if level >= 2 else ("down", 1)
    if slot == 2:
        return ("up", 2) if level >= 2 else ("down", 2)
    return (("down", 3), ("up", 1), ("down", 1), ("up", 3))[level]


def gather_tokens_body(rows, place, own, p1, p2, s1, s3, out, held):
    level, quarter = place[0], place[2]
    part = rows // 4
    inner = jnp.logical_or(level == 1, level == 2)
    for j in range(6):
        cols = slice(BLOCK * j, BLOCK * (j + 1))
        block = lax.rem(6 * level + j, 8)
        column = pl.ds(pl.multiple_of(block * BLOCK, BLOCK), BLOCK)
        held[0:rows, :] = own[:, column].astype(jnp.float32)
        for k in range(4):
            where = pl.multiple_of(jnp.bitwise_xor(quarter, k) * part, part)
            held[pl.ds(rows + where, part), :] = p1[k][:, cols]
            held[pl.ds(2 * rows + where, part), :] = p2[k][:, cols]

            @pl.when(inner)
            def _():
                held[pl.ds(3 * rows + where, part), :] = s1[k][:, cols]

            @pl.when(jnp.logical_not(inner))
            def _():
                held[pl.ds(3 * rows + where, part), :] = s3[k][:, cols]

        out[j] = held[...].T.astype(jnp.bfloat16)


def gather_tokens(place, own, slots):
    rows = own.shape[0]

    def body(place, own, *refs):
        groups = [refs[4 * i : 4 * i + 4] for i in range(4)]
        gather_tokens_body(rows, place, own, *groups, refs[16], refs[17])

    return pl.pallas_call(
        body,
        out_shape=jax.ShapeDtypeStruct((6, BLOCK, 4 * rows), jnp.bfloat16),
        in_specs=[pl.BlockSpec(memory_space=pltpu.SMEM)]
        + [pl.BlockSpec(memory_space=pltpu.VMEM)] * 17,
        out_specs=pl.BlockSpec(memory_space=pltpu.VMEM),
        scratch_shapes=[pltpu.VMEM((4 * rows, BLOCK), jnp.float32)],
        compiler_params=pltpu.CompilerParams(vmem_limit_bytes=48 * 2**20),
        name="arrange_tokens",
    )(place, own, *[piece for slot in slots for piece in slot])


def weight_part(place, tok, own, moved, names):
    rows = own.shape[1]
    width = own.shape[2]

    def body(place, tok, own, *refs):
        send, keep, held = refs[-3], refs[-2], refs[-1]
        table = dict(zip(names, refs[:-3]))
        level, column = place[0], place[1]
        for z in range(LEVELS):

            @pl.when(level == z)
            def _():
                low = (6 * z) // 8
                for side, stream in enumerate((low, min(low + 1, (6 * z + 5) // 8))):
                    held[side, 0:rows, :] = own[stream].astype(jnp.bfloat16)
                    for slot in (1, 2, 3):
                        way, far = source(z, slot)
                        held[side, slot * rows : (slot + 1) * rows, :] = table[(stream, way, far)][
                            ...
                        ].astype(jnp.bfloat16)

        low = lax.div(6 * level, 8)
        for i in range(3):
            for out, col in ((send, 1 - column), (keep, column)):
                j = 3 * col + i
                side = lax.div(6 * level + j, 8) - low
                out[BLOCK * i : BLOCK * (i + 1), :] = jnp.dot(
                    tok[j], held[side], preferred_element_type=jnp.float32
                )

    half = jax.ShapeDtypeStruct((3 * BLOCK, width), jnp.float32)
    return pl.pallas_call(
        body,
        out_shape=(half, half),
        in_specs=[pl.BlockSpec(memory_space=pltpu.SMEM)]
        + [pl.BlockSpec(memory_space=pltpu.VMEM)] * (2 + len(names)),
        out_specs=(pl.BlockSpec(memory_space=pltpu.VMEM),) * 2,
        scratch_shapes=[pltpu.VMEM((2, 4 * rows, width), jnp.bfloat16)],
        compiler_params=pltpu.CompilerParams(vmem_limit_bytes=48 * 2**20),
        name="weight_part",
    )(place, tok, own, *[moved[name] for name in names])


CHUNKS = 2


def lined(tokens, in_weight, kernel, out_grad):
    rows, features = tokens.shape
    chans = in_weight.shape[2]
    rep = lax.axis_index("rep")
    quarter = lax.axis_index("shard")
    level, column = rep // 2, rep % 2
    place = jnp.stack([level, column, quarter]).astype(jnp.int32)
    scale = 1.0 / math.sqrt(rows * lax.axis_size("rep"))
    part = rows // 4
    wide = features // 4
    upper = level >= 2

    piece = lax.dynamic_slice(tokens, (quarter * part, 0), (part, features)).astype(jnp.float32)
    ups, downs = {}, {}
    for k in range(4):
        needed = [z for z in range(LEVELS) if any((3 * z + i) % 4 == k for i in range(3))]
        ups[k], downs[k] = spread(piece[:, wide * k : wide * (k + 1)], needed)

    def chosen(use_up, far_up, far_down):
        whole = []
        for k in range(4):
            up = ups[k][far_up - 1] if len(ups[k]) >= far_up else None
            down = downs[k][far_down - 1] if len(downs[k]) >= far_down else None
            if up is None:
                up = down
            if down is None:
                down = up
            whole.append(jnp.where(use_up, up, down))
        doubled = jnp.concatenate(whole + whole[:2], axis=1)
        return lax.dynamic_slice(doubled, (0, wide * ((3 * level) % 4)), (part, 3 * wide))

    def share(array, levels):
        def pairs(flip):
            return [
                (4 * (2 * z + y) + q, 4 * (2 * z + y) + (q ^ flip))
                for z in levels
                for y in range(2)
                for q in range(4)
            ]

        across = lax.ppermute(array, ("rep", "shard"), pairs(2))
        beside = lax.ppermute(array, ("rep", "shard"), pairs(1))
        both = lax.ppermute(across, ("rep", "shard"), pairs(1))
        return (array, beside, across, both)

    slots = [
        share(chosen(upper, 1, 1), range(LEVELS)),
        share(chosen(upper, 2, 2), range(LEVELS)),
        share(chosen(level == 1, 1, 1), (1, 2)),
        share(chosen(level == 3, 3, 3), (0, 3)),
    ]

    wide_grad, taps = gated_grads(tokens, in_weight, kernel, out_grad)
    wide_grad = jnp.transpose(wide_grad, (1, 0, 2))

    tok = gather_tokens(place, tokens, slots)
    got = []
    cw = chans // CHUNKS
    for h in range(CHUNKS):
        moved = {}
        mine = wide_grad[:, :, cw * h : cw * (h + 1)]
        for stream in range(3):
            needed = [
                z for z in range(LEVELS) if (6 * z) // 8 <= stream <= (6 * z + 5) // 8
            ]
            up, down = spread(mine[stream], needed)
            for i, array in enumerate(up):
                moved[(stream, "up", i + 1)] = array
            for i, array in enumerate(down):
                moved[(stream, "down", i + 1)] = array
        used = set()
        for z in range(LEVELS):
            for stream in {(6 * z) // 8, (6 * z + 5) // 8}:
                for slot in (1, 2, 3):
                    used.add((stream,) + source(z, slot))
        names = sorted(used)
        send, keep = weight_part(place, tok, mine, moved, names)
        other = lax.ppermute(send, "rep", [(r, r ^ 1) for r in range(2 * LEVELS)])
        got.append((keep + other) * scale)
    weight_grad = jnp.concatenate(got, axis=1)

    mixed_grad = wide_grad.astype(jnp.bfloat16)
    partial = jnp.einsum("stc,sdc->td", mixed_grad, in_weight, preferred_element_type=jnp.float32)
    partial = partial.reshape(rows, 2, 2, wide)
    core, side = quarter % 2, quarter // 2
    pick = lambda array, index, axis: lax.dynamic_index_in_dim(array, index, axis, keepdims=False)
    first = pick(partial, core, 2) + lax.ppermute(
        pick(partial, 1 - core, 2), "shard", [(q, q ^ 1) for q in range(4)]
    )
    token_grad = pick(first, side, 1) + lax.ppermute(
        pick(first, 1 - side, 1), "shard", [(q, q ^ 2) for q in range(4)]
    )

    for bit in (1, 2, 4):
        taps = taps + lax.ppermute(taps, "rep", [(r, r ^ bit) for r in range(2 * LEVELS)])
    return (token_grad.astype(jnp.bfloat16), weight_grad, taps * scale)


def solution(mesh):
    placed = (P("rep", None), P(None, None, "shard"), P(None, None, "shard"), P("rep", "shard"))
    line = mesh.shape["rep"] == 2 * LEVELS and mesh.shape["shard"] == 4
    return jax.shard_map(
        lined if line else plain,
        mesh=mesh,
        in_specs=placed,
        out_specs=(P("rep", "shard"), P("rep", "shard"), P(None, None, "shard")),
        check_vma=False,
    )
```

```python
import functools
import math

import jax
import jax.numpy as jnp
from jax import lax
from jax.experimental import pallas as pl
from jax.experimental.pallas import tpu as pltpu
from jax.sharding import PartitionSpec as P

SEQ = 128


def causal_mix(values, kernel):
    width = kernel.shape[0]
    length = values.shape[1]
    padded = jnp.pad(values, ((0, 0), (width - 1, 0), (0, 0), (0, 0)))
    total = jnp.zeros_like(values)
    for offset in range(width):
        total = total + kernel[offset] * padded[:, width - 1 - offset : width - 1 - offset + length]
    return total


def causal_mix_back(grads, kernel):
    width = kernel.shape[0]
    length = grads.shape[1]
    padded = jnp.pad(grads, ((0, 0), (0, width - 1), (0, 0), (0, 0)))
    total = jnp.zeros_like(grads)
    for offset in range(width):
        total = total + kernel[offset] * padded[:, offset : offset + length]
    return total


def kernel_terms(values, grads, width):
    length = values.shape[1]
    padded = jnp.pad(values, ((0, 0), (width - 1, 0), (0, 0), (0, 0)))
    terms = []
    for offset in range(width):
        shifted = padded[:, width - 1 - offset : width - 1 - offset + length]
        terms.append(jnp.sum(shifted * grads, axis=(0, 1)))
    return jnp.stack(terms, axis=0)


def gated_grads(tokens, in_weight, kernel, out_grad):
    rows = tokens.shape[0]
    chans = in_weight.shape[2]
    mixed = jnp.einsum("td,sdc->tsc", tokens, in_weight, preferred_element_type=jnp.float32)
    stored = lax.optimization_barrier(mixed.astype(jnp.bfloat16))
    values = stored.astype(jnp.float32).reshape(rows // SEQ, SEQ, 3, chans)
    conv = causal_mix(values, kernel)
    query = conv[:, :, 0]
    keyed = conv[:, :, 1]
    valued = conv[:, :, 2]
    upstream = out_grad.astype(jnp.float32).reshape(rows // SEQ, SEQ, chans)
    conv_grad = jnp.stack(
        [upstream * keyed * valued, upstream * query * valued, upstream * query * keyed], axis=2
    )
    mixed_grad = causal_mix_back(conv_grad, kernel).reshape(rows, 3, chans)
    return mixed_grad, kernel_terms(values, conv_grad, kernel.shape[0])


def plain(tokens, in_weight, kernel, out_grad):
    features = tokens.shape[1]
    chans = in_weight.shape[2]
    scale = 1.0 / math.sqrt(tokens.shape[0] * lax.axis_size("rep"))
    wide_grad, taps = gated_grads(tokens, in_weight, kernel, out_grad)
    mixed_grad = wide_grad.astype(jnp.bfloat16)
    partial_grad = jnp.einsum(
        "tsc,sdc->td", mixed_grad, in_weight, preferred_element_type=jnp.float32
    )
    token_grad = lax.psum_scatter(partial_grad, "shard", scatter_dimension=1, tiled=True).astype(
        jnp.bfloat16
    )
    local_grad = (
        jnp.einsum("td,tsc->sdc", tokens, mixed_grad, preferred_element_type=jnp.float32) * scale
    )
    weight_grad = lax.psum_scatter(
        local_grad.reshape(3 * features, chans), "rep", scatter_dimension=0, tiled=True
    )
    kernel_grad = lax.psum(taps * scale, "rep")
    return (token_grad, weight_grad, kernel_grad)


LEVELS = 4
BLOCK = 512
BLOCKS = 8
OWN = 6
VMEM = pl.BlockSpec(memory_space=pltpu.VMEM)
SMEM = pl.BlockSpec(memory_space=pltpu.SMEM)
PARAMS = pltpu.CompilerParams(vmem_limit_bytes=48 * 2**20)


def lines(array, hops):
    perm = [(2 * a + y, 2 * b + y) for a, b in hops for y in range(2)]
    return lax.ppermute(array, "rep", perm)


PAIRS = ((0, 1), (1, 0), (2, 3), (3, 2))
INWARD = ((0, 1), (3, 2))
MIDDLE = ((1, 2), (2, 1))
OUTWARD = ((1, 0), (2, 3))


def turn_tokens(place, tokens):
    rows = tokens.shape[0]
    slab = BLOCK // 4

    def body(place, tokens, whole, piece):
        start = pl.multiple_of(place[2] * slab, slab)
        for b in range(BLOCKS):
            whole[b] = tokens[:, BLOCK * b : BLOCK * (b + 1)].T
            piece[b] = tokens[:, pl.ds(pl.multiple_of(BLOCK * b + start, slab), slab)].astype(
                jnp.float32
            ).T

    return pl.pallas_call(
        body,
        out_shape=(
            jax.ShapeDtypeStruct((BLOCKS, BLOCK, rows), jnp.bfloat16),
            jax.ShapeDtypeStruct((BLOCKS, slab, rows), jnp.float32),
        ),
        in_specs=[SMEM, VMEM],
        out_specs=(VMEM, VMEM),
        compiler_params=PARAMS,
        name="turn_tokens",
    )(place, tokens)


def arrange_tokens(place, whole, slots):
    rows = whole.shape[2]
    slab = BLOCK // 4

    def body(place, whole, *refs):
        out = refs[-1]
        for j in range(OWN):
            out[j, :, 0:rows] = whole[lax.rem(OWN * place[0] + j, BLOCKS)]
            for slot in range(3):
                for k in range(4):
                    where = pl.multiple_of(jnp.bitwise_xor(place[2], k) * slab, slab)
                    out[j, pl.ds(where, slab), (slot + 1) * rows : (slot + 2) * rows] = refs[
                        4 * slot + k
                    ][j].astype(jnp.bfloat16)

    return pl.pallas_call(
        body,
        out_shape=jax.ShapeDtypeStruct((OWN, BLOCK, 4 * rows), jnp.bfloat16),
        in_specs=[SMEM] + [VMEM] * 13,
        out_specs=VMEM,
        compiler_params=PARAMS,
        name="arrange_tokens",
    )(place, whole, *[piece for slot in slots for piece in slot])


def weight_part(place, tok, own, first, inner, middle, relayed, outer):
    rows, width = own.shape[1:]

    def body(place, tok, own, first, inner, middle, relayed, outer, send, keep, held):
        level, column = place[0], place[1]

        def fill(side, *parts):
            for slot, part in enumerate(parts):
                held[side, slot * rows : (slot + 1) * rows, :] = part.astype(jnp.bfloat16)

        @pl.when(level == 0)
        def _():
            fill(0, own[0], first[...], outer[0], outer[1])

        @pl.when(level == 1)
        def _():
            fill(0, own[0], inner[0], middle[0], relayed[0])
            fill(1, own[1], inner[1], middle[1], relayed[1])

        @pl.when(level == 2)
        def _():
            fill(0, own[1], inner[0], middle[0], relayed[1])
            fill(1, own[2], inner[1], middle[1], relayed[0])

        @pl.when(level == 3)
        def _():
            fill(0, own[2], first[...], outer[0], outer[1])

        low = lax.div(OWN * level, BLOCKS)
        for out, col in ((send, 1 - column), (keep, column)):
            for i in range(OWN // 2):
                j = (OWN // 2) * col + i
                side = lax.div(OWN * level + j, BLOCKS) - low
                out[BLOCK * i : BLOCK * (i + 1), :] = jnp.dot(
                    tok[j], held[side], preferred_element_type=jnp.float32
                )

    half = jax.ShapeDtypeStruct((OWN // 2 * BLOCK, width), jnp.float32)
    return pl.pallas_call(
        body,
        out_shape=(half, half),
        in_specs=[SMEM] + [VMEM] * 7,
        out_specs=(VMEM, VMEM),
        scratch_shapes=[pltpu.VMEM((2, 4 * rows, width), jnp.bfloat16)],
        compiler_params=PARAMS,
        name="weight_part",
    )(place, tok, own, first, inner, middle, relayed, outer)


def token_part(order, grads, weight):
    rows, chans = grads.shape[1:]
    wide = weight.shape[1] // 4
    count = order.shape[0]

    def body(order, grads, weight, out):
        now = lax.dot_general(
            grads[...], weight[...], (((1,), (1,)), ((), ())), preferred_element_type=jnp.float32
        )

        @pl.when(pl.program_id(1) == 0)
        def _():
            out[...] = now

        @pl.when(pl.program_id(1) > 0)
        def _():
            out[...] += now

    return pl.pallas_call(
        body,
        out_shape=jax.ShapeDtypeStruct((count, rows, wide), jnp.float32),
        grid_spec=pltpu.PrefetchScalarGridSpec(
            num_scalar_prefetch=1,
            grid=(count, 3),
            in_specs=[
                pl.BlockSpec((None, rows, chans), lambda i, s, order: (s, 0, 0)),
                pl.BlockSpec((None, wide, chans), lambda i, s, order: (s, order[i], 0)),
            ],
            out_specs=pl.BlockSpec((None, rows, wide), lambda i, s, order: (i, 0, 0)),
        ),
        compiler_params=PARAMS,
        name="token_part",
    )(order, grads, weight)


CHUNKS = 2


def lined(tokens, in_weight, kernel, out_grad):
    rows, features = tokens.shape
    chans = in_weight.shape[2]
    rep = lax.axis_index("rep")
    quarter = lax.axis_index("shard")
    level, column = rep // 2, rep % 2
    place = jnp.stack([level, column, quarter]).astype(jnp.int32)
    scale = 1.0 / math.sqrt(rows * lax.axis_size("rep"))
    inside = jnp.logical_or(level == 1, level == 2)
    low = level <= 1

    whole, piece = turn_tokens(place, tokens)
    near = lines(piece, PAIRS)
    mid = lines(piece, MIDDLE)
    far = lines(near, MIDDLE)

    def ended(array):
        return jnp.where(low, array[:OWN], array[BLOCKS - OWN :])

    def level_blocks(array):
        z1 = jnp.concatenate([array[6:], array[:4]], axis=0)
        z2 = jnp.concatenate([array[4:], array[:2]], axis=0)
        return jnp.where(level == 1, z1, z2)

    def share(array):
        across = lax.ppermute(array, "shard", [(q, q ^ 2) for q in range(4)])
        beside = lax.ppermute(array, "shard", [(q, q ^ 1) for q in range(4)])
        both = lax.ppermute(across, "shard", [(q, q ^ 1) for q in range(4)])
        return (array, beside, across, both)

    slots = [share(jnp.where(inside, level_blocks(near), ended(near)))]
    for got in (mid, far):
        outer = lines(ended(got), OUTWARD)
        slots.append(share(jnp.where(inside, level_blocks(got), outer)))

    wide_grad, taps = gated_grads(tokens, in_weight, kernel, out_grad)
    wide_grad = jnp.transpose(wide_grad, (1, 0, 2))

    tok = arrange_tokens(place, whole, slots)
    parts = []
    cw = chans // CHUNKS
    for h in range(CHUNKS):
        mine = wide_grad[:, :, cw * h : cw * (h + 1)]
        even = jnp.logical_or(level == 0, level == 2)
        first = lines(jnp.where(even, mine[2], mine[0]), PAIRS)
        inner = lines(jnp.where(low, mine[0:2], mine[1:3]), INWARD)
        middle = lines(jnp.where(low, mine[1:3], mine[0:2]), MIDDLE)
        relayed = lines(jnp.stack([first, jnp.where(low, inner[1], inner[0])]), MIDDLE)
        outer = lines(jnp.stack([jnp.where(low, middle[0], middle[1]), relayed[0]]), OUTWARD)
        send, keep = weight_part(place, tok, mine, first, inner, middle, relayed, outer)
        other = lax.ppermute(send, "rep", [(r, r ^ 1) for r in range(2 * LEVELS)])
        parts.append((keep + other) * scale)
    weight_grad = jnp.concatenate(parts, axis=1)

    mixed_grad = wide_grad.astype(jnp.bfloat16)
    order = [jnp.bitwise_xor(quarter, k).astype(jnp.int32) for k in (3, 1, 2, 0)]
    send = token_part(jnp.stack(order[:2]), mixed_grad, in_weight)
    keep = token_part(jnp.stack(order[2:]), mixed_grad, in_weight)
    other = lax.ppermute(send, "shard", [(q, q ^ 1) for q in range(4)])
    last = lax.ppermute(keep[0] + other[0], "shard", [(q, q ^ 2) for q in range(4)])
    token_grad = (keep[1] + other[1] + last).astype(jnp.bfloat16)

    for bit in (1, 2, 4):
        taps = taps + lax.ppermute(taps, "rep", [(r, r ^ bit) for r in range(2 * LEVELS)])
    return (token_grad, weight_grad, taps * scale)


def solution(mesh):
    placed = (P("rep", None), P(None, None, "shard"), P(None, None, "shard"), P("rep", "shard"))
    line = mesh.shape["rep"] == 2 * LEVELS and mesh.shape["shard"] == 4
    return jax.shard_map(
        lined if line else plain,
        mesh=mesh,
        in_specs=placed,
        out_specs=(P("rep", "shard"), P("rep", "shard"), P(None, None, "shard")),
        check_vma=False,
    )
```

```python
import functools
import math

import jax
import jax.numpy as jnp
from jax import lax
from jax.experimental import pallas as pl
from jax.experimental.pallas import tpu as pltpu
from jax.sharding import PartitionSpec as P

SEQ = 128


def causal_mix(values, kernel):
    width = kernel.shape[0]
    length = values.shape[1]
    padded = jnp.pad(values, ((0, 0), (width - 1, 0), (0, 0), (0, 0)))
    total = jnp.zeros_like(values)
    for offset in range(width):
        total = total + kernel[offset] * padded[:, width - 1 - offset : width - 1 - offset + length]
    return total


def causal_mix_back(grads, kernel):
    width = kernel.shape[0]
    length = grads.shape[1]
    padded = jnp.pad(grads, ((0, 0), (0, width - 1), (0, 0), (0, 0)))
    total = jnp.zeros_like(grads)
    for offset in range(width):
        total = total + kernel[offset] * padded[:, offset : offset + length]
    return total


def kernel_terms(values, grads, width):
    length = values.shape[1]
    padded = jnp.pad(values, ((0, 0), (width - 1, 0), (0, 0), (0, 0)))
    terms = []
    for offset in range(width):
        shifted = padded[:, width - 1 - offset : width - 1 - offset + length]
        terms.append(jnp.sum(shifted * grads, axis=(0, 1)))
    return jnp.stack(terms, axis=0)


def gated_grads(tokens, in_weight, kernel, out_grad):
    rows = tokens.shape[0]
    chans = in_weight.shape[2]
    mixed = jnp.einsum("td,sdc->tsc", tokens, in_weight, preferred_element_type=jnp.float32)
    stored = lax.optimization_barrier(mixed.astype(jnp.bfloat16))
    values = stored.astype(jnp.float32).reshape(rows // SEQ, SEQ, 3, chans)
    conv = causal_mix(values, kernel)
    query = conv[:, :, 0]
    keyed = conv[:, :, 1]
    valued = conv[:, :, 2]
    upstream = out_grad.astype(jnp.float32).reshape(rows // SEQ, SEQ, chans)
    conv_grad = jnp.stack(
        [upstream * keyed * valued, upstream * query * valued, upstream * query * keyed], axis=2
    )
    mixed_grad = causal_mix_back(conv_grad, kernel).reshape(rows, 3, chans)
    return mixed_grad, kernel_terms(values, conv_grad, kernel.shape[0])


def plain(tokens, in_weight, kernel, out_grad):
    features = tokens.shape[1]
    chans = in_weight.shape[2]
    scale = 1.0 / math.sqrt(tokens.shape[0] * lax.axis_size("rep"))
    wide_grad, taps = gated_grads(tokens, in_weight, kernel, out_grad)
    mixed_grad = wide_grad.astype(jnp.bfloat16)
    partial_grad = jnp.einsum(
        "tsc,sdc->td", mixed_grad, in_weight, preferred_element_type=jnp.float32
    )
    token_grad = lax.psum_scatter(partial_grad, "shard", scatter_dimension=1, tiled=True).astype(
        jnp.bfloat16
    )
    local_grad = (
        jnp.einsum("td,tsc->sdc", tokens, mixed_grad, preferred_element_type=jnp.float32) * scale
    )
    weight_grad = lax.psum_scatter(
        local_grad.reshape(3 * features, chans), "rep", scatter_dimension=0, tiled=True
    )
    kernel_grad = lax.psum(taps * scale, "rep")
    return (token_grad, weight_grad, kernel_grad)


LEVELS = 4
BLOCK = 512
BLOCKS = 8
OWN = 6
VMEM = pl.BlockSpec(memory_space=pltpu.VMEM)
SMEM = pl.BlockSpec(memory_space=pltpu.SMEM)
PARAMS = pltpu.CompilerParams(vmem_limit_bytes=48 * 2**20)


def lines(array, hops):
    perm = [(2 * a + y, 2 * b + y) for a, b in hops for y in range(2)]
    return lax.ppermute(array, "rep", perm)


def after(array, *earlier):
    return lax.optimization_barrier((array,) + earlier)[0]


PAIRS = ((0, 1), (1, 0), (2, 3), (3, 2))
INWARD = ((0, 1), (3, 2))
MIDDLE = ((1, 2), (2, 1))
OUTWARD = ((1, 0), (2, 3))


def turn_tokens(place, tokens):
    rows = tokens.shape[0]
    slab = BLOCK // 4

    def body(place, tokens, whole, piece):
        start = pl.multiple_of(place[2] * slab, slab)
        for b in range(BLOCKS):
            whole[b] = tokens[:, BLOCK * b : BLOCK * (b + 1)].T
            piece[b] = tokens[:, pl.ds(pl.multiple_of(BLOCK * b + start, slab), slab)].astype(
                jnp.float32
            ).T

    return pl.pallas_call(
        body,
        out_shape=(
            jax.ShapeDtypeStruct((BLOCKS, BLOCK, rows), jnp.bfloat16),
            jax.ShapeDtypeStruct((BLOCKS, slab, rows), jnp.float32),
        ),
        in_specs=[SMEM, VMEM],
        out_specs=(VMEM, VMEM),
        compiler_params=PARAMS,
        name="turn_tokens",
    )(place, tokens)


def arrange_tokens(place, whole, slots):
    rows = whole.shape[2]
    slab = BLOCK // 4

    def body(place, whole, *refs):
        out = refs[-1]
        for j in range(OWN):
            out[j, :, 0:rows] = whole[lax.rem(OWN * place[0] + j, BLOCKS)]
            for slot in range(3):
                for k in range(4):
                    where = pl.multiple_of(jnp.bitwise_xor(place[2], k) * slab, slab)
                    out[j, pl.ds(where, slab), (slot + 1) * rows : (slot + 2) * rows] = refs[
                        4 * slot + k
                    ][j].astype(jnp.bfloat16)

    return pl.pallas_call(
        body,
        out_shape=jax.ShapeDtypeStruct((OWN, BLOCK, 4 * rows), jnp.bfloat16),
        in_specs=[SMEM] + [VMEM] * 13,
        out_specs=VMEM,
        compiler_params=PARAMS,
        name="arrange_tokens",
    )(place, whole, *[piece for slot in slots for piece in slot])


def weight_part(place, tok, own, first, inner, middle, relayed, outer):
    rows, width = own.shape[1:]

    def body(place, tok, own, first, inner, middle, relayed, outer, send, keep, held):
        level, column = place[0], place[1]

        def fill(side, *parts):
            for slot, part in enumerate(parts):
                held[side, slot * rows : (slot + 1) * rows, :] = part.astype(jnp.bfloat16)

        @pl.when(level == 0)
        def _():
            fill(0, own[0], first[...], outer[0], outer[1])

        @pl.when(level == 1)
        def _():
            fill(0, own[0], inner[0], middle[0], relayed[0])
            fill(1, own[1], inner[1], middle[1], relayed[1])

        @pl.when(level == 2)
        def _():
            fill(0, own[1], inner[0], middle[0], relayed[1])
            fill(1, own[2], inner[1], middle[1], relayed[0])

        @pl.when(level == 3)
        def _():
            fill(0, own[2], first[...], outer[0], outer[1])

        low = lax.div(OWN * level, BLOCKS)
        for out, col in ((send, 1 - column), (keep, column)):
            for i in range(OWN // 2):
                j = (OWN // 2) * col + i
                side = lax.div(OWN * level + j, BLOCKS) - low
                out[BLOCK * i : BLOCK * (i + 1), :] = jnp.dot(
                    tok[j], held[side], preferred_element_type=jnp.float32
                )

    half = jax.ShapeDtypeStruct((OWN // 2 * BLOCK, width), jnp.float32)
    return pl.pallas_call(
        body,
        out_shape=(half, half),
        in_specs=[SMEM] + [VMEM] * 7,
        out_specs=(VMEM, VMEM),
        scratch_shapes=[pltpu.VMEM((2, 4 * rows, width), jnp.bfloat16)],
        compiler_params=PARAMS,
        name="weight_part",
    )(place, tok, own, first, inner, middle, relayed, outer)


def token_part(order, grads, weight):
    rows, chans = grads.shape[1:]
    wide = weight.shape[1] // 4
    count = order.shape[0]

    def body(order, grads, weight, out):
        now = lax.dot_general(
            grads[...], weight[...], (((1,), (1,)), ((), ())), preferred_element_type=jnp.float32
        )

        @pl.when(pl.program_id(1) == 0)
        def _():
            out[...] = now

        @pl.when(pl.program_id(1) > 0)
        def _():
            out[...] += now

    return pl.pallas_call(
        body,
        out_shape=jax.ShapeDtypeStruct((count, rows, wide), jnp.float32),
        grid_spec=pltpu.PrefetchScalarGridSpec(
            num_scalar_prefetch=1,
            grid=(count, 3),
            in_specs=[
                pl.BlockSpec((None, rows, chans), lambda i, s, order: (s, 0, 0)),
                pl.BlockSpec((None, wide, chans), lambda i, s, order: (s, order[i], 0)),
            ],
            out_specs=pl.BlockSpec((None, rows, wide), lambda i, s, order: (i, 0, 0)),
        ),
        compiler_params=PARAMS,
        name="token_part",
    )(order, grads, weight)


CHUNKS = 2


def lined(tokens, in_weight, kernel, out_grad):
    rows, features = tokens.shape
    chans = in_weight.shape[2]
    rep = lax.axis_index("rep")
    quarter = lax.axis_index("shard")
    level, column = rep // 2, rep % 2
    place = jnp.stack([level, column, quarter]).astype(jnp.int32)
    scale = 1.0 / math.sqrt(rows * lax.axis_size("rep"))
    inside = jnp.logical_or(level == 1, level == 2)
    low = level <= 1

    wide_grad, taps = gated_grads(tokens, in_weight, kernel, out_grad)
    wide_grad = jnp.transpose(wide_grad, (1, 0, 2))

    whole, piece = turn_tokens(place, tokens)
    near = lines(piece, PAIRS)
    mid = lines(piece, MIDDLE)

    def ended(array):
        return jnp.where(low, array[:OWN], array[BLOCKS - OWN :])

    def level_blocks(array):
        z1 = jnp.concatenate([array[6:], array[:4]], axis=0)
        z2 = jnp.concatenate([array[4:], array[:2]], axis=0)
        return jnp.where(level == 1, z1, z2)

    def share(array):
        across = lax.ppermute(array, "shard", [(q, q ^ 2) for q in range(4)])
        beside = lax.ppermute(array, "shard", [(q, q ^ 1) for q in range(4)])
        both = lax.ppermute(across, "shard", [(q, q ^ 1) for q in range(4)])
        return (array, beside, across, both)

    cw = chans // CHUNKS
    chunks = [wide_grad[:, :, cw * h : cw * (h + 1)] for h in range(CHUNKS)]
    even = jnp.logical_or(level == 0, level == 2)
    inners = [lines(jnp.where(low, mine[0:2], mine[1:3]), INWARD) for mine in chunks]
    firsts = [lines(jnp.where(even, mine[2], mine[0]), PAIRS) for mine in chunks]

    def tap_step(taps, bit):
        return taps + lax.ppermute(taps, "rep", [(r, r ^ bit) for r in range(2 * LEVELS)])

    taps = tap_step(taps, 1)

    far = lines(near, MIDDLE)
    slots = [share(jnp.where(inside, level_blocks(near), ended(near)))]
    outer2 = lines(after(ended(mid), near), OUTWARD)

    middles = [
        lines(after(jnp.where(low, mine[1:3], mine[0:2]), near, mid), MIDDLE) for mine in chunks
    ]
    slots.append(share(jnp.where(inside, level_blocks(mid), outer2)))
    outer3 = lines(ended(far), OUTWARD)
    taps = tap_step(after(taps, far), 2)
    slots.append(share(after(jnp.where(inside, level_blocks(far), outer3), slots[1][3], taps)))

    mixed_grad = after(wide_grad, far, taps).astype(jnp.bfloat16)
    order = [jnp.bitwise_xor(quarter, k).astype(jnp.int32) for k in (3, 1, 2, 0)]
    send = token_part(jnp.stack(order[:2]), mixed_grad, in_weight)
    keep = token_part(jnp.stack(order[2:]), mixed_grad, in_weight)
    other = lax.ppermute(send, "shard", [(q, q ^ 1) for q in range(4)])
    last = lax.ppermute(
        after(keep[0] + other[0], slots[2][2]), "shard", [(q, q ^ 2) for q in range(4)]
    )
    token_grad = (keep[1] + other[1] + last).astype(jnp.bfloat16)

    tok = arrange_tokens(place, whole, slots)
    parts = []
    for h, mine in enumerate(chunks):
        first, inner, middle = firsts[h], inners[h], middles[h]
        relay = jnp.stack([first, jnp.where(low, inner[1], inner[0])])
        relayed = lines(after(relay, far), MIDDLE)
        outgoing = jnp.stack([jnp.where(low, middle[0], middle[1]), relayed[0]])
        if h == 0:
            taps = tap_step(taps, 4)
        else:
            outgoing = after(outgoing, taps)
        outer = lines(outgoing, OUTWARD)
        send, keep = weight_part(place, tok, mine, first, inner, middle, relayed, outer)
        other = lax.ppermute(send, "rep", [(r, r ^ 1) for r in range(2 * LEVELS)])
        parts.append((keep + other) * scale)
    weight_grad = jnp.concatenate(parts, axis=1)
    return (token_grad, weight_grad, taps * scale)


def solution(mesh):
    placed = (P("rep", None), P(None, None, "shard"), P(None, None, "shard"), P("rep", "shard"))
    line = mesh.shape["rep"] == 2 * LEVELS and mesh.shape["shard"] == 4
    return jax.shard_map(
        lined if line else plain,
        mesh=mesh,
        in_specs=placed,
        out_specs=(P("rep", "shard"), P("rep", "shard"), P(None, None, "shard")),
        check_vma=False,
    )
```

```python
import functools
import math

import jax
import jax.numpy as jnp
from jax import lax
from jax.experimental import pallas as pl
from jax.experimental.pallas import tpu as pltpu
from jax.sharding import PartitionSpec as P

SEQ = 128


def causal_mix(values, kernel):
    width = kernel.shape[0]
    length = values.shape[1]
    padded = jnp.pad(values, ((0, 0), (width - 1, 0), (0, 0), (0, 0)))
    total = jnp.zeros_like(values)
    for offset in range(width):
        total = total + kernel[offset] * padded[:, width - 1 - offset : width - 1 - offset + length]
    return total


def causal_mix_back(grads, kernel):
    width = kernel.shape[0]
    length = grads.shape[1]
    padded = jnp.pad(grads, ((0, 0), (0, width - 1), (0, 0), (0, 0)))
    total = jnp.zeros_like(grads)
    for offset in range(width):
        total = total + kernel[offset] * padded[:, offset : offset + length]
    return total


def kernel_terms(values, grads, width):
    length = values.shape[1]
    padded = jnp.pad(values, ((0, 0), (width - 1, 0), (0, 0), (0, 0)))
    terms = []
    for offset in range(width):
        shifted = padded[:, width - 1 - offset : width - 1 - offset + length]
        terms.append(jnp.sum(shifted * grads, axis=(0, 1)))
    return jnp.stack(terms, axis=0)


def gated_grads(tokens, in_weight, kernel, out_grad):
    rows = tokens.shape[0]
    chans = in_weight.shape[2]
    mixed = jnp.einsum("td,sdc->tsc", tokens, in_weight, preferred_element_type=jnp.float32)
    stored = lax.optimization_barrier(mixed.astype(jnp.bfloat16))
    values = stored.astype(jnp.float32).reshape(rows // SEQ, SEQ, 3, chans)
    conv = causal_mix(values, kernel)
    query = conv[:, :, 0]
    keyed = conv[:, :, 1]
    valued = conv[:, :, 2]
    upstream = out_grad.astype(jnp.float32).reshape(rows // SEQ, SEQ, chans)
    conv_grad = jnp.stack(
        [upstream * keyed * valued, upstream * query * valued, upstream * query * keyed], axis=2
    )
    mixed_grad = causal_mix_back(conv_grad, kernel).reshape(rows, 3, chans)
    return mixed_grad, kernel_terms(values, conv_grad, kernel.shape[0])


def plain(tokens, in_weight, kernel, out_grad):
    features = tokens.shape[1]
    chans = in_weight.shape[2]
    scale = 1.0 / math.sqrt(tokens.shape[0] * lax.axis_size("rep"))
    wide_grad, taps = gated_grads(tokens, in_weight, kernel, out_grad)
    mixed_grad = wide_grad.astype(jnp.bfloat16)
    partial_grad = jnp.einsum(
        "tsc,sdc->td", mixed_grad, in_weight, preferred_element_type=jnp.float32
    )
    token_grad = lax.psum_scatter(partial_grad, "shard", scatter_dimension=1, tiled=True).astype(
        jnp.bfloat16
    )
    local_grad = (
        jnp.einsum("td,tsc->sdc", tokens, mixed_grad, preferred_element_type=jnp.float32) * scale
    )
    weight_grad = lax.psum_scatter(
        local_grad.reshape(3 * features, chans), "rep", scatter_dimension=0, tiled=True
    )
    kernel_grad = lax.psum(taps * scale, "rep")
    return (token_grad, weight_grad, kernel_grad)


LEVELS = 4
BLOCK = 512
BLOCKS = 8
OWN = 6
VMEM = pl.BlockSpec(memory_space=pltpu.VMEM)
SMEM = pl.BlockSpec(memory_space=pltpu.SMEM)
PARAMS = pltpu.CompilerParams(vmem_limit_bytes=48 * 2**20)


def lines(array, hops):
    perm = [(2 * a + y, 2 * b + y) for a, b in hops for y in range(2)]
    return lax.ppermute(array, "rep", perm)


def after(array, *earlier):
    return lax.optimization_barrier((array,) + earlier)[0]


PAIRS = ((0, 1), (1, 0), (2, 3), (3, 2))
INWARD = ((0, 1), (3, 2))
MIDDLE = ((1, 2), (2, 1))
OUTWARD = ((1, 0), (2, 3))


def turn_tokens(place, tokens):
    rows = tokens.shape[0]
    slab = BLOCK // 4

    def body(place, tokens, whole, piece):
        start = pl.multiple_of(place[2] * slab, slab)
        for b in range(BLOCKS):
            whole[b] = tokens[:, BLOCK * b : BLOCK * (b + 1)].T
            piece[b] = tokens[:, pl.ds(pl.multiple_of(BLOCK * b + start, slab), slab)].astype(
                jnp.float32
            ).T

    return pl.pallas_call(
        body,
        out_shape=(
            jax.ShapeDtypeStruct((BLOCKS, BLOCK, rows), jnp.bfloat16),
            jax.ShapeDtypeStruct((BLOCKS, slab, rows), jnp.float32),
        ),
        in_specs=[SMEM, VMEM],
        out_specs=(VMEM, VMEM),
        compiler_params=PARAMS,
        name="turn_tokens",
    )(place, tokens)


def gate(place, tokens, in_weight, kernel, out_grad, chunk, width):
    rows, features = tokens.shape
    taps = kernel.shape[0]
    steps = 4
    deep = features // steps
    pad = 8

    def body(place, tokens, weight, kernel, out_grad, own, grad, first, inner, middle, total, held, pads, back):
        step = pl.program_id(0)
        for s in range(3):
            now = jnp.dot(tokens[...], weight[s], preferred_element_type=jnp.float32)

            @pl.when(step == 0)
            def _():
                total[s] = now

            @pl.when(step > 0)
            def _():
                total[s] += now

        @pl.when(step == steps - 1)
        def _():
            blank = jnp.zeros((pad, width), jnp.float32)
            sums = [[None] * taps for _ in range(3)]
            for q in range(rows // SEQ):
                here = slice(q * SEQ, (q + 1) * SEQ)
                conv = []
                for s in range(3):
                    values = total[s, here, :].astype(jnp.bfloat16).astype(jnp.float32)
                    pads[s, 0:pad, :] = blank
                    pads[s, pad : pad + SEQ, :] = values
                    mix = kernel[0, s : s + 1, :] * values
                    for j in range(1, taps):
                        mix += kernel[j, s : s + 1, :] * pads[s, pad - j : pad - j + SEQ, :]
                    conv.append(mix)
                up = out_grad[here, :].astype(jnp.float32)
                query, keyed, valued = conv
                grads = (up * keyed * valued, up * query * valued, up * query * keyed)
                for s in range(3):
                    g = grads[s]
                    back[s, 0:SEQ, :] = g
                    back[s, SEQ : SEQ + pad, :] = blank
                    mixed = kernel[0, s : s + 1, :] * g
                    for j in range(taps):
                        if j:
                            mixed += kernel[j, s : s + 1, :] * back[s, j : j + SEQ, :]
                        term = jnp.sum(
                            pads[s, pad - j : pad - j + SEQ, :] * g, axis=0, keepdims=True
                        )
                        sums[s][j] = term if q == 0 else sums[s][j] + term
                    held[s, here, :] = mixed
            for s in range(3):
                own[s] = held[s].astype(jnp.bfloat16)
                for j in range(taps):
                    grad[j, s : s + 1, :] = sums[s][j]
            level = place[0]
            first[...] = held[2 - 2 * lax.rem(level, 2)]
            low = jnp.where(level <= 1, 0, 1)
            for i in range(2):
                inner[i] = held[low + i]
                middle[i] = held[1 - low + i]

    one = jax.ShapeDtypeStruct((rows, width), jnp.float32)
    two = jax.ShapeDtypeStruct((2, rows, width), jnp.float32)
    full = lambda shape: pl.BlockSpec(shape, lambda k: (0,) * len(shape))
    return pl.pallas_call(
        body,
        out_shape=(
            jax.ShapeDtypeStruct((3, rows, width), jnp.bfloat16),
            jax.ShapeDtypeStruct((taps, 3, width), jnp.float32),
            one,
            two,
            two,
        ),
        grid=(steps,),
        in_specs=[
            SMEM,
            pl.BlockSpec((rows, deep), lambda k: (0, k)),
            pl.BlockSpec((3, deep, width), lambda k: (0, k, chunk)),
            pl.BlockSpec((taps, 3, width), lambda k: (0, 0, chunk)),
            pl.BlockSpec((rows, width), lambda k: (0, chunk)),
        ],
        out_specs=(
            full((3, rows, width)),
            full((taps, 3, width)),
            full((rows, width)),
            full((2, rows, width)),
            full((2, rows, width)),
        ),
        scratch_shapes=[
            pltpu.VMEM((3, rows, width), jnp.float32),
            pltpu.VMEM((3, rows, width), jnp.float32),
            pltpu.VMEM((3, pad + SEQ, width), jnp.float32),
            pltpu.VMEM((3, SEQ + pad, width), jnp.float32),
        ],
        compiler_params=PARAMS,
        cost_estimate=pl.CostEstimate(
            flops=2 * rows * features * 3 * width,
            bytes_accessed=2 * features * 3 * width,
            transcendentals=0,
        ),
        name="gate",
    )(place, tokens, in_weight, kernel, out_grad)


def arrange_tokens(place, whole, slots):
    rows = whole.shape[2]
    slab = BLOCK // 4

    def body(place, whole, *refs):
        out = refs[-1]
        for j in range(OWN):
            out[j, :, 0:rows] = whole[lax.rem(OWN * place[0] + j, BLOCKS)]
            for slot in range(3):
                for k in range(4):
                    where = pl.multiple_of(jnp.bitwise_xor(place[2], k) * slab, slab)
                    out[j, pl.ds(where, slab), (slot + 1) * rows : (slot + 2) * rows] = refs[
                        4 * slot + k
                    ][j].astype(jnp.bfloat16)

    return pl.pallas_call(
        body,
        out_shape=jax.ShapeDtypeStruct((OWN, BLOCK, 4 * rows), jnp.bfloat16),
        in_specs=[SMEM] + [VMEM] * 13,
        out_specs=VMEM,
        compiler_params=PARAMS,
        name="arrange_tokens",
    )(place, whole, *[piece for slot in slots for piece in slot])


def weight_part(place, tok, own, first, inner, middle, relayed, outer):
    rows, width = own.shape[1:]

    def body(place, tok, own, first, inner, middle, relayed, outer, send, keep, held):
        level, column = place[0], place[1]

        def fill(side, *parts):
            for slot, part in enumerate(parts):
                held[side, slot * rows : (slot + 1) * rows, :] = part.astype(jnp.bfloat16)

        @pl.when(level == 0)
        def _():
            fill(0, own[0], first[...], outer[0], outer[1])

        @pl.when(level == 1)
        def _():
            fill(0, own[0], inner[0], middle[0], relayed[0])
            fill(1, own[1], inner[1], middle[1], relayed[1])

        @pl.when(level == 2)
        def _():
            fill(0, own[1], inner[0], middle[0], relayed[1])
            fill(1, own[2], inner[1], middle[1], relayed[0])

        @pl.when(level == 3)
        def _():
            fill(0, own[2], first[...], outer[0], outer[1])

        low = lax.div(OWN * level, BLOCKS)
        for out, col in ((send, 1 - column), (keep, column)):
            for i in range(OWN // 2):
                j = (OWN // 2) * col + i
                side = lax.div(OWN * level + j, BLOCKS) - low
                out[BLOCK * i : BLOCK * (i + 1), :] = jnp.dot(
                    tok[j], held[side], preferred_element_type=jnp.float32
                )

    half = jax.ShapeDtypeStruct((OWN // 2 * BLOCK, width), jnp.float32)
    return pl.pallas_call(
        body,
        out_shape=(half, half),
        in_specs=[SMEM] + [VMEM] * 7,
        out_specs=(VMEM, VMEM),
        scratch_shapes=[pltpu.VMEM((2, 4 * rows, width), jnp.bfloat16)],
        compiler_params=PARAMS,
        name="weight_part",
    )(place, tok, own, first, inner, middle, relayed, outer)


def token_part(order, grads, weight):
    rows, width = grads[0].shape[1:]
    wide = weight.shape[1] // 4
    chans = weight.shape[2]
    count = order.shape[0]

    def body(order, *refs):
        weight, out = refs[-2:]
        now = None
        for h, part in enumerate(refs[:-2]):
            term = lax.dot_general(
                part[...],
                weight[:, width * h : width * (h + 1)],
                (((1,), (1,)), ((), ())),
                preferred_element_type=jnp.float32,
            )
            now = term if now is None else now + term

        @pl.when(pl.program_id(1) == 0)
        def _():
            out[...] = now

        @pl.when(pl.program_id(1) > 0)
        def _():
            out[...] += now

    return pl.pallas_call(
        body,
        out_shape=jax.ShapeDtypeStruct((count, rows, wide), jnp.float32),
        grid_spec=pltpu.PrefetchScalarGridSpec(
            num_scalar_prefetch=1,
            grid=(count, 3),
            in_specs=[pl.BlockSpec((None, rows, width), lambda i, s, order: (s, 0, 0))] * len(grads)
            + [pl.BlockSpec((None, wide, chans), lambda i, s, order: (s, order[i], 0))],
            out_specs=pl.BlockSpec((None, rows, wide), lambda i, s, order: (i, 0, 0)),
        ),
        compiler_params=PARAMS,
        cost_estimate=pl.CostEstimate(
            flops=2 * count * rows * wide * 3 * chans,
            bytes_accessed=2 * count * wide * 3 * chans,
            transcendentals=0,
        ),
        name="token_part",
    )(order, *grads, weight)


CHUNKS = 2


def lined(tokens, in_weight, kernel, out_grad):
    rows, features = tokens.shape
    chans = in_weight.shape[2]
    rep = lax.axis_index("rep")
    quarter = lax.axis_index("shard")
    level, column = rep // 2, rep % 2
    place = jnp.stack([level, column, quarter]).astype(jnp.int32)
    scale = 1.0 / math.sqrt(rows * lax.axis_size("rep"))
    inside = jnp.logical_or(level == 1, level == 2)
    low = level <= 1

    whole, piece = turn_tokens(place, tokens)
    near = lines(piece, PAIRS)
    mid = lines(piece, MIDDLE)

    def ended(array):
        return jnp.where(low, array[:OWN], array[BLOCKS - OWN :])

    def level_blocks(array):
        z1 = jnp.concatenate([array[6:], array[:4]], axis=0)
        z2 = jnp.concatenate([array[4:], array[:2]], axis=0)
        return jnp.where(level == 1, z1, z2)

    def share(array):
        across = lax.ppermute(array, "shard", [(q, q ^ 2) for q in range(4)])
        beside = lax.ppermute(array, "shard", [(q, q ^ 1) for q in range(4)])
        both = lax.ppermute(across, "shard", [(q, q ^ 1) for q in range(4)])
        return (array, beside, across, both)

    def tap_step(taps, bit, *earlier):
        other = lax.ppermute(taps, "rep", [(r, r ^ bit) for r in range(2 * LEVELS)])
        return taps + after(other, *earlier)

    cw = chans // CHUNKS
    owns, firsts, inners, middles, taps = [], [], [], [], []
    for h in range(CHUNKS):
        own, tap, first, inner, middle = gate(place, tokens, in_weight, kernel, out_grad, h, cw)
        owns.append(own)
        taps.append(tap)
        inners.append(lines(inner, INWARD))
        firsts.append(lines(first, PAIRS))
        middles.append(middle)
    taps = jnp.concatenate(taps, axis=2)

    far = lines(near, MIDDLE)
    middles = [lines(after(middle, near), MIDDLE) for middle in middles]
    slots = [share(jnp.where(inside, level_blocks(near), ended(near)))]
    outer2 = lines(after(ended(mid), near), OUTWARD)

    taps = tap_step(taps, 1, far)
    outer3 = lines(ended(far), OUTWARD)
    slots.append(share(jnp.where(inside, level_blocks(mid), after(outer2, far))))

    def relay(h, *earlier):
        first, inner = after(firsts[h], *earlier), after(inners[h], *earlier)
        return lines(jnp.stack([first, jnp.where(low, inner[1], inner[0])]), MIDDLE)

    relays = [relay(0, middles[0]), relay(1, middles[1])]
    taps = tap_step(taps, 2, middles[0])
    slots.append(share(jnp.where(inside, level_blocks(far), after(outer3, middles[0]))))

    grads = [after(own, far) for own in owns]
    order = [jnp.bitwise_xor(quarter, k).astype(jnp.int32) for k in (3, 1, 2, 0)]
    send = token_part(jnp.stack(order[:2]), grads, in_weight)
    keep = token_part(jnp.stack(order[2:]), [after(g, middles[1]) for g in grads], in_weight)
    other = lax.ppermute(send, "shard", [(q, q ^ 1) for q in range(4)])
    last = lax.ppermute(
        after(keep[0] + other[0], slots[2][2]), "shard", [(q, q ^ 2) for q in range(4)]
    )
    token_grad = (keep[1] + other[1] + last).astype(jnp.bfloat16)

    tok = arrange_tokens(place, whole, slots)
    parts = []
    for h in range(CHUNKS):
        middle, relayed = middles[h], relays[h]
        outgoing = jnp.stack([jnp.where(low, middle[0], middle[1]), relayed[0]])
        if h == 0:
            taps = tap_step(taps, 4)
        else:
            outgoing = after(outgoing, taps)
        outer = lines(outgoing, OUTWARD)
        send, keep = weight_part(
            place, tok, owns[h], firsts[h], inners[h], middle, relayed, outer
        )
        other = lax.ppermute(send, "rep", [(r, r ^ 1) for r in range(2 * LEVELS)])
        parts.append((keep + other) * scale)
    weight_grad = jnp.concatenate(parts, axis=1)
    return (token_grad, weight_grad, taps * scale)


def solution(mesh):
    placed = (P("rep", None), P(None, None, "shard"), P(None, None, "shard"), P("rep", "shard"))
    line = mesh.shape["rep"] == 2 * LEVELS and mesh.shape["shard"] == 4
    return jax.shard_map(
        lined if line else plain,
        mesh=mesh,
        in_specs=placed,
        out_specs=(P("rep", "shard"), P("rep", "shard"), P(None, None, "shard")),
        check_vma=False,
    )
```

```python
import functools
import math

import jax
import jax.numpy as jnp
from jax import lax
from jax.experimental import pallas as pl
from jax.experimental.pallas import tpu as pltpu
from jax.sharding import PartitionSpec as P

SEQ = 128


def causal_mix(values, kernel):
    width = kernel.shape[0]
    length = values.shape[1]
    padded = jnp.pad(values, ((0, 0), (width - 1, 0), (0, 0), (0, 0)))
    total = jnp.zeros_like(values)
    for offset in range(width):
        total = total + kernel[offset] * padded[:, width - 1 - offset : width - 1 - offset + length]
    return total


def causal_mix_back(grads, kernel):
    width = kernel.shape[0]
    length = grads.shape[1]
    padded = jnp.pad(grads, ((0, 0), (0, width - 1), (0, 0), (0, 0)))
    total = jnp.zeros_like(grads)
    for offset in range(width):
        total = total + kernel[offset] * padded[:, offset : offset + length]
    return total


def kernel_terms(values, grads, width):
    length = values.shape[1]
    padded = jnp.pad(values, ((0, 0), (width - 1, 0), (0, 0), (0, 0)))
    terms = []
    for offset in range(width):
        shifted = padded[:, width - 1 - offset : width - 1 - offset + length]
        terms.append(jnp.sum(shifted * grads, axis=(0, 1)))
    return jnp.stack(terms, axis=0)


def gated_grads(tokens, in_weight, kernel, out_grad):
    rows = tokens.shape[0]
    chans = in_weight.shape[2]
    mixed = jnp.einsum("td,sdc->tsc", tokens, in_weight, preferred_element_type=jnp.float32)
    stored = lax.optimization_barrier(mixed.astype(jnp.bfloat16))
    values = stored.astype(jnp.float32).reshape(rows // SEQ, SEQ, 3, chans)
    conv = causal_mix(values, kernel)
    query = conv[:, :, 0]
    keyed = conv[:, :, 1]
    valued = conv[:, :, 2]
    upstream = out_grad.astype(jnp.float32).reshape(rows // SEQ, SEQ, chans)
    conv_grad = jnp.stack(
        [upstream * keyed * valued, upstream * query * valued, upstream * query * keyed], axis=2
    )
    mixed_grad = causal_mix_back(conv_grad, kernel).reshape(rows, 3, chans)
    return mixed_grad, kernel_terms(values, conv_grad, kernel.shape[0])


def plain(tokens, in_weight, kernel, out_grad):
    features = tokens.shape[1]
    chans = in_weight.shape[2]
    scale = 1.0 / math.sqrt(tokens.shape[0] * lax.axis_size("rep"))
    wide_grad, taps = gated_grads(tokens, in_weight, kernel, out_grad)
    mixed_grad = wide_grad.astype(jnp.bfloat16)
    partial_grad = jnp.einsum(
        "tsc,sdc->td", mixed_grad, in_weight, preferred_element_type=jnp.float32
    )
    token_grad = lax.psum_scatter(partial_grad, "shard", scatter_dimension=1, tiled=True).astype(
        jnp.bfloat16
    )
    local_grad = (
        jnp.einsum("td,tsc->sdc", tokens, mixed_grad, preferred_element_type=jnp.float32) * scale
    )
    weight_grad = lax.psum_scatter(
        local_grad.reshape(3 * features, chans), "rep", scatter_dimension=0, tiled=True
    )
    kernel_grad = lax.psum(taps * scale, "rep")
    return (token_grad, weight_grad, kernel_grad)


LEVELS = 4
BLOCK = 512
BLOCKS = 8
OWN = 6
HALF = 3
LANES = 128
VMEM = pl.BlockSpec(memory_space=pltpu.VMEM)
SMEM = pl.BlockSpec(memory_space=pltpu.SMEM)
PARAMS = pltpu.CompilerParams(vmem_limit_bytes=48 * 2**20)
PAIRS = ((0, 1), (1, 0), (2, 3), (3, 2))
INWARD = ((0, 1), (3, 2))
MIDDLE = ((1, 2), (2, 1))
OUTWARD = ((1, 0), (2, 3))
ENDS = (0, 3)
INNER = (1, 2)


def lines(array, hops):
    perm = [(2 * a + y, 2 * b + y) for a, b in hops for y in range(2)]
    return lax.ppermute(array, "rep", perm)


def sides(array, levels=range(LEVELS)):
    return lax.ppermute(array, "rep", [(2 * z + y, 2 * z + 1 - y) for z in levels for y in range(2)])


def share(array):
    across = lax.ppermute(array, "shard", [(q, q ^ 2) for q in range(4)])
    beside = lax.ppermute(array, "shard", [(q, q ^ 1) for q in range(4)])
    both = lax.ppermute(across, "shard", [(q, q ^ 1) for q in range(4)])
    return (array, beside, across, both)


def device_block(level, column, i):
    return lax.rem(OWN * level + HALF * column + i, BLOCKS)


def turn_tokens(place, tokens):
    rows = tokens.shape[0]
    slab = BLOCK // 4

    def body(place, tokens, piece, theirs):
        start = pl.multiple_of(place[2] * slab, slab)
        for b in range(BLOCKS):
            piece[b] = tokens[:, pl.ds(pl.multiple_of(BLOCK * b + start, slab), slab)].astype(
                jnp.float32
            ).T
        for i in range(HALF):
            theirs[i] = piece[device_block(place[0], 1 - place[1], i)]

    return pl.pallas_call(
        body,
        out_shape=(
            jax.ShapeDtypeStruct((BLOCKS, slab, rows), jnp.float32),
            jax.ShapeDtypeStruct((HALF, slab, rows), jnp.float32),
        ),
        in_specs=[SMEM, VMEM],
        out_specs=(VMEM, VMEM),
        compiler_params=PARAMS,
        name="turn_tokens",
    )(place, tokens)


def other_blocks(place, inner, ends=None):
    def body(place, *refs):
        inner, out = refs[0], refs[-1]
        for i in range(HALF):
            if ends is None:
                out[i] = inner[device_block(place[0], 1 - place[1], i)]
                continue
            inside = jnp.logical_or(place[0] == 1, place[0] == 2)

            @pl.when(inside)
            def _():
                out[i] = inner[device_block(place[0], 1 - place[1], i)]

            @pl.when(jnp.logical_not(inside))
            def _():
                out[i] = refs[1][HALF * (1 - place[1]) + i]

    arrays = (inner,) if ends is None else (inner, ends)
    return pl.pallas_call(
        body,
        out_shape=jax.ShapeDtypeStruct((HALF,) + inner.shape[1:], inner.dtype),
        in_specs=[SMEM] + [VMEM] * len(arrays),
        out_specs=VMEM,
        compiler_params=PARAMS,
        name="other_blocks",
    )(place, *arrays)


def own_blocks(place, got, inner, ends=None):
    def body(place, got, *refs):
        inner, out = refs[0], refs[-1]
        for i in range(HALF):
            out[HALF + i] = got[i]
            if ends is None:
                out[i] = inner[device_block(place[0], place[1], i)]
                continue
            inside = jnp.logical_or(place[0] == 1, place[0] == 2)

            @pl.when(inside)
            def _():
                out[i] = inner[device_block(place[0], place[1], i)]

            @pl.when(jnp.logical_not(inside))
            def _():
                out[i] = refs[1][HALF * place[1] + i]

    arrays = (inner,) if ends is None else (inner, ends)
    return pl.pallas_call(
        body,
        out_shape=jax.ShapeDtypeStruct((OWN,) + inner.shape[1:], inner.dtype),
        in_specs=[SMEM] + [VMEM] * (1 + len(arrays)),
        out_specs=VMEM,
        compiler_params=PARAMS,
        name="own_blocks",
    )(place, got, *arrays)


def gate(place, tokens, in_weight, kernel, out_grad):
    rows, features = tokens.shape
    chans = in_weight.shape[2]
    taps = kernel.shape[0]
    steps = 4
    width = min(chans, 2 * LANES)
    deep = features // steps
    pad = 8

    def body(place, tokens, weight, kernel, out_grad, own, grad, first, inner, middle, total, held, pads, back):
        step = pl.program_id(1)
        for s in range(3):
            now = jnp.dot(tokens[...], weight[s], preferred_element_type=jnp.float32)

            @pl.when(step == 0)
            def _():
                total[s] = now

            @pl.when(step > 0)
            def _():
                total[s] += now

        @pl.when(step == steps - 1)
        def _():
            blank = jnp.zeros((pad, LANES), jnp.float32)
            for lane in range(0, width, LANES):
                lanes = slice(lane, lane + LANES)
                sums = [[None] * taps for _ in range(3)]
                for q in range(rows // SEQ):
                    here = slice(q * SEQ, (q + 1) * SEQ)
                    conv = []
                    for s in range(3):
                        values = total[s, here, lanes].astype(jnp.bfloat16).astype(jnp.float32)
                        pads[s, 0:pad, :] = blank
                        pads[s, pad : pad + SEQ, :] = values
                        mix = kernel[0, s : s + 1, lanes] * values
                        for j in range(1, taps):
                            mix += kernel[j, s : s + 1, lanes] * pads[s, pad - j : pad - j + SEQ, :]
                        conv.append(mix)
                    up = out_grad[here, lanes].astype(jnp.float32)
                    query, keyed, valued = conv
                    grads = (up * keyed * valued, up * query * valued, up * query * keyed)
                    for s in range(3):
                        back[s, 0:SEQ, :] = grads[s]
                        back[s, SEQ : SEQ + pad, :] = blank
                    for s in range(3):
                        values = pads[s, pad : pad + SEQ, :]
                        mixed = None
                        for j in range(taps):
                            moved = back[s, j : j + SEQ, :]
                            term = kernel[j, s : s + 1, lanes] * moved
                            mixed = term if mixed is None else mixed + term
                            folded = jnp.sum((values * moved).reshape(SEQ // 8, 8, LANES), axis=0)
                            sums[s][j] = folded if q == 0 else sums[s][j] + folded
                        held[s, here, lanes] = mixed
                for s in range(3):
                    for j in range(taps):
                        grad[j, s : s + 1, lanes] = jnp.sum(sums[s][j], axis=0, keepdims=True)
            for s in range(3):
                own[s] = held[s].astype(jnp.bfloat16)
            level = place[0]
            first[...] = held[2 - 2 * lax.rem(level, 2)]
            low = jnp.where(level <= 1, 0, 1)
            for i in range(2):
                inner[i] = held[low + i]
                middle[i] = held[1 - low + i]

    one = jax.ShapeDtypeStruct((rows, chans), jnp.float32)
    two = jax.ShapeDtypeStruct((2, rows, chans), jnp.float32)
    return pl.pallas_call(
        body,
        out_shape=(
            jax.ShapeDtypeStruct((3, rows, chans), jnp.bfloat16),
            jax.ShapeDtypeStruct((taps, 3, chans), jnp.float32),
            one,
            two,
            two,
        ),
        grid=(chans // width, steps),
        in_specs=[
            SMEM,
            pl.BlockSpec((rows, deep), lambda c, k: (0, k)),
            pl.BlockSpec((3, deep, width), lambda c, k: (0, k, c)),
            pl.BlockSpec((taps, 3, width), lambda c, k: (0, 0, c)),
            pl.BlockSpec((rows, width), lambda c, k: (0, c)),
        ],
        out_specs=(
            pl.BlockSpec((3, rows, width), lambda c, k: (0, 0, c)),
            pl.BlockSpec((taps, 3, width), lambda c, k: (0, 0, c)),
            pl.BlockSpec((rows, width), lambda c, k: (0, c)),
            pl.BlockSpec((2, rows, width), lambda c, k: (0, 0, c)),
            pl.BlockSpec((2, rows, width), lambda c, k: (0, 0, c)),
        ),
        scratch_shapes=[
            pltpu.VMEM((3, rows, width), jnp.float32),
            pltpu.VMEM((3, rows, width), jnp.float32),
            pltpu.VMEM((3, pad + SEQ, LANES), jnp.float32),
            pltpu.VMEM((3, SEQ + pad, LANES), jnp.float32),
        ],
        compiler_params=PARAMS,
        cost_estimate=pl.CostEstimate(
            flops=2 * rows * features * 3 * chans,
            bytes_accessed=2 * features * 3 * chans,
            transcendentals=0,
        ),
        name="gate",
    )(place, tokens, in_weight, kernel, out_grad)


def relay_payload(place, first, inner):
    def body(place, first, inner, out):
        @pl.when(place[0] <= 1)
        def _():
            out[0] = inner[1]
            out[1] = first[...]

        @pl.when(place[0] > 1)
        def _():
            out[0] = first[...]
            out[1] = inner[0]

    return pl.pallas_call(
        body,
        out_shape=jax.ShapeDtypeStruct(inner.shape, inner.dtype),
        in_specs=[SMEM, VMEM, VMEM],
        out_specs=VMEM,
        compiler_params=PARAMS,
        name="relay_payload",
    )(place, first, inner)


def arrange_tokens(place, own, slots):
    slab = BLOCK // 4
    rows = slots[0][0].shape[2]
    counts = [slot[0].shape[0] // HALF for slot in slots]
    total = (0 if own is None else 1) + sum(counts)

    def body(place, *refs):
        out = refs[-1]
        at = 0
        if own is not None:
            for i in range(HALF):
                block = device_block(place[0], place[1], i)
                columns = pl.ds(pl.multiple_of(block * BLOCK, BLOCK), BLOCK)
                out[i, :, 0:rows] = refs[0][:, columns].T
            refs = refs[1:]
            at = 1
        for n, count in enumerate(counts):
            for c in range(count):
                for i in range(HALF):
                    for k in range(4):
                        where = pl.multiple_of(jnp.bitwise_xor(place[2], k) * slab, slab)
                        out[i, pl.ds(where, slab), (at + c) * rows : (at + c + 1) * rows] = refs[
                            4 * n + k
                        ][HALF * c + i].astype(jnp.bfloat16)
            at += count

    arrays = ([] if own is None else [own]) + [piece for slot in slots for piece in slot]
    return pl.pallas_call(
        body,
        out_shape=jax.ShapeDtypeStruct((HALF, BLOCK, total * rows), jnp.bfloat16),
        in_specs=[SMEM] + [VMEM] * len(arrays),
        out_specs=VMEM,
        compiler_params=PARAMS,
        name="arrange_tokens",
    )(place, *arrays)


def weight_part(place, tok, own, slots, scale=None, so_far=None):
    rows, chans = slots[0][1].shape[1:]
    count = (0 if own is None else 1) + len(slots)
    arrays = ([] if own is None else [own]) + [a for slot in slots for a in slot if a is not None]
    last = scale is not None

    def body(place, tok, *refs):
        out, held = refs[-2], refs[-1]
        level, column = place[0], place[1]
        i = pl.program_id(0)
        inside = jnp.logical_or(level == 1, level == 2)
        at = 0

        @pl.when(i == 0)
        def _():
            at = 0
            refs_left = list(refs)
            if own is not None:
                ref = refs_left.pop(0)
                major = jnp.where(inside, level - 1 + column, jnp.where(level == 0, 0, 2))
                held[0, 0:rows, :] = ref[major]
                held[1, 0:rows, :] = ref[1]
                at = 1
            for ends, _inner in slots:
                here = slice(at * rows, (at + 1) * rows)
                if ends is None:
                    ref = refs_left.pop(0)
                    major = jnp.where(inside, column, jnp.where(level == 0, 0, 1))
                    held[0, here, :] = ref[major].astype(jnp.bfloat16)
                    held[1, here, :] = ref[jnp.where(level == 2, 0, 1)].astype(jnp.bfloat16)
                else:
                    end, ref = refs_left.pop(0), refs_left.pop(0)

                    @pl.when(inside)
                    def _():
                        held[0, here, :] = ref[column].astype(jnp.bfloat16)
                        held[1, here, :] = ref[jnp.where(level == 2, 0, 1)].astype(jnp.bfloat16)

                    @pl.when(jnp.logical_not(inside))
                    def _():
                        held[0, here, :] = end[...].astype(jnp.bfloat16)

                at += 1

        second = jnp.logical_or(
            jnp.logical_and(jnp.logical_and(level == 1, column == 0), i == 2),
            jnp.logical_and(jnp.logical_and(level == 2, column == 1), i == 0),
        )
        got = jnp.dot(
            tok[...], held[second.astype(jnp.int32)], preferred_element_type=jnp.float32
        )
        if so_far is not None:
            got = got + refs[-3][...]
        out[...] = got * scale if last else got

    whole = lambda a: pl.BlockSpec(a.shape, lambda i: (0,) * a.ndim)
    more = [] if so_far is None else [so_far]
    part = pl.BlockSpec((BLOCK, chans), lambda i: (i, 0))
    return pl.pallas_call(
        body,
        out_shape=jax.ShapeDtypeStruct((HALF * BLOCK, chans), jnp.float32),
        grid=(HALF,),
        in_specs=[SMEM, pl.BlockSpec((None, BLOCK, count * rows), lambda i: (i, 0, 0))]
        + [whole(a) for a in arrays]
        + [part] * len(more),
        out_specs=part,
        scratch_shapes=[pltpu.VMEM((2, count * rows, chans), jnp.bfloat16)],
        compiler_params=PARAMS,
        cost_estimate=pl.CostEstimate(
            flops=2 * HALF * BLOCK * count * rows * chans,
            bytes_accessed=2 * HALF * BLOCK * count * rows + 8 * count * rows * chans,
            transcendentals=0,
        ),
        name="weight_part",
    )(place, tok, *arrays, *more)


def token_part(grads, weight):
    rows, chans = grads.shape[1:]
    wide = weight.shape[1] // 4

    def body(grads, weight, out):
        now = lax.dot_general(
            grads[...], weight[...], (((1,), (1,)), ((), ())), preferred_element_type=jnp.float32
        )

        @pl.when(pl.program_id(1) == 0)
        def _():
            out[...] = now

        @pl.when(pl.program_id(1) > 0)
        def _():
            out[...] += now

    return pl.pallas_call(
        body,
        out_shape=jax.ShapeDtypeStruct((rows, 4 * wide), jnp.float32),
        grid=(4, 3),
        in_specs=[
            pl.BlockSpec((None, rows, chans), lambda i, s: (s, 0, 0)),
            pl.BlockSpec((None, wide, chans), lambda i, s: (s, i, 0)),
        ],
        out_specs=pl.BlockSpec((rows, wide), lambda i, s: (0, i)),
        compiler_params=PARAMS,
        cost_estimate=pl.CostEstimate(
            flops=8 * rows * wide * 3 * chans,
            bytes_accessed=8 * wide * 3 * chans + 16 * rows * wide,
            transcendentals=0,
        ),
        name="token_part",
    )(grads, weight)


def lined(tokens, in_weight, kernel, out_grad):
    rows, features = tokens.shape
    rep = lax.axis_index("rep")
    level, column = rep // 2, rep % 2
    place = jnp.stack([level, column, lax.axis_index("shard")]).astype(jnp.int32)
    scale = 1.0 / math.sqrt(rows * lax.axis_size("rep"))
    later = jnp.where(level <= 1, 0, 1)

    piece, theirs = turn_tokens(place, tokens)
    near = lines(piece, PAIRS)
    mid = lines(piece, MIDDLE)
    slots = [share(sides(theirs))]

    own, taps, first_out, inner_out, middle_out = gate(place, tokens, in_weight, kernel, out_grad)
    partial = token_part(own, in_weight)
    token_grad = lax.psum_scatter(partial, "shard", scatter_dimension=1, tiled=True)

    def ended(array):
        return lax.dynamic_slice_in_dim(array, 2 * later, OWN, 0)

    far = lines(near, MIDDLE)
    got = sides(other_blocks(place, near))
    slots.append(share(own_blocks(place, got, near)))
    for array in (mid, far):
        outer = lines(ended(array), OUTWARD)
        got = sides(other_blocks(place, array, outer))
        slots.append(share(own_blocks(place, got, array, outer)))

    own_y = sides(inner_out)
    middle = lines(middle_out, MIDDLE)
    inner = lines(inner_out, INWARD)
    first = lines(first_out, PAIRS)
    relayed = lines(relay_payload(place, first, inner), MIDDLE)
    pick = lambda array: lax.dynamic_index_in_dim(array, later, 0, keepdims=False)
    middle_end = lines(pick(middle), OUTWARD)
    relayed_end = lines(pick(relayed), OUTWARD)

    def both(ends, inner):
        return [(ends, inner), (sides(ends, ENDS), sides(inner, INNER))]

    early = [(None, own_y)] + both(first, inner) + both(middle_end, middle)
    late = both(relayed_end, relayed)

    for bit in (1, 2, 4):
        taps = taps + lax.ppermute(taps, "rep", [(r, r ^ bit) for r in range(2 * LEVELS)])

    so_far = weight_part(place, arrange_tokens(place, tokens, slots[:3]), own, early)
    weight_grad = weight_part(
        place, arrange_tokens(place, None, slots[3:]), None, late, scale, so_far
    )
    return (token_grad.astype(jnp.bfloat16), weight_grad, taps * scale)


def solution(mesh):
    placed = (P("rep", None), P(None, None, "shard"), P(None, None, "shard"), P("rep", "shard"))
    line = mesh.shape["rep"] == 2 * LEVELS and mesh.shape["shard"] == 4
    return jax.shard_map(
        lined if line else plain,
        mesh=mesh,
        in_specs=placed,
        out_specs=(P("rep", "shard"), P("rep", "shard"), P(None, None, "shard")),
        check_vma=False,
    )
```

```python
import functools
import math

import jax
import jax.numpy as jnp
from jax import lax
from jax.experimental import pallas as pl
from jax.experimental.pallas import tpu as pltpu
from jax.sharding import PartitionSpec as P

SEQ = 128


def causal_mix(values, kernel):
    width = kernel.shape[0]
    length = values.shape[1]
    padded = jnp.pad(values, ((0, 0), (width - 1, 0), (0, 0), (0, 0)))
    total = jnp.zeros_like(values)
    for offset in range(width):
        total = total + kernel[offset] * padded[:, width - 1 - offset : width - 1 - offset + length]
    return total


def causal_mix_back(grads, kernel):
    width = kernel.shape[0]
    length = grads.shape[1]
    padded = jnp.pad(grads, ((0, 0), (0, width - 1), (0, 0), (0, 0)))
    total = jnp.zeros_like(grads)
    for offset in range(width):
        total = total + kernel[offset] * padded[:, offset : offset + length]
    return total


def kernel_terms(values, grads, width):
    length = values.shape[1]
    padded = jnp.pad(values, ((0, 0), (width - 1, 0), (0, 0), (0, 0)))
    terms = []
    for offset in range(width):
        shifted = padded[:, width - 1 - offset : width - 1 - offset + length]
        terms.append(jnp.sum(shifted * grads, axis=(0, 1)))
    return jnp.stack(terms, axis=0)


def gated_grads(tokens, in_weight, kernel, out_grad):
    rows = tokens.shape[0]
    chans = in_weight.shape[2]
    mixed = jnp.einsum("td,sdc->tsc", tokens, in_weight, preferred_element_type=jnp.float32)
    stored = lax.optimization_barrier(mixed.astype(jnp.bfloat16))
    values = stored.astype(jnp.float32).reshape(rows // SEQ, SEQ, 3, chans)
    conv = causal_mix(values, kernel)
    query = conv[:, :, 0]
    keyed = conv[:, :, 1]
    valued = conv[:, :, 2]
    upstream = out_grad.astype(jnp.float32).reshape(rows // SEQ, SEQ, chans)
    conv_grad = jnp.stack(
        [upstream * keyed * valued, upstream * query * valued, upstream * query * keyed], axis=2
    )
    mixed_grad = causal_mix_back(conv_grad, kernel).reshape(rows, 3, chans)
    return mixed_grad, kernel_terms(values, conv_grad, kernel.shape[0])


def plain(tokens, in_weight, kernel, out_grad):
    features = tokens.shape[1]
    chans = in_weight.shape[2]
    scale = 1.0 / math.sqrt(tokens.shape[0] * lax.axis_size("rep"))
    wide_grad, taps = gated_grads(tokens, in_weight, kernel, out_grad)
    mixed_grad = wide_grad.astype(jnp.bfloat16)
    partial_grad = jnp.einsum(
        "tsc,sdc->td", mixed_grad, in_weight, preferred_element_type=jnp.float32
    )
    token_grad = lax.psum_scatter(partial_grad, "shard", scatter_dimension=1, tiled=True).astype(
        jnp.bfloat16
    )
    local_grad = (
        jnp.einsum("td,tsc->sdc", tokens, mixed_grad, preferred_element_type=jnp.float32) * scale
    )
    weight_grad = lax.psum_scatter(
        local_grad.reshape(3 * features, chans), "rep", scatter_dimension=0, tiled=True
    )
    kernel_grad = lax.psum(taps * scale, "rep")
    return (token_grad, weight_grad, kernel_grad)


LEVELS = 4
BLOCK = 512
BLOCKS = 8
OWN = 6
HALF = 3
LANES = 128
VMEM = pl.BlockSpec(memory_space=pltpu.VMEM)
SMEM = pl.BlockSpec(memory_space=pltpu.SMEM)
PARAMS = pltpu.CompilerParams(vmem_limit_bytes=48 * 2**20)
ANY = pl.BlockSpec(memory_space=pl.ANY)
PAIRS = ((0, 1), (1, 0), (2, 3), (3, 2))
MIDDLE = ((1, 2), (2, 1))
OUTWARD = ((1, 0), (2, 3))
ENDS = (0, 3)
INNER = (1, 2)


def ordered(body, arrays, in_specs, after=(), **call):
    count = len(arrays)

    def short(*refs):
        body(*refs[:count], *refs[count + len(after) :])

    return pl.pallas_call(
        short,
        in_specs=list(in_specs) + [ANY] * len(after),
        compiler_params=PARAMS,
        **call,
    )(*arrays, *after)


def lines(array, hops):
    perm = [(2 * a + y, 2 * b + y) for a, b in hops for y in range(2)]
    return lax.ppermute(array, "rep", perm)


def sides(array, levels=range(LEVELS)):
    return lax.ppermute(array, "rep", [(2 * z + y, 2 * z + 1 - y) for z in levels for y in range(2)])


def share(array):
    across = lax.ppermute(array, "shard", [(q, q ^ 2) for q in range(4)])
    beside = lax.ppermute(array, "shard", [(q, q ^ 1) for q in range(4)])
    both = lax.ppermute(across, "shard", [(q, q ^ 1) for q in range(4)])
    return (array, beside, across, both)


def device_block(level, column, i):
    return lax.rem(OWN * level + HALF * column + i, BLOCKS)


def turn_tokens(place, tokens):
    rows = tokens.shape[0]
    slab = BLOCK // 4

    def body(place, tokens, piece, theirs):
        start = pl.multiple_of(place[2] * slab, slab)
        for b in range(BLOCKS):
            piece[b] = tokens[:, pl.ds(pl.multiple_of(BLOCK * b + start, slab), slab)].astype(
                jnp.float32
            ).T
        for i in range(HALF):
            theirs[i] = piece[device_block(place[0], 1 - place[1], i)]

    return pl.pallas_call(
        body,
        out_shape=(
            jax.ShapeDtypeStruct((BLOCKS, slab, rows), jnp.float32),
            jax.ShapeDtypeStruct((HALF, slab, rows), jnp.float32),
        ),
        in_specs=[SMEM, VMEM],
        out_specs=(VMEM, VMEM),
        compiler_params=PARAMS,
        name="turn_tokens",
    )(place, tokens)


def other_blocks(place, inner, ends=None, after=()):
    def body(place, *refs):
        inner, out = refs[0], refs[-1]
        for i in range(HALF):
            if ends is None:
                out[i] = inner[device_block(place[0], 1 - place[1], i)]
                continue
            inside = jnp.logical_or(place[0] == 1, place[0] == 2)

            @pl.when(inside)
            def _():
                out[i] = inner[device_block(place[0], 1 - place[1], i)]

            @pl.when(jnp.logical_not(inside))
            def _():
                out[i] = refs[1][HALF * (1 - place[1]) + i]

    arrays = (place, inner) if ends is None else (place, inner, ends)
    return ordered(
        body,
        arrays,
        [SMEM] + [VMEM] * (len(arrays) - 1),
        after,
        out_shape=jax.ShapeDtypeStruct((HALF,) + inner.shape[1:], inner.dtype),
        out_specs=VMEM,
        name="other_blocks",
    )


def own_blocks(place, got, inner, ends=None, after=()):
    def body(place, got, *refs):
        inner, out = refs[0], refs[-1]
        for i in range(HALF):
            out[HALF + i] = got[i]
            if ends is None:
                out[i] = inner[device_block(place[0], place[1], i)]
                continue
            inside = jnp.logical_or(place[0] == 1, place[0] == 2)

            @pl.when(inside)
            def _():
                out[i] = inner[device_block(place[0], place[1], i)]

            @pl.when(jnp.logical_not(inside))
            def _():
                out[i] = refs[1][HALF * place[1] + i]

    arrays = (place, got, inner) if ends is None else (place, got, inner, ends)
    return ordered(
        body,
        arrays,
        [SMEM] + [VMEM] * (len(arrays) - 1),
        after,
        out_shape=jax.ShapeDtypeStruct((OWN,) + inner.shape[1:], inner.dtype),
        out_specs=VMEM,
        name="own_blocks",
    )


def gate(place, tokens, in_weight, kernel, out_grad, after=()):
    rows, features = tokens.shape
    chans = in_weight.shape[2]
    taps = kernel.shape[0]
    steps = 4
    width = min(chans, 2 * LANES)
    deep = features // steps
    pad = 8

    def body(place, tokens, weight, kernel, out_grad, own, grad, wide, inner, middle, total, held, pads, back):
        step = pl.program_id(1)
        for s in range(3):
            now = jnp.dot(tokens[...], weight[s], preferred_element_type=jnp.float32)

            @pl.when(step == 0)
            def _():
                total[s] = now

            @pl.when(step > 0)
            def _():
                total[s] += now

        @pl.when(step == steps - 1)
        def _():
            blank = jnp.zeros((pad, LANES), jnp.float32)
            for lane in range(0, width, LANES):
                lanes = slice(lane, lane + LANES)
                sums = [[None] * taps for _ in range(3)]
                for q in range(rows // SEQ):
                    here = slice(q * SEQ, (q + 1) * SEQ)
                    conv = []
                    for s in range(3):
                        values = total[s, here, lanes].astype(jnp.bfloat16).astype(jnp.float32)
                        pads[s, 0:pad, :] = blank
                        pads[s, pad : pad + SEQ, :] = values
                        mix = kernel[0, s : s + 1, lanes] * values
                        for j in range(1, taps):
                            mix += kernel[j, s : s + 1, lanes] * pads[s, pad - j : pad - j + SEQ, :]
                        conv.append(mix)
                    up = out_grad[here, lanes].astype(jnp.float32)
                    query, keyed, valued = conv
                    grads = (up * keyed * valued, up * query * valued, up * query * keyed)
                    for s in range(3):
                        back[s, 0:SEQ, :] = grads[s]
                        back[s, SEQ : SEQ + pad, :] = blank
                    for s in range(3):
                        values = pads[s, pad : pad + SEQ, :]
                        mixed = None
                        for j in range(taps):
                            moved = back[s, j : j + SEQ, :]
                            term = kernel[j, s : s + 1, lanes] * moved
                            mixed = term if mixed is None else mixed + term
                            folded = jnp.sum((values * moved).reshape(SEQ // 8, 8, LANES), axis=0)
                            sums[s][j] = folded if q == 0 else sums[s][j] + folded
                        held[s, here, lanes] = mixed
                for s in range(3):
                    for j in range(taps):
                        grad[j, s : s + 1, lanes] = jnp.sum(sums[s][j], axis=0, keepdims=True)
            for s in range(3):
                own[s] = held[s].astype(jnp.bfloat16)
                wide[s] = held[s]
            level = place[0]
            low = jnp.where(level <= 1, 0, 1)
            for i in range(2):
                inner[i] = held[low + i]
                middle[i] = held[1 - low + i]

    three = jax.ShapeDtypeStruct((3, rows, chans), jnp.float32)
    two = jax.ShapeDtypeStruct((2, rows, chans), jnp.float32)
    return ordered(
        body,
        (place, tokens, in_weight, kernel, out_grad),
        [
            SMEM,
            pl.BlockSpec((rows, deep), lambda c, k: (0, k)),
            pl.BlockSpec((3, deep, width), lambda c, k: (0, k, c)),
            pl.BlockSpec((taps, 3, width), lambda c, k: (0, 0, c)),
            pl.BlockSpec((rows, width), lambda c, k: (0, c)),
        ],
        after,
        out_shape=(
            jax.ShapeDtypeStruct((3, rows, chans), jnp.bfloat16),
            jax.ShapeDtypeStruct((taps, 3, chans), jnp.float32),
            three,
            two,
            two,
        ),
        grid=(chans // width, steps),
        out_specs=(
            pl.BlockSpec((3, rows, width), lambda c, k: (0, 0, c)),
            pl.BlockSpec((taps, 3, width), lambda c, k: (0, 0, c)),
            pl.BlockSpec((3, rows, width), lambda c, k: (0, 0, c)),
            pl.BlockSpec((2, rows, width), lambda c, k: (0, 0, c)),
            pl.BlockSpec((2, rows, width), lambda c, k: (0, 0, c)),
        ),
        scratch_shapes=[
            pltpu.VMEM((3, rows, width), jnp.float32),
            pltpu.VMEM((3, rows, width), jnp.float32),
            pltpu.VMEM((3, pad + SEQ, LANES), jnp.float32),
            pltpu.VMEM((3, SEQ + pad, LANES), jnp.float32),
        ],
        name="gate",
    )


def relay_payloads(place, pair, after=()):
    def body(place, pair, across, side):
        low = jnp.where(place[0] <= 1, 0, 1)
        for i in range(2):
            across[i] = pair[1 - low + i]
            side[i] = pair[low + i]

    two = jax.ShapeDtypeStruct((2,) + pair.shape[1:], pair.dtype)
    return ordered(
        body,
        (place, pair),
        [SMEM, VMEM],
        after,
        out_shape=(two, two),
        out_specs=(VMEM, VMEM),
        name="relay_payloads",
    )


def part_of(place, array, step, count, after=()):
    def body(place, array, out):
        start = jnp.where(place[0] <= 1, 0, step)
        for i in range(count):
            out[i] = array[start + i]

    return ordered(
        body,
        (place, array),
        [SMEM, VMEM],
        after,
        out_shape=jax.ShapeDtypeStruct((count,) + array.shape[1:], array.dtype),
        out_specs=VMEM,
        name="part_of",
    )


def add(a, b, scale, after=()):
    def body(a, b, out):
        out[...] = (a[...] + b[...]) * scale

    return ordered(
        body,
        (a, b),
        [VMEM, VMEM],
        after,
        out_shape=jax.ShapeDtypeStruct(a.shape, a.dtype),
        out_specs=VMEM,
        name="add",
    )


def arrange_tokens(place, own, slots, after=()):
    slab = BLOCK // 4
    rows = slots[0][0].shape[2]
    counts = [slot[0].shape[0] // HALF for slot in slots]
    total = (0 if own is None else 1) + sum(counts)

    def body(place, *refs):
        out = refs[-1]
        at = 0
        if own is not None:
            for i in range(HALF):
                block = device_block(place[0], place[1], i)
                columns = pl.ds(pl.multiple_of(block * BLOCK, BLOCK), BLOCK)
                out[i, :, 0:rows] = refs[0][:, columns].T
            refs = refs[1:]
            at = 1
        for n, count in enumerate(counts):
            for c in range(count):
                for i in range(HALF):
                    for k in range(4):
                        where = pl.multiple_of(jnp.bitwise_xor(place[2], k) * slab, slab)
                        out[i, pl.ds(where, slab), (at + c) * rows : (at + c + 1) * rows] = refs[
                            4 * n + k
                        ][HALF * c + i].astype(jnp.bfloat16)
            at += count

    arrays = [place] + ([] if own is None else [own]) + [piece for slot in slots for piece in slot]
    return ordered(
        body,
        arrays,
        [SMEM] + [VMEM] * (len(arrays) - 1),
        after,
        out_shape=jax.ShapeDtypeStruct((HALF, BLOCK, total * rows), jnp.bfloat16),
        out_specs=VMEM,
        name="arrange_tokens",
    )


def weight_part(place, tok, slots, scale=None, so_far=None, after=()):
    rows, chans = slots[0][0].shape[1:]
    count = len(slots)
    arrays = [a for slot in slots for a in slot if a is not None]

    def body(place, tok, *refs):
        out, held = refs[-2], refs[-1]
        level, column = place[0], place[1]
        i = pl.program_id(0)
        inside = jnp.logical_or(level == 1, level == 2)
        high = jnp.where(level <= 1, 0, 1)

        @pl.when(i == 0)
        def _():
            left = list(refs)
            for at, (streams, ends) in enumerate(slots):
                here = slice(at * rows, (at + 1) * rows)
                ref = left.pop(0)
                if streams.shape[0] == 3:
                    major = jnp.where(inside, level - 1 + column, 2 * high)
                    minor = 1
                else:
                    major = jnp.where(inside, column, high)
                    minor = 1 - high
                if ends is None:
                    held[0, here, :] = ref[major].astype(jnp.bfloat16)
                else:
                    end = left.pop(0)

                    @pl.when(inside)
                    def _():
                        held[0, here, :] = ref[major].astype(jnp.bfloat16)

                    @pl.when(jnp.logical_not(inside))
                    def _():
                        held[0, here, :] = end[0].astype(jnp.bfloat16)

                held[1, here, :] = ref[minor].astype(jnp.bfloat16)

        second = jnp.logical_or(
            jnp.logical_and(jnp.logical_and(level == 1, column == 0), i == 2),
            jnp.logical_and(jnp.logical_and(level == 2, column == 1), i == 0),
        )
        got = jnp.dot(
            tok[...], held[second.astype(jnp.int32)], preferred_element_type=jnp.float32
        )
        if so_far is not None:
            got = got + refs[-3][...]
        out[...] = got if scale is None else got * scale

    whole = lambda a: pl.BlockSpec(a.shape, lambda i: (0,) * a.ndim)
    more = [] if so_far is None else [so_far]
    part = pl.BlockSpec((BLOCK, chans), lambda i: (i, 0))
    return ordered(
        body,
        [place, tok] + arrays + more,
        [SMEM, pl.BlockSpec((None, BLOCK, count * rows), lambda i: (i, 0, 0))]
        + [whole(a) for a in arrays]
        + [part] * len(more),
        after,
        out_shape=jax.ShapeDtypeStruct((HALF * BLOCK, chans), jnp.float32),
        grid=(HALF,),
        out_specs=part,
        scratch_shapes=[pltpu.VMEM((2, count * rows, chans), jnp.bfloat16)],
        name="weight_part",
    )


def token_part(grads, weight, after=()):
    rows, chans = grads.shape[1:]
    wide = weight.shape[1] // 4

    def body(grads, weight, out):
        now = lax.dot_general(
            grads[...], weight[...], (((1,), (1,)), ((), ())), preferred_element_type=jnp.float32
        )

        @pl.when(pl.program_id(1) == 0)
        def _():
            out[...] = now

        @pl.when(pl.program_id(1) > 0)
        def _():
            out[...] += now

    return ordered(
        body,
        (grads, weight),
        [
            pl.BlockSpec((None, rows, chans), lambda i, s: (s, 0, 0)),
            pl.BlockSpec((None, wide, chans), lambda i, s: (s, i, 0)),
        ],
        after,
        out_shape=jax.ShapeDtypeStruct((rows, 4 * wide), jnp.float32),
        grid=(4, 3),
        out_specs=pl.BlockSpec((rows, wide), lambda i, s: (0, i)),
        name="token_part",
    )


def lined(tokens, in_weight, kernel, out_grad):
    rows, features = tokens.shape
    rep = lax.axis_index("rep")
    level, column = rep // 2, rep % 2
    place = jnp.stack([level, column, lax.axis_index("shard")]).astype(jnp.int32)
    scale = 1.0 / math.sqrt(rows * lax.axis_size("rep"))

    def tap_step(taps, bit):
        return lax.ppermute(taps, "rep", [(r, r ^ bit) for r in range(2 * LEVELS)])

    piece, theirs = turn_tokens(place, tokens)
    near = lines(piece, PAIRS)
    mid = lines(piece, MIDDLE)
    got0 = sides(theirs)
    own, taps, wide, inner_out, middle_out = gate(
        place, tokens, in_weight, kernel, out_grad, after=(theirs,)
    )
    pair = lines(wide, PAIRS)
    own_y = sides(inner_out)
    slots = [share(got0)]

    far = lines(near, MIDDLE)
    send1 = other_blocks(place, near, after=(inner_out,))
    got1 = sides(send1)
    send = part_of(place, mid, BLOCKS - OWN, OWN, after=(near, send1))
    outer2 = lines(send, OUTWARD)
    middle = lines(middle_out, MIDDLE)
    partial = token_part(own, in_weight, after=(send, slots[0][1]))
    token_grad = lax.psum_scatter(partial, "shard", scatter_dimension=1, tiled=True)

    tap1 = tap_step(taps, 1)
    send2 = other_blocks(place, mid, outer2, after=(partial, slots[0][3]))
    got2 = sides(send2)
    send = part_of(place, far, BLOCKS - OWN, OWN, after=(send2,))
    outer3 = lines(send, OUTWARD)
    own1 = own_blocks(place, got1, near, after=(send,))
    slots.append(share(own1))
    relay_out, side1_out = relay_payloads(place, pair, after=(own1,))
    relayed = lines(relay_out, MIDDLE)
    side1 = sides(side1_out)
    taps = add(taps, tap1, 1.0, after=(relay_out,))
    own2 = own_blocks(place, got2, mid, outer2, after=(taps, own_y))
    slots.append(share(own2))
    tap2 = tap_step(taps, 2)
    send3 = other_blocks(place, far, outer3, after=(own2,))
    got3 = sides(send3)
    send = part_of(place, middle, 1, 1, after=(send3,))
    middle_end = lines(send, OUTWARD)
    side2 = sides(middle, INNER)
    own3 = own_blocks(place, got3, far, outer3, after=(send,))
    slots.append(share(own3))
    taps = add(taps, tap2, 1.0, after=(own3,))
    tap4 = tap_step(taps, 4)
    side2_end = sides(middle_end, ENDS)
    send = part_of(place, relayed, 1, 1, after=(taps,))
    relayed_end = lines(send, OUTWARD)
    side3 = sides(relayed, INNER)
    tok = arrange_tokens(place, tokens, slots[:3], after=(send,))
    early = [(own, None), (own_y, None), (pair, None), (side1, None)]
    early += [(middle, middle_end), (side2, side2_end)]
    so_far = weight_part(place, tok, early)
    tok = arrange_tokens(place, None, slots[3:], after=(so_far,))
    taps = add(taps, tap4, scale, after=(tok,))
    side3_end = sides(relayed_end, ENDS)
    weight_grad = weight_part(
        place,
        tok,
        [(relayed, relayed_end), (side3, side3_end)],
        scale,
        so_far,
        after=(taps,),
    )
    return (token_grad.astype(jnp.bfloat16), weight_grad, taps)


def solution(mesh):
    placed = (P("rep", None), P(None, None, "shard"), P(None, None, "shard"), P("rep", "shard"))
    line = mesh.shape["rep"] == 2 * LEVELS and mesh.shape["shard"] == 4
    return jax.shard_map(
        lined if line else plain,
        mesh=mesh,
        in_specs=placed,
        out_specs=(P("rep", "shard"), P("rep", "shard"), P(None, None, "shard")),
        check_vma=False,
    )
```

```python
import functools
import math

import jax
import jax.numpy as jnp
from jax import lax
from jax.experimental import pallas as pl
from jax.experimental.pallas import tpu as pltpu
from jax.sharding import PartitionSpec as P

SEQ = 128


def causal_mix(values, kernel):
    width = kernel.shape[0]
    length = values.shape[1]
    padded = jnp.pad(values, ((0, 0), (width - 1, 0), (0, 0), (0, 0)))
    total = jnp.zeros_like(values)
    for offset in range(width):
        total = total + kernel[offset] * padded[:, width - 1 - offset : width - 1 - offset + length]
    return total


def causal_mix_back(grads, kernel):
    width = kernel.shape[0]
    length = grads.shape[1]
    padded = jnp.pad(grads, ((0, 0), (0, width - 1), (0, 0), (0, 0)))
    total = jnp.zeros_like(grads)
    for offset in range(width):
        total = total + kernel[offset] * padded[:, offset : offset + length]
    return total


def kernel_terms(values, grads, width):
    length = values.shape[1]
    padded = jnp.pad(values, ((0, 0), (width - 1, 0), (0, 0), (0, 0)))
    terms = []
    for offset in range(width):
        shifted = padded[:, width - 1 - offset : width - 1 - offset + length]
        terms.append(jnp.sum(shifted * grads, axis=(0, 1)))
    return jnp.stack(terms, axis=0)


def gated_grads(tokens, in_weight, kernel, out_grad):
    rows = tokens.shape[0]
    chans = in_weight.shape[2]
    mixed = jnp.einsum("td,sdc->tsc", tokens, in_weight, preferred_element_type=jnp.float32)
    stored = lax.optimization_barrier(mixed.astype(jnp.bfloat16))
    values = stored.astype(jnp.float32).reshape(rows // SEQ, SEQ, 3, chans)
    conv = causal_mix(values, kernel)
    query = conv[:, :, 0]
    keyed = conv[:, :, 1]
    valued = conv[:, :, 2]
    upstream = out_grad.astype(jnp.float32).reshape(rows // SEQ, SEQ, chans)
    conv_grad = jnp.stack(
        [upstream * keyed * valued, upstream * query * valued, upstream * query * keyed], axis=2
    )
    mixed_grad = causal_mix_back(conv_grad, kernel).reshape(rows, 3, chans)
    return mixed_grad, kernel_terms(values, conv_grad, kernel.shape[0])


def plain(tokens, in_weight, kernel, out_grad):
    features = tokens.shape[1]
    chans = in_weight.shape[2]
    scale = 1.0 / math.sqrt(tokens.shape[0] * lax.axis_size("rep"))
    wide_grad, taps = gated_grads(tokens, in_weight, kernel, out_grad)
    mixed_grad = wide_grad.astype(jnp.bfloat16)
    partial_grad = jnp.einsum(
        "tsc,sdc->td", mixed_grad, in_weight, preferred_element_type=jnp.float32
    )
    token_grad = lax.psum_scatter(partial_grad, "shard", scatter_dimension=1, tiled=True).astype(
        jnp.bfloat16
    )
    local_grad = (
        jnp.einsum("td,tsc->sdc", tokens, mixed_grad, preferred_element_type=jnp.float32) * scale
    )
    weight_grad = lax.psum_scatter(
        local_grad.reshape(3 * features, chans), "rep", scatter_dimension=0, tiled=True
    )
    kernel_grad = lax.psum(taps * scale, "rep")
    return (token_grad, weight_grad, kernel_grad)


LEVELS = 4
BLOCK = 512
BLOCKS = 8
OWN = 6
HALF = 3
LANES = 128
VMEM = pl.BlockSpec(memory_space=pltpu.VMEM)
SMEM = pl.BlockSpec(memory_space=pltpu.SMEM)
ANY = pl.BlockSpec(memory_space=pl.ANY)
PARAMS = pltpu.CompilerParams(vmem_limit_bytes=48 * 2**20)
NOTHING = pl.CostEstimate(flops=128, bytes_accessed=128, transcendentals=0)
PAIRS = ((0, 1), (1, 0), (2, 3), (3, 2))
INWARD = ((0, 1), (3, 2))
MIDDLE = ((1, 2), (2, 1))
OUTWARD = ((1, 0), (2, 3))


class Order:
    def __init__(self, clock):
        self.clock = clock

    def call(self, body, arrays, in_specs, *, out_shape, out_specs, scalars=(), grid=(), scratch_shapes=(), name):
        several = isinstance(out_shape, tuple)
        shapes = out_shape if several else (out_shape,)
        specs = tuple(out_specs) if several else (out_specs,)
        held, count, outs = len(scalars), len(arrays), len(shapes)

        def short(*refs):
            ins = refs[: held + count]
            rest = refs[held + count + 1 :]
            body(*ins, *rest[:outs], *rest[outs + 1 :])

        result = pl.pallas_call(
            short,
            out_shape=shapes + (jax.ShapeDtypeStruct(self.clock.shape, self.clock.dtype),),
            grid_spec=pltpu.PrefetchScalarGridSpec(
                num_scalar_prefetch=held,
                grid=grid,
                in_specs=list(in_specs) + [ANY],
                out_specs=specs + (ANY,),
                scratch_shapes=scratch_shapes,
            ),
            input_output_aliases={held + count: outs},
            compiler_params=PARAMS,
            cost_estimate=NOTHING,
            name=name,
        )(*scalars, *arrays, self.clock)
        self.clock = result[-1]
        return result[:-1] if several else result[0]

    def wait(self, *arrays):
        def body(*refs):
            pass

        every = arrays + (self.clock,)
        result = pl.pallas_call(
            body,
            out_shape=tuple(jax.ShapeDtypeStruct(a.shape, a.dtype) for a in every),
            in_specs=[ANY] * len(every),
            out_specs=(ANY,) * len(every),
            input_output_aliases={i: i for i in range(len(every))},
            cost_estimate=NOTHING,
            name="wait",
        )(*every)
        self.clock = result[-1]
        return result[0] if len(arrays) == 1 else result[:-1]


def lines(array, hops):
    perm = [(2 * a + y, 2 * b + y) for a, b in hops for y in range(2)]
    return lax.ppermute(array, "rep", perm)


def flipped(array, axis, flip):
    return lax.ppermute(array, axis, [(r, r ^ flip) for r in range(lax.axis_size(axis))])


def device_block(level, column, i):
    return lax.rem(OWN * level + HALF * column + i, BLOCKS)


def turn_tokens(order, place, tokens):
    rows = tokens.shape[0]
    slab = BLOCK // 4

    def body(place, tokens, piece):
        start = pl.multiple_of(place[2] * slab, slab)
        for b in range(BLOCKS):
            piece[b] = tokens[:, pl.ds(pl.multiple_of(BLOCK * b + start, slab), slab)].astype(
                jnp.float32
            ).T

    return order.call(
        body,
        (place, tokens),
        [SMEM, VMEM],
        out_shape=jax.ShapeDtypeStruct((BLOCKS, slab, rows), jnp.float32),
        out_specs=VMEM,
        name="turn_tokens",
    )


def column_blocks(order, place, slots, own, got=None, part=(0, 0)):
    arrays = [a for slot in slots for a in slot if a is not None]
    begin, extra = part
    first = slots[0][0]
    count = HALF * len(slots)

    def body(place, *refs):
        out = refs[-1]
        left = list(refs)
        column = place[1] if own else 1 - place[1]
        inside = jnp.logical_or(place[0] == 1, place[0] == 2)
        for n, (_, ends) in enumerate(slots):
            inner = left.pop(0)
            end = None if ends is None else left.pop(0)
            for i in range(HALF):
                block = device_block(place[0], column, i)
                if end is None:
                    out[HALF * n + i] = inner[block]
                    continue

                @pl.when(inside)
                def _():
                    out[HALF * n + i] = inner[block]

                @pl.when(jnp.logical_not(inside))
                def _():
                    out[HALF * n + i] = end[HALF * column + i]

        for i in range(extra):
            out[count + i] = left[0][begin + i]

    return order.call(
        body,
        [place] + arrays + ([] if got is None else [got]),
        [SMEM] + [VMEM] * (len(arrays) + (extra > 0)),
        out_shape=jax.ShapeDtypeStruct((count + extra,) + first.shape[1:], first.dtype),
        out_specs=VMEM,
        name="own_blocks" if own else "other_blocks",
    )


def gate(order, place, tokens, in_weight, kernel, out_grad):
    rows, features = tokens.shape
    chans = in_weight.shape[2]
    taps = kernel.shape[0]
    steps = 4
    width = min(chans, 2 * LANES)
    deep = features // steps
    pad = 8

    def body(place, tokens, weight, kernel, out_grad, own, grad, first, inner, middle, total, held, pads, back):
        step = pl.program_id(1)
        for s in range(3):
            now = jnp.dot(tokens[...], weight[s], preferred_element_type=jnp.float32)

            @pl.when(step == 0)
            def _():
                total[s] = now

            @pl.when(step > 0)
            def _():
                total[s] += now

        @pl.when(step == steps - 1)
        def _():
            blank = jnp.zeros((pad, LANES), jnp.float32)
            for lane in range(0, width, LANES):
                lanes = slice(lane, lane + LANES)
                sums = [[None] * taps for _ in range(3)]
                for q in range(rows // SEQ):
                    here = slice(q * SEQ, (q + 1) * SEQ)
                    conv = []
                    for s in range(3):
                        values = total[s, here, lanes].astype(jnp.bfloat16).astype(jnp.float32)
                        pads[s, 0:pad, :] = blank
                        pads[s, pad : pad + SEQ, :] = values
                        mix = kernel[0, s : s + 1, lanes] * values
                        for j in range(1, taps):
                            mix += kernel[j, s : s + 1, lanes] * pads[s, pad - j : pad - j + SEQ, :]
                        conv.append(mix)
                    up = out_grad[here, lanes].astype(jnp.float32)
                    query, keyed, valued = conv
                    grads = (up * keyed * valued, up * query * valued, up * query * keyed)
                    for s in range(3):
                        back[s, 0:SEQ, :] = grads[s]
                        back[s, SEQ : SEQ + pad, :] = blank
                    for s in range(3):
                        values = pads[s, pad : pad + SEQ, :]
                        mixed = None
                        for j in range(taps):
                            moved = back[s, j : j + SEQ, :]
                            term = kernel[j, s : s + 1, lanes] * moved
                            mixed = term if mixed is None else mixed + term
                            folded = jnp.sum((values * moved).reshape(SEQ // 8, 8, LANES), axis=0)
                            sums[s][j] = folded if q == 0 else sums[s][j] + folded
                        held[s, here, lanes] = mixed
                for s in range(3):
                    for j in range(taps):
                        grad[j, s : s + 1, lanes] = jnp.sum(sums[s][j], axis=0, keepdims=True)
            for s in range(3):
                own[s] = held[s].astype(jnp.bfloat16)
            level = place[0]
            first[0] = held[2 - 2 * lax.rem(level, 2)]
            low = jnp.where(level <= 1, 0, 1)
            for i in range(2):
                inner[i] = held[low + i]
                middle[i] = held[1 - low + i]

    one = jax.ShapeDtypeStruct((1, rows, chans), jnp.float32)
    two = jax.ShapeDtypeStruct((2, rows, chans), jnp.float32)
    return order.call(
        body,
        (place, tokens, in_weight, kernel, out_grad),
        [
            SMEM,
            pl.BlockSpec((rows, deep), lambda c, k: (0, k)),
            pl.BlockSpec((3, deep, width), lambda c, k: (0, k, c)),
            pl.BlockSpec((taps, 3, width), lambda c, k: (0, 0, c)),
            pl.BlockSpec((rows, width), lambda c, k: (0, c)),
        ],
        out_shape=(
            jax.ShapeDtypeStruct((3, rows, chans), jnp.bfloat16),
            jax.ShapeDtypeStruct((taps, 3, chans), jnp.float32),
            one,
            two,
            two,
        ),
        grid=(chans // width, steps),
        out_specs=(
            pl.BlockSpec((3, rows, width), lambda c, k: (0, 0, c)),
            pl.BlockSpec((taps, 3, width), lambda c, k: (0, 0, c)),
            pl.BlockSpec((1, rows, width), lambda c, k: (0, 0, c)),
            pl.BlockSpec((2, rows, width), lambda c, k: (0, 0, c)),
            pl.BlockSpec((2, rows, width), lambda c, k: (0, 0, c)),
        ),
        scratch_shapes=[
            pltpu.VMEM((3, rows, width), jnp.float32),
            pltpu.VMEM((3, rows, width), jnp.float32),
            pltpu.VMEM((3, pad + SEQ, LANES), jnp.float32),
            pltpu.VMEM((3, SEQ + pad, LANES), jnp.float32),
        ],
        name="gate",
    )


def relay_payload(order, place, first, inner):
    def body(place, first, inner, out, side):
        @pl.when(place[0] <= 1)
        def _():
            out[0] = inner[1]
            out[1] = first[0]

        @pl.when(place[0] > 1)
        def _():
            out[0] = first[0]
            out[1] = inner[0]

        level_own(place, inner, first, side)

    two = jax.ShapeDtypeStruct(inner.shape, inner.dtype)
    return order.call(
        body,
        (place, first, inner),
        [SMEM, VMEM, VMEM],
        out_shape=(two, two),
        out_specs=(VMEM, VMEM),
        name="relay_payload",
    )


def level_own(place, inner, ends, out):
    inside = jnp.logical_or(place[0] == 1, place[0] == 2)

    @pl.when(inside)
    def _():
        out[...] = inner[...]

    @pl.when(jnp.logical_not(inside))
    def _():
        out[jnp.where(place[0] == 0, 0, 1)] = ends[0]
        out[jnp.where(place[0] == 0, 1, 0)] = ends[0]


def side_payload(order, place, inner, ends):
    return order.call(
        level_own,
        (place, inner, ends),
        [SMEM, VMEM, VMEM],
        out_shape=jax.ShapeDtypeStruct(inner.shape, inner.dtype),
        out_specs=VMEM,
        name="side_payload",
    )


def part_of(order, place, array, step, count):
    def body(place, array, out):
        start = jnp.where(place[0] <= 1, 0, step)
        for i in range(count):
            out[i] = array[start + i]

    return order.call(
        body,
        (place, array),
        [SMEM, VMEM],
        out_shape=jax.ShapeDtypeStruct((count,) + array.shape[1:], array.dtype),
        out_specs=VMEM,
        name="part_of",
    )


def add(order, mine, other, scale=1.0):
    pair = mine.ndim == 3 and mine.shape[0] == 2

    def body(mine, other, out, again):
        if pair:
            out[...] = mine[1] + other[1]
            again[...] = mine[0] + other[0]
        else:
            total = (mine[...] + other[...]) * scale
            out[...] = total
            again[...] = total

    shape = jax.ShapeDtypeStruct(mine.shape[1:] if pair else mine.shape, mine.dtype)
    return order.call(
        body,
        (mine, other),
        [VMEM] * 2,
        out_shape=(shape, shape),
        out_specs=(VMEM,) * 2,
        name="add",
    )


def arrange_tokens(order, place, own, slots):
    slab = BLOCK // 4
    rows = slots[0][0].shape[2]
    counts = [slot[0].shape[0] // HALF for slot in slots]
    total = (0 if own is None else 1) + sum(counts)

    def body(place, *refs):
        out = refs[-1]
        at = 0
        if own is not None:
            for i in range(HALF):
                block = device_block(place[0], place[1], i)
                columns = pl.ds(pl.multiple_of(block * BLOCK, BLOCK), BLOCK)
                out[i, :, 0:rows] = refs[0][:, columns].T
            refs = refs[1:]
            at = 1
        for n, count in enumerate(counts):
            for c in range(count):
                for i in range(HALF):
                    for k in range(4):
                        where = pl.multiple_of(jnp.bitwise_xor(place[2], k) * slab, slab)
                        out[i, pl.ds(where, slab), (at + c) * rows : (at + c + 1) * rows] = refs[
                            4 * n + k
                        ][HALF * c + i].astype(jnp.bfloat16)
            at += count

    arrays = [place] + ([] if own is None else [own]) + [piece for slot in slots for piece in slot]
    return order.call(
        body,
        arrays,
        [SMEM] + [VMEM] * (len(arrays) - 1),
        out_shape=jax.ShapeDtypeStruct((HALF, BLOCK, total * rows), jnp.bfloat16),
        out_specs=VMEM,
        name="arrange_tokens",
    )


def weight_part(order, place, tok, slots, scale=None, so_far=None):
    rows, chans = slots[0][0].shape[1:]
    count = len(slots)
    arrays = [a for slot in slots for a in slot if a is not None]

    def body(place, tok, *refs):
        out, held = refs[-2], refs[-1]
        level, column = place[0], place[1]
        i = pl.program_id(0)
        inside = jnp.logical_or(level == 1, level == 2)
        high = jnp.where(level <= 1, 0, 1)

        @pl.when(i == 0)
        def _():
            left = list(refs)
            for at, (streams, ends) in enumerate(slots):
                here = slice(at * rows, (at + 1) * rows)
                ref = left.pop(0)
                if streams.shape[0] == 3:
                    major = jnp.where(inside, level - 1 + column, 2 * high)
                    minor = 1
                else:
                    major = jnp.where(inside, column, high)
                    minor = 1 - high
                if ends is None:
                    held[0, here, :] = ref[major].astype(jnp.bfloat16)
                else:
                    end = left.pop(0)

                    @pl.when(inside)
                    def _():
                        held[0, here, :] = ref[major].astype(jnp.bfloat16)

                    @pl.when(jnp.logical_not(inside))
                    def _():
                        held[0, here, :] = end[0].astype(jnp.bfloat16)

                held[1, here, :] = ref[minor].astype(jnp.bfloat16)

        second = jnp.logical_or(
            jnp.logical_and(jnp.logical_and(level == 1, column == 0), i == 2),
            jnp.logical_and(jnp.logical_and(level == 2, column == 1), i == 0),
        )
        got = jnp.dot(
            tok[...], held[second.astype(jnp.int32)], preferred_element_type=jnp.float32
        )
        if so_far is not None:
            got = got + refs[-3][...]
        out[...] = got if scale is None else got * scale

    whole = lambda a: pl.BlockSpec(a.shape, lambda i: (0,) * a.ndim)
    more = [] if so_far is None else [so_far]
    part = pl.BlockSpec((BLOCK, chans), lambda i: (i, 0))
    return order.call(
        body,
        [place, tok] + arrays + more,
        [SMEM, pl.BlockSpec((None, BLOCK, count * rows), lambda i: (i, 0, 0))]
        + [whole(a) for a in arrays]
        + [part] * len(more),
        out_shape=jax.ShapeDtypeStruct((HALF * BLOCK, chans), jnp.float32),
        grid=(HALF,),
        out_specs=part,
        scratch_shapes=[pltpu.VMEM((2, count * rows, chans), jnp.bfloat16)],
        name="weight_part",
    )


def token_part(order, quarters, grads, weight):
    rows, chans = grads.shape[1:]
    wide = weight.shape[1] // 4
    count = quarters.shape[0]

    def body(quarters, grads, weight, out):
        now = lax.dot_general(
            grads[...], weight[...], (((1,), (1,)), ((), ())), preferred_element_type=jnp.float32
        )

        @pl.when(pl.program_id(1) == 0)
        def _():
            out[...] = now

        @pl.when(pl.program_id(1) > 0)
        def _():
            out[...] += now

    return order.call(
        body,
        (grads, weight),
        [
            pl.BlockSpec((None, rows, chans), lambda i, s, quarters: (s, 0, 0)),
            pl.BlockSpec((None, wide, chans), lambda i, s, quarters: (s, quarters[i], 0)),
        ],
        scalars=(quarters,),
        out_shape=jax.ShapeDtypeStruct((count, rows, wide), jnp.float32),
        grid=(count, 3),
        out_specs=pl.BlockSpec((None, rows, wide), lambda i, s, quarters: (i, 0, 0)),
        name="token_part",
    )


def lined(tokens, in_weight, kernel, out_grad):
    rows = tokens.shape[0]
    rep, quarter = lax.axis_index("rep"), lax.axis_index("shard")
    level, column = rep // 2, rep % 2
    place = jnp.stack([level, column, quarter]).astype(jnp.int32)
    scale = 1.0 / math.sqrt(rows * lax.axis_size("rep"))
    order = Order(jnp.zeros((8, LANES), jnp.float32))
    quarters = [jnp.bitwise_xor(quarter, k).astype(jnp.int32) for k in (3, 1, 2, 0)]
    piece = turn_tokens(order, place, tokens)
    near = lines(piece, PAIRS)
    mid = lines(piece, MIDDLE)
    own, taps, first_out, inner_out, middle_out = gate(
        order, place, tokens, in_weight, kernel, out_grad
    )
    own_y = flipped(inner_out, "rep", 1)
    inner = lines(inner_out, INWARD)
    first = lines(first_out, PAIRS)
    middle = lines(middle_out, MIDDLE)
    taps1 = flipped(taps, "rep", 1)
    near = order.wait(near)
    far = lines(near, MIDDLE)
    over = column_blocks(order, place, [(piece, None), (near, None)], False)
    got1 = flipped(over, "rep", 1)
    mid = order.wait(mid)
    outer2 = lines(part_of(order, place, mid, BLOCKS - OWN, OWN), OUTWARD)
    send = token_part(order, jnp.stack(quarters[:2]), own, in_weight)
    summed = flipped(send, "shard", 1)
    keep = token_part(order, jnp.stack(quarters[2:]), own, in_weight)
    own_y, inner, outer2 = order.wait(own_y, inner, outer2)
    over = column_blocks(order, place, [(mid, outer2)], False)
    got2 = flipped(over, "rep", 1)
    far = order.wait(far)
    outer3 = lines(part_of(order, place, far, BLOCKS - OWN, OWN), OUTWARD)
    first = order.wait(first)
    relay, side1 = relay_payload(order, place, first, inner)
    relayed = lines(relay, MIDDLE)
    side1 = flipped(side1, "rep", 1)
    middle, got2 = order.wait(middle, got2)
    own2 = column_blocks(order, place, [(mid, outer2)], True, got2, (0, HALF))
    across2 = flipped(own2, "shard", 2)
    beside2 = flipped(own2, "shard", 1)
    got1 = order.wait(got1)
    own1 = column_blocks(order, place, [(near, None)], True, got1, (0, OWN))
    across1 = flipped(own1, "shard", 2)
    beside1 = flipped(own1, "shard", 1)
    middle_end = lines(part_of(order, place, middle, 1, 1), OUTWARD)
    summed = order.wait(summed)
    token_grad, away = add(order, keep, summed)
    last = flipped(away, "shard", 2)
    across1, beside1, side1, outer3, relayed = order.wait(
        across1, beside1, side1, outer3, relayed
    )
    both1 = flipped(across1, "shard", 1)
    over = column_blocks(order, place, [(far, outer3)], False)
    got3 = flipped(over, "rep", 1)
    middle_end = order.wait(middle_end)
    relayed_end = lines(part_of(order, place, relayed, 1, 1), OUTWARD)
    beside2, taps1 = order.wait(beside2, taps1)
    taps, taps_out = add(order, taps, taps1)
    taps2 = flipped(taps_out, "rep", 2)
    relayed_end = order.wait(relayed_end)
    side2 = flipped(side_payload(order, place, middle, middle_end), "rep", 1)
    across2, got3 = order.wait(across2, got3)
    both2 = flipped(across2, "shard", 1)
    own3 = column_blocks(order, place, [(far, outer3)], True, got3, (0, HALF))
    across3 = flipped(own3, "shard", 2)
    beside3 = flipped(own3, "shard", 1)
    both2, both1 = order.wait(both2, both1)
    side3 = flipped(side_payload(order, place, relayed, relayed_end), "rep", 1)
    tok = arrange_tokens(order, place, tokens, [(own1, beside1, across1, both1)])
    early = [(own, None), (inner, first), (own_y, None), (side1, None)]
    so_far = weight_part(order, place, tok, early)
    side2, across3, beside3 = order.wait(side2, across3, beside3)
    both3 = flipped(across3, "shard", 1)
    both3 = order.wait(both3)
    tok = arrange_tokens(order, place, None, [(own2, beside2, across2, both2)])
    taps2 = order.wait(taps2)
    taps, taps_out = add(order, taps, taps2)
    taps4 = flipped(taps_out, "rep", 4)
    so_far = weight_part(order, place, tok, [(middle, middle_end), (side2, None)], None, so_far)
    last = order.wait(last)
    token_grad = (token_grad + last).astype(jnp.bfloat16)
    tok = arrange_tokens(order, place, None, [(own3, beside3, across3, both3)])
    side3, taps4 = order.wait(side3, taps4)
    taps, _ = add(order, taps, taps4, scale=scale)
    late = [(relayed, relayed_end), (side3, None)]
    weight_grad = weight_part(order, place, tok, late, scale, so_far)
    return (token_grad, weight_grad, taps)


def solution(mesh):
    placed = (P("rep", None), P(None, None, "shard"), P(None, None, "shard"), P("rep", "shard"))
    line = mesh.shape["rep"] == 2 * LEVELS and mesh.shape["shard"] == 4
    return jax.shard_map(
        lined if line else plain,
        mesh=mesh,
        in_specs=placed,
        out_specs=(P("rep", "shard"), P("rep", "shard"), P(None, None, "shard")),
        check_vma=False,
    )
```

```python
import functools
import math

import jax
import jax.numpy as jnp
from jax import lax
from jax.experimental import pallas as pl
from jax.experimental.pallas import tpu as pltpu
from jax.sharding import PartitionSpec as P

SEQ = 128


def causal_mix(values, kernel):
    width = kernel.shape[0]
    length = values.shape[1]
    padded = jnp.pad(values, ((0, 0), (width - 1, 0), (0, 0), (0, 0)))
    total = jnp.zeros_like(values)
    for offset in range(width):
        total = total + kernel[offset] * padded[:, width - 1 - offset : width - 1 - offset + length]
    return total


def causal_mix_back(grads, kernel):
    width = kernel.shape[0]
    length = grads.shape[1]
    padded = jnp.pad(grads, ((0, 0), (0, width - 1), (0, 0), (0, 0)))
    total = jnp.zeros_like(grads)
    for offset in range(width):
        total = total + kernel[offset] * padded[:, offset : offset + length]
    return total


def kernel_terms(values, grads, width):
    length = values.shape[1]
    padded = jnp.pad(values, ((0, 0), (width - 1, 0), (0, 0), (0, 0)))
    terms = []
    for offset in range(width):
        shifted = padded[:, width - 1 - offset : width - 1 - offset + length]
        terms.append(jnp.sum(shifted * grads, axis=(0, 1)))
    return jnp.stack(terms, axis=0)


def gated_grads(tokens, in_weight, kernel, out_grad):
    rows = tokens.shape[0]
    chans = in_weight.shape[2]
    mixed = jnp.einsum("td,sdc->tsc", tokens, in_weight, preferred_element_type=jnp.float32)
    stored = lax.optimization_barrier(mixed.astype(jnp.bfloat16))
    values = stored.astype(jnp.float32).reshape(rows // SEQ, SEQ, 3, chans)
    conv = causal_mix(values, kernel)
    query = conv[:, :, 0]
    keyed = conv[:, :, 1]
    valued = conv[:, :, 2]
    upstream = out_grad.astype(jnp.float32).reshape(rows // SEQ, SEQ, chans)
    conv_grad = jnp.stack(
        [upstream * keyed * valued, upstream * query * valued, upstream * query * keyed], axis=2
    )
    mixed_grad = causal_mix_back(conv_grad, kernel).reshape(rows, 3, chans)
    return mixed_grad, kernel_terms(values, conv_grad, kernel.shape[0])


def plain(tokens, in_weight, kernel, out_grad):
    features = tokens.shape[1]
    chans = in_weight.shape[2]
    scale = 1.0 / math.sqrt(tokens.shape[0] * lax.axis_size("rep"))
    wide_grad, taps = gated_grads(tokens, in_weight, kernel, out_grad)
    mixed_grad = wide_grad.astype(jnp.bfloat16)
    partial_grad = jnp.einsum(
        "tsc,sdc->td", mixed_grad, in_weight, preferred_element_type=jnp.float32
    )
    token_grad = lax.psum_scatter(partial_grad, "shard", scatter_dimension=1, tiled=True).astype(
        jnp.bfloat16
    )
    local_grad = (
        jnp.einsum("td,tsc->sdc", tokens, mixed_grad, preferred_element_type=jnp.float32) * scale
    )
    weight_grad = lax.psum_scatter(
        local_grad.reshape(3 * features, chans), "rep", scatter_dimension=0, tiled=True
    )
    kernel_grad = lax.psum(taps * scale, "rep")
    return (token_grad, weight_grad, kernel_grad)


LEVELS = 4
BLOCK = 512
BLOCKS = 8
OWN = 6
HALF = 3
LANES = 128
VMEM = pl.BlockSpec(memory_space=pltpu.VMEM)
SMEM = pl.BlockSpec(memory_space=pltpu.SMEM)
ANY = pl.BlockSpec(memory_space=pl.ANY)
PARAMS = pltpu.CompilerParams(vmem_limit_bytes=48 * 2**20)
NOTHING = pl.CostEstimate(flops=128, bytes_accessed=128, transcendentals=0)
PAIRS = ((0, 1), (1, 0), (2, 3), (3, 2))
INWARD = ((0, 1), (3, 2))
MIDDLE = ((1, 2), (2, 1))
OUTWARD = ((1, 0), (2, 3))


class Order:
    def __init__(self):
        self.after = []

    def call(self, body, arrays, in_specs, *, out_shape, out_specs, scalars=(), grid=(), scratch_shapes=(), name):
        held, count = len(scalars), len(arrays)
        after = [a for a in self.after if not any(a is b for b in arrays)]

        def short(*refs):
            body(*refs[: held + count], *refs[held + count + len(after) :])

        result = pl.pallas_call(
            short,
            out_shape=out_shape,
            grid_spec=pltpu.PrefetchScalarGridSpec(
                num_scalar_prefetch=held,
                grid=grid,
                in_specs=list(in_specs) + [ANY] * len(after),
                out_specs=out_specs,
                scratch_shapes=scratch_shapes,
            ),
            compiler_params=PARAMS,
            cost_estimate=NOTHING,
            name=name,
        )(*scalars, *arrays, *after)
        self.after = [result[0] if isinstance(result, (list, tuple)) else result]
        return result

    def wait(self, *arrays):
        self.after.extend(arrays)
        return arrays[0] if len(arrays) == 1 else arrays


def lines(array, hops):
    perm = [(2 * a + y, 2 * b + y) for a, b in hops for y in range(2)]
    return lax.ppermute(array, "rep", perm)


def flipped(array, axis, flip):
    return lax.ppermute(array, axis, [(r, r ^ flip) for r in range(lax.axis_size(axis))])


def device_block(level, column, i):
    return lax.rem(OWN * level + HALF * column + i, BLOCKS)


def turn_tokens(order, place, tokens):
    rows = tokens.shape[0]
    slab = BLOCK // 4

    def body(place, tokens, piece):
        start = pl.multiple_of(place[2] * slab, slab)
        for b in range(BLOCKS):
            piece[b] = tokens[:, pl.ds(pl.multiple_of(BLOCK * b + start, slab), slab)].astype(
                jnp.float32
            ).T

    return order.call(
        body,
        (place, tokens),
        [SMEM, VMEM],
        out_shape=jax.ShapeDtypeStruct((BLOCKS, slab, rows), jnp.float32),
        out_specs=VMEM,
        name="turn_tokens",
    )


def column_blocks(order, place, slots, own, got=None, part=(0, 0)):
    arrays = [a for slot in slots for a in slot if a is not None]
    begin, extra = part
    first = slots[0][0]
    count = HALF * len(slots)

    def body(place, *refs):
        out = refs[-1]
        left = list(refs)
        column = place[1] if own else 1 - place[1]
        inside = jnp.logical_or(place[0] == 1, place[0] == 2)
        for n, (_, ends) in enumerate(slots):
            inner = left.pop(0)
            end = None if ends is None else left.pop(0)
            for i in range(HALF):
                block = device_block(place[0], column, i)
                if end is None:
                    out[HALF * n + i] = inner[block]
                    continue

                @pl.when(inside)
                def _():
                    out[HALF * n + i] = inner[block]

                @pl.when(jnp.logical_not(inside))
                def _():
                    out[HALF * n + i] = end[HALF * column + i]

        for i in range(extra):
            out[count + i] = left[0][begin + i]

    return order.call(
        body,
        [place] + arrays + ([] if got is None else [got]),
        [SMEM] + [VMEM] * (len(arrays) + (extra > 0)),
        out_shape=jax.ShapeDtypeStruct((count + extra,) + first.shape[1:], first.dtype),
        out_specs=VMEM,
        name="own_blocks" if own else "other_blocks",
    )


def gate(order, place, tokens, in_weight, kernel, out_grad):
    rows, features = tokens.shape
    chans = in_weight.shape[2]
    taps = kernel.shape[0]
    steps = 4
    width = min(chans, 2 * LANES)
    deep = features // steps
    pad = 8

    def body(place, tokens, weight, kernel, out_grad, own, grad, first, inner, middle, total, held, pads, back):
        step = pl.program_id(1)
        for s in range(3):
            now = jnp.dot(tokens[...], weight[s], preferred_element_type=jnp.float32)

            @pl.when(step == 0)
            def _():
                total[s] = now

            @pl.when(step > 0)
            def _():
                total[s] += now

        @pl.when(step == steps - 1)
        def _():
            blank = jnp.zeros((pad, LANES), jnp.float32)
            for lane in range(0, width, LANES):
                lanes = slice(lane, lane + LANES)
                sums = [[None] * taps for _ in range(3)]
                for q in range(rows // SEQ):
                    here = slice(q * SEQ, (q + 1) * SEQ)
                    conv = []
                    for s in range(3):
                        values = total[s, here, lanes].astype(jnp.bfloat16).astype(jnp.float32)
                        pads[s, 0:pad, :] = blank
                        pads[s, pad : pad + SEQ, :] = values
                        mix = kernel[0, s : s + 1, lanes] * values
                        for j in range(1, taps):
                            mix += kernel[j, s : s + 1, lanes] * pads[s, pad - j : pad - j + SEQ, :]
                        conv.append(mix)
                    up = out_grad[here, lanes].astype(jnp.float32)
                    query, keyed, valued = conv
                    grads = (up * keyed * valued, up * query * valued, up * query * keyed)
                    for s in range(3):
                        back[s, 0:SEQ, :] = grads[s]
                        back[s, SEQ : SEQ + pad, :] = blank
                    for s in range(3):
                        values = pads[s, pad : pad + SEQ, :]
                        mixed = None
                        for j in range(taps):
                            moved = back[s, j : j + SEQ, :]
                            term = kernel[j, s : s + 1, lanes] * moved
                            mixed = term if mixed is None else mixed + term
                            folded = jnp.sum((values * moved).reshape(SEQ // 8, 8, LANES), axis=0)
                            sums[s][j] = folded if q == 0 else sums[s][j] + folded
                        held[s, here, lanes] = mixed
                for s in range(3):
                    for j in range(taps):
                        grad[j, s : s + 1, lanes] = jnp.sum(sums[s][j], axis=0, keepdims=True)
            for s in range(3):
                own[s] = held[s].astype(jnp.bfloat16)
            level = place[0]
            first[0] = held[2 - 2 * lax.rem(level, 2)]
            low = jnp.where(level <= 1, 0, 1)
            for i in range(2):
                inner[i] = held[low + i]
                middle[i] = held[1 - low + i]

    one = jax.ShapeDtypeStruct((1, rows, chans), jnp.float32)
    two = jax.ShapeDtypeStruct((2, rows, chans), jnp.float32)
    return order.call(
        body,
        (place, tokens, in_weight, kernel, out_grad),
        [
            SMEM,
            pl.BlockSpec((rows, deep), lambda c, k: (0, k)),
            pl.BlockSpec((3, deep, width), lambda c, k: (0, k, c)),
            pl.BlockSpec((taps, 3, width), lambda c, k: (0, 0, c)),
            pl.BlockSpec((rows, width), lambda c, k: (0, c)),
        ],
        out_shape=(
            jax.ShapeDtypeStruct((3, rows, chans), jnp.bfloat16),
            jax.ShapeDtypeStruct((taps, 3, chans), jnp.float32),
            one,
            two,
            two,
        ),
        grid=(chans // width, steps),
        out_specs=(
            pl.BlockSpec((3, rows, width), lambda c, k: (0, 0, c)),
            pl.BlockSpec((taps, 3, width), lambda c, k: (0, 0, c)),
            pl.BlockSpec((1, rows, width), lambda c, k: (0, 0, c)),
            pl.BlockSpec((2, rows, width), lambda c, k: (0, 0, c)),
            pl.BlockSpec((2, rows, width), lambda c, k: (0, 0, c)),
        ),
        scratch_shapes=[
            pltpu.VMEM((3, rows, width), jnp.float32),
            pltpu.VMEM((3, rows, width), jnp.float32),
            pltpu.VMEM((3, pad + SEQ, LANES), jnp.float32),
            pltpu.VMEM((3, SEQ + pad, LANES), jnp.float32),
        ],
        name="gate",
    )


def relay_payload(order, place, first, inner):
    def body(place, first, inner, out, side):
        @pl.when(place[0] <= 1)
        def _():
            out[0] = inner[1]
            out[1] = first[0]

        @pl.when(place[0] > 1)
        def _():
            out[0] = first[0]
            out[1] = inner[0]

        level_own(place, inner, first, side)

    two = jax.ShapeDtypeStruct(inner.shape, inner.dtype)
    return order.call(
        body,
        (place, first, inner),
        [SMEM, VMEM, VMEM],
        out_shape=(two, two),
        out_specs=(VMEM, VMEM),
        name="relay_payload",
    )


def level_own(place, inner, ends, out):
    inside = jnp.logical_or(place[0] == 1, place[0] == 2)

    @pl.when(inside)
    def _():
        out[...] = inner[...]

    @pl.when(jnp.logical_not(inside))
    def _():
        out[jnp.where(place[0] == 0, 0, 1)] = ends[0]
        out[jnp.where(place[0] == 0, 1, 0)] = ends[0]


def side_payload(order, place, inner, ends):
    return order.call(
        level_own,
        (place, inner, ends),
        [SMEM, VMEM, VMEM],
        out_shape=jax.ShapeDtypeStruct(inner.shape, inner.dtype),
        out_specs=VMEM,
        name="side_payload",
    )


def part_of(order, place, array, step, count):
    def body(place, array, out):
        start = jnp.where(place[0] <= 1, 0, step)
        for i in range(count):
            out[i] = array[start + i]

    return order.call(
        body,
        (place, array),
        [SMEM, VMEM],
        out_shape=jax.ShapeDtypeStruct((count,) + array.shape[1:], array.dtype),
        out_specs=VMEM,
        name="part_of",
    )


def add(order, mine, other, scale=1.0):
    pair = mine.ndim == 3 and mine.shape[0] == 2

    def body(mine, other, out, again):
        if pair:
            out[...] = mine[1] + other[1]
            again[...] = mine[0] + other[0]
        else:
            total = (mine[...] + other[...]) * scale
            out[...] = total
            again[...] = total

    shape = jax.ShapeDtypeStruct(mine.shape[1:] if pair else mine.shape, mine.dtype)
    return order.call(
        body,
        (mine, other),
        [VMEM] * 2,
        out_shape=(shape, shape),
        out_specs=(VMEM,) * 2,
        name="add",
    )


def arrange_tokens(order, place, own, slots):
    slab = BLOCK // 4
    rows = slots[0][0].shape[2]
    counts = [slot[0].shape[0] // HALF for slot in slots]
    total = (0 if own is None else 1) + sum(counts)

    def body(place, *refs):
        out = refs[-1]
        at = 0
        if own is not None:
            for i in range(HALF):
                block = device_block(place[0], place[1], i)
                columns = pl.ds(pl.multiple_of(block * BLOCK, BLOCK), BLOCK)
                out[i, :, 0:rows] = refs[0][:, columns].T
            refs = refs[1:]
            at = 1
        for n, count in enumerate(counts):
            for c in range(count):
                for i in range(HALF):
                    for k in range(4):
                        where = pl.multiple_of(jnp.bitwise_xor(place[2], k) * slab, slab)
                        out[i, pl.ds(where, slab), (at + c) * rows : (at + c + 1) * rows] = refs[
                            4 * n + k
                        ][HALF * c + i].astype(jnp.bfloat16)
            at += count

    arrays = [place] + ([] if own is None else [own]) + [piece for slot in slots for piece in slot]
    return order.call(
        body,
        arrays,
        [SMEM] + [VMEM] * (len(arrays) - 1),
        out_shape=jax.ShapeDtypeStruct((HALF, BLOCK, total * rows), jnp.bfloat16),
        out_specs=VMEM,
        name="arrange_tokens",
    )


def weight_part(order, place, tok, slots, scale=None, so_far=None):
    rows, chans = slots[0][0].shape[1:]
    count = len(slots)
    arrays = [a for slot in slots for a in slot if a is not None]

    def body(place, tok, *refs):
        out, held = refs[-2], refs[-1]
        level, column = place[0], place[1]
        i = pl.program_id(0)
        inside = jnp.logical_or(level == 1, level == 2)
        high = jnp.where(level <= 1, 0, 1)

        @pl.when(i == 0)
        def _():
            left = list(refs)
            for at, (streams, ends) in enumerate(slots):
                here = slice(at * rows, (at + 1) * rows)
                ref = left.pop(0)
                if streams.shape[0] == 3:
                    major = jnp.where(inside, level - 1 + column, 2 * high)
                    minor = 1
                else:
                    major = jnp.where(inside, column, high)
                    minor = 1 - high
                if ends is None:
                    held[0, here, :] = ref[major].astype(jnp.bfloat16)
                else:
                    end = left.pop(0)

                    @pl.when(inside)
                    def _():
                        held[0, here, :] = ref[major].astype(jnp.bfloat16)

                    @pl.when(jnp.logical_not(inside))
                    def _():
                        held[0, here, :] = end[0].astype(jnp.bfloat16)

                held[1, here, :] = ref[minor].astype(jnp.bfloat16)

        second = jnp.logical_or(
            jnp.logical_and(jnp.logical_and(level == 1, column == 0), i == 2),
            jnp.logical_and(jnp.logical_and(level == 2, column == 1), i == 0),
        )
        got = jnp.dot(
            tok[...], held[second.astype(jnp.int32)], preferred_element_type=jnp.float32
        )
        if so_far is not None:
            got = got + refs[-3][...]
        out[...] = got if scale is None else got * scale

    whole = lambda a: pl.BlockSpec(a.shape, lambda i: (0,) * a.ndim)
    more = [] if so_far is None else [so_far]
    part = pl.BlockSpec((BLOCK, chans), lambda i: (i, 0))
    return order.call(
        body,
        [place, tok] + arrays + more,
        [SMEM, pl.BlockSpec((None, BLOCK, count * rows), lambda i: (i, 0, 0))]
        + [whole(a) for a in arrays]
        + [part] * len(more),
        out_shape=jax.ShapeDtypeStruct((HALF * BLOCK, chans), jnp.float32),
        grid=(HALF,),
        out_specs=part,
        scratch_shapes=[pltpu.VMEM((2, count * rows, chans), jnp.bfloat16)],
        name="weight_part",
    )


def token_part(order, quarters, grads, weight):
    rows, chans = grads.shape[1:]
    wide = weight.shape[1] // 4
    count = quarters.shape[0]

    def body(quarters, grads, weight, out):
        now = lax.dot_general(
            grads[...], weight[...], (((1,), (1,)), ((), ())), preferred_element_type=jnp.float32
        )

        @pl.when(pl.program_id(1) == 0)
        def _():
            out[...] = now

        @pl.when(pl.program_id(1) > 0)
        def _():
            out[...] += now

    return order.call(
        body,
        (grads, weight),
        [
            pl.BlockSpec((None, rows, chans), lambda i, s, quarters: (s, 0, 0)),
            pl.BlockSpec((None, wide, chans), lambda i, s, quarters: (s, quarters[i], 0)),
        ],
        scalars=(quarters,),
        out_shape=jax.ShapeDtypeStruct((count, rows, wide), jnp.float32),
        grid=(count, 3),
        out_specs=pl.BlockSpec((None, rows, wide), lambda i, s, quarters: (i, 0, 0)),
        name="token_part",
    )


def lined(tokens, in_weight, kernel, out_grad):
    rows = tokens.shape[0]
    rep, quarter = lax.axis_index("rep"), lax.axis_index("shard")
    level, column = rep // 2, rep % 2
    place = jnp.stack([level, column, quarter]).astype(jnp.int32)
    scale = 1.0 / math.sqrt(rows * lax.axis_size("rep"))
    order = Order()
    quarters = [jnp.bitwise_xor(quarter, k).astype(jnp.int32) for k in (3, 1, 2, 0)]
    piece = turn_tokens(order, place, tokens)
    near = lines(piece, PAIRS)
    mid = lines(piece, MIDDLE)
    own, taps, first_out, inner_out, middle_out = gate(
        order, place, tokens, in_weight, kernel, out_grad
    )
    own_y = flipped(inner_out, "rep", 1)
    inner = lines(inner_out, INWARD)
    first = lines(first_out, PAIRS)
    middle = lines(middle_out, MIDDLE)
    taps1 = flipped(taps, "rep", 1)
    near = order.wait(near)
    far = lines(near, MIDDLE)
    over = column_blocks(order, place, [(piece, None), (near, None)], False)
    got1 = flipped(over, "rep", 1)
    mid = order.wait(mid)
    outer2 = lines(part_of(order, place, mid, BLOCKS - OWN, OWN), OUTWARD)
    send = token_part(order, jnp.stack(quarters[:2]), own, in_weight)
    summed = flipped(send, "shard", 1)
    inner, own_y, far = order.wait(inner, own_y, far)
    keep = token_part(order, jnp.stack(quarters[2:]), own, in_weight)
    outer3 = lines(part_of(order, place, far, BLOCKS - OWN, OWN), OUTWARD)
    outer2 = order.wait(outer2)
    over = column_blocks(order, place, [(mid, outer2)], False)
    got2 = flipped(over, "rep", 1)
    first = order.wait(first)
    relay, side1 = relay_payload(order, place, first, inner)
    relayed = lines(relay, MIDDLE)
    side1 = flipped(side1, "rep", 1)
    middle, got1 = order.wait(middle, got1)
    own1 = column_blocks(order, place, [(near, None)], True, got1, (0, OWN))
    across1 = flipped(own1, "shard", 2)
    beside1 = flipped(own1, "shard", 1)
    beside1, outer3, side1 = order.wait(beside1, outer3, side1)
    middle_end = lines(part_of(order, place, middle, 1, 1), OUTWARD)
    summed, got2 = order.wait(summed, got2)
    own2 = column_blocks(order, place, [(mid, outer2)], True, got2, (0, HALF))
    across2 = flipped(own2, "shard", 2)
    beside2 = flipped(own2, "shard", 1)
    over = column_blocks(order, place, [(far, outer3)], False)
    got3 = flipped(over, "rep", 1)
    middle_end = order.wait(middle_end)
    side2 = flipped(side_payload(order, place, middle, middle_end), "rep", 1)
    across1 = order.wait(across1)
    both1 = flipped(across1, "shard", 1)
    token_grad, away = add(order, keep, summed)
    last = flipped(away, "shard", 2)
    relayed = order.wait(relayed)
    relayed_end = lines(part_of(order, place, relayed, 1, 1), OUTWARD)
    beside2, taps1 = order.wait(beside2, taps1)
    taps, taps_out = add(order, taps, taps1)
    taps2 = flipped(taps_out, "rep", 2)
    across2, relayed_end, got3 = order.wait(across2, relayed_end, got3)
    both2 = flipped(across2, "shard", 1)
    own3 = column_blocks(order, place, [(far, outer3)], True, got3, (0, HALF))
    across3 = flipped(own3, "shard", 2)
    beside3 = flipped(own3, "shard", 1)
    both1 = order.wait(both1)
    tok = arrange_tokens(order, place, tokens, [(own1, beside1, across1, both1)])
    both2 = order.wait(both2)
    early = [(own, None), (inner, first), (own_y, None), (side1, None)]
    so_far = weight_part(order, place, tok, early)
    side3 = flipped(side_payload(order, place, relayed, relayed_end), "rep", 1)
    side2, across3 = order.wait(side2, across3)
    both3 = flipped(across3, "shard", 1)
    both3 = order.wait(both3)
    tok = arrange_tokens(order, place, None, [(own2, beside2, across2, both2)])
    so_far = weight_part(order, place, tok, [(middle, middle_end), (side2, None)], None, so_far)
    taps2 = order.wait(taps2)
    taps, taps_out = add(order, taps, taps2)
    taps4 = flipped(taps_out, "rep", 4)
    taps4, beside3, last = order.wait(taps4, beside3, last)
    token_grad = (token_grad + last).astype(jnp.bfloat16)
    tok = arrange_tokens(order, place, None, [(own3, beside3, across3, both3)])
    side3 = order.wait(side3)
    late = [(relayed, relayed_end), (side3, None)]
    weight_grad = weight_part(order, place, tok, late, scale, so_far)
    taps, _ = add(order, taps, taps4, scale=scale)
    return (token_grad, weight_grad, taps)


def solution(mesh):
    placed = (P("rep", None), P(None, None, "shard"), P(None, None, "shard"), P("rep", "shard"))
    line = mesh.shape["rep"] == 2 * LEVELS and mesh.shape["shard"] == 4
    return jax.shard_map(
        lined if line else plain,
        mesh=mesh,
        in_specs=placed,
        out_specs=(P("rep", "shard"), P("rep", "shard"), P(None, None, "shard")),
        check_vma=False,
    )
```

```python
import functools
import math

import jax
import jax.numpy as jnp
from jax import lax
from jax.experimental import pallas as pl
from jax.experimental.pallas import tpu as pltpu
from jax.sharding import PartitionSpec as P

SEQ = 128


def causal_mix(values, kernel):
    width = kernel.shape[0]
    length = values.shape[1]
    padded = jnp.pad(values, ((0, 0), (width - 1, 0), (0, 0), (0, 0)))
    total = jnp.zeros_like(values)
    for offset in range(width):
        total = total + kernel[offset] * padded[:, width - 1 - offset : width - 1 - offset + length]
    return total


def causal_mix_back(grads, kernel):
    width = kernel.shape[0]
    length = grads.shape[1]
    padded = jnp.pad(grads, ((0, 0), (0, width - 1), (0, 0), (0, 0)))
    total = jnp.zeros_like(grads)
    for offset in range(width):
        total = total + kernel[offset] * padded[:, offset : offset + length]
    return total


def kernel_terms(values, grads, width):
    length = values.shape[1]
    padded = jnp.pad(values, ((0, 0), (width - 1, 0), (0, 0), (0, 0)))
    terms = []
    for offset in range(width):
        shifted = padded[:, width - 1 - offset : width - 1 - offset + length]
        terms.append(jnp.sum(shifted * grads, axis=(0, 1)))
    return jnp.stack(terms, axis=0)


def gated_grads(tokens, in_weight, kernel, out_grad):
    rows = tokens.shape[0]
    chans = in_weight.shape[2]
    mixed = jnp.einsum("td,sdc->tsc", tokens, in_weight, preferred_element_type=jnp.float32)
    stored = lax.optimization_barrier(mixed.astype(jnp.bfloat16))
    values = stored.astype(jnp.float32).reshape(rows // SEQ, SEQ, 3, chans)
    conv = causal_mix(values, kernel)
    query = conv[:, :, 0]
    keyed = conv[:, :, 1]
    valued = conv[:, :, 2]
    upstream = out_grad.astype(jnp.float32).reshape(rows // SEQ, SEQ, chans)
    conv_grad = jnp.stack(
        [upstream * keyed * valued, upstream * query * valued, upstream * query * keyed], axis=2
    )
    mixed_grad = causal_mix_back(conv_grad, kernel).reshape(rows, 3, chans)
    return mixed_grad, kernel_terms(values, conv_grad, kernel.shape[0])


def plain(tokens, in_weight, kernel, out_grad):
    features = tokens.shape[1]
    chans = in_weight.shape[2]
    scale = 1.0 / math.sqrt(tokens.shape[0] * lax.axis_size("rep"))
    wide_grad, taps = gated_grads(tokens, in_weight, kernel, out_grad)
    mixed_grad = wide_grad.astype(jnp.bfloat16)
    partial_grad = jnp.einsum(
        "tsc,sdc->td", mixed_grad, in_weight, preferred_element_type=jnp.float32
    )
    token_grad = lax.psum_scatter(partial_grad, "shard", scatter_dimension=1, tiled=True).astype(
        jnp.bfloat16
    )
    local_grad = (
        jnp.einsum("td,tsc->sdc", tokens, mixed_grad, preferred_element_type=jnp.float32) * scale
    )
    weight_grad = lax.psum_scatter(
        local_grad.reshape(3 * features, chans), "rep", scatter_dimension=0, tiled=True
    )
    kernel_grad = lax.psum(taps * scale, "rep")
    return (token_grad, weight_grad, kernel_grad)


LEVELS = 4
BLOCK = 512
BLOCKS = 8
OWN = 6
HALF = 3
LANES = 128
VMEM = pl.BlockSpec(memory_space=pltpu.VMEM)
SMEM = pl.BlockSpec(memory_space=pltpu.SMEM)
ANY = pl.BlockSpec(memory_space=pl.ANY)
NOTHING = pl.CostEstimate(flops=128, bytes_accessed=128, transcendentals=0)
PAIRS = ((0, 1), (1, 0), (2, 3), (3, 2))
INWARD = ((0, 1), (3, 2))
MIDDLE = ((1, 2), (2, 1))
OUTWARD = ((1, 0), (2, 3))


class Order:
    def __init__(self):
        self.after = []

    def call(self, body, arrays, in_specs, *, out_shape, out_specs, scalars=(), grid=(), scratch_shapes=(), name, vmem=10):
        held, count = len(scalars), len(arrays)
        after = [a for a in self.after if not any(a is b for b in arrays)]

        def short(*refs):
            body(*refs[: held + count], *refs[held + count + len(after) :])

        result = pl.pallas_call(
            short,
            out_shape=out_shape,
            grid_spec=pltpu.PrefetchScalarGridSpec(
                num_scalar_prefetch=held,
                grid=grid,
                in_specs=list(in_specs) + [ANY] * len(after),
                out_specs=out_specs,
                scratch_shapes=scratch_shapes,
            ),
            compiler_params=pltpu.CompilerParams(vmem_limit_bytes=vmem * 2**20),
            cost_estimate=NOTHING,
            name=name,
        )(*scalars, *arrays, *after)
        self.after = [result[0] if isinstance(result, (list, tuple)) else result]
        return result

    def wait(self, *arrays):
        self.after.extend(arrays)
        return arrays[0] if len(arrays) == 1 else arrays


def lines(array, hops):
    perm = [(2 * a + y, 2 * b + y) for a, b in hops for y in range(2)]
    return lax.ppermute(array, "rep", perm)


def flipped(array, axis, flip):
    return lax.ppermute(array, axis, [(r, r ^ flip) for r in range(lax.axis_size(axis))])


def device_block(level, column, i):
    return lax.rem(OWN * level + HALF * column + i, BLOCKS)


def turn_tokens(order, place, tokens):
    rows = tokens.shape[0]
    slab = BLOCK // 4

    def body(place, tokens, piece):
        start = pl.multiple_of(place[2] * slab, slab)
        for b in range(BLOCKS):
            piece[b] = tokens[:, pl.ds(pl.multiple_of(BLOCK * b + start, slab), slab)].astype(
                jnp.float32
            ).T

    return order.call(
        body,
        (place, tokens),
        [SMEM, VMEM],
        out_shape=jax.ShapeDtypeStruct((BLOCKS, slab, rows), jnp.float32),
        out_specs=VMEM,
        name="turn_tokens",
    )


def column_blocks(order, place, slots, own, got=None, part=(0, 0)):
    arrays = [a for slot in slots for a in slot if a is not None]
    begin, extra = part
    first = slots[0][0]
    count = HALF * len(slots)

    def body(place, *refs):
        out = refs[-1]
        left = list(refs)
        column = place[1] if own else 1 - place[1]
        inside = jnp.logical_or(place[0] == 1, place[0] == 2)
        for n, (_, ends) in enumerate(slots):
            inner = left.pop(0)
            end = None if ends is None else left.pop(0)
            for i in range(HALF):
                block = device_block(place[0], column, i)
                if end is None:
                    out[HALF * n + i] = inner[block]
                    continue

                @pl.when(inside)
                def _():
                    out[HALF * n + i] = inner[block]

                @pl.when(jnp.logical_not(inside))
                def _():
                    out[HALF * n + i] = end[HALF * column + i]

        for i in range(extra):
            out[count + i] = left[0][begin + i]

    return order.call(
        body,
        [place] + arrays + ([] if got is None else [got]),
        [SMEM] + [VMEM] * (len(arrays) + (extra > 0)),
        out_shape=jax.ShapeDtypeStruct((count + extra,) + first.shape[1:], first.dtype),
        out_specs=VMEM,
        name="own_blocks" if own else "other_blocks",
    )


def gate(order, place, tokens, in_weight, kernel, out_grad):
    rows, features = tokens.shape
    chans = in_weight.shape[2]
    taps = kernel.shape[0]
    steps = 4
    width = min(chans, 2 * LANES)
    deep = features // steps
    pad = 8

    def body(place, tokens, weight, kernel, out_grad, own, grad, first, inner, middle, total, held, pads, back):
        step = pl.program_id(1)
        for s in range(3):
            now = jnp.dot(tokens[...], weight[s], preferred_element_type=jnp.float32)

            @pl.when(step == 0)
            def _():
                total[s] = now

            @pl.when(step > 0)
            def _():
                total[s] += now

        @pl.when(step == steps - 1)
        def _():
            blank = jnp.zeros((pad, LANES), jnp.float32)
            for lane in range(0, width, LANES):
                lanes = slice(lane, lane + LANES)
                sums = [[None] * taps for _ in range(3)]
                for q in range(rows // SEQ):
                    here = slice(q * SEQ, (q + 1) * SEQ)
                    conv = []
                    for s in range(3):
                        values = total[s, here, lanes].astype(jnp.bfloat16).astype(jnp.float32)
                        pads[s, 0:pad, :] = blank
                        pads[s, pad : pad + SEQ, :] = values
                        mix = kernel[0, s : s + 1, lanes] * values
                        for j in range(1, taps):
                            mix += kernel[j, s : s + 1, lanes] * pads[s, pad - j : pad - j + SEQ, :]
                        conv.append(mix)
                    up = out_grad[here, lanes].astype(jnp.float32)
                    query, keyed, valued = conv
                    grads = (up * keyed * valued, up * query * valued, up * query * keyed)
                    for s in range(3):
                        back[s, 0:SEQ, :] = grads[s]
                        back[s, SEQ : SEQ + pad, :] = blank
                    for s in range(3):
                        values = pads[s, pad : pad + SEQ, :]
                        mixed = None
                        for j in range(taps):
                            moved = back[s, j : j + SEQ, :]
                            term = kernel[j, s : s + 1, lanes] * moved
                            mixed = term if mixed is None else mixed + term
                            folded = jnp.sum((values * moved).reshape(SEQ // 8, 8, LANES), axis=0)
                            sums[s][j] = folded if q == 0 else sums[s][j] + folded
                        held[s, here, lanes] = mixed
                for s in range(3):
                    for j in range(taps):
                        grad[j, s : s + 1, lanes] = jnp.sum(sums[s][j], axis=0, keepdims=True)
            for s in range(3):
                own[s] = held[s].astype(jnp.bfloat16)
            level = place[0]
            first[0] = held[2 - 2 * lax.rem(level, 2)]
            low = jnp.where(level <= 1, 0, 1)
            for i in range(2):
                inner[i] = held[low + i]
                middle[i] = held[1 - low + i]

    one = jax.ShapeDtypeStruct((1, rows, chans), jnp.float32)
    two = jax.ShapeDtypeStruct((2, rows, chans), jnp.float32)
    return order.call(
        body,
        (place, tokens, in_weight, kernel, out_grad),
        [
            SMEM,
            pl.BlockSpec((rows, deep), lambda c, k: (0, k)),
            pl.BlockSpec((3, deep, width), lambda c, k: (0, k, c)),
            pl.BlockSpec((taps, 3, width), lambda c, k: (0, 0, c)),
            pl.BlockSpec((rows, width), lambda c, k: (0, c)),
        ],
        out_shape=(
            jax.ShapeDtypeStruct((3, rows, chans), jnp.bfloat16),
            jax.ShapeDtypeStruct((taps, 3, chans), jnp.float32),
            one,
            two,
            two,
        ),
        grid=(chans // width, steps),
        out_specs=(
            pl.BlockSpec((3, rows, width), lambda c, k: (0, 0, c)),
            pl.BlockSpec((taps, 3, width), lambda c, k: (0, 0, c)),
            pl.BlockSpec((1, rows, width), lambda c, k: (0, 0, c)),
            pl.BlockSpec((2, rows, width), lambda c, k: (0, 0, c)),
            pl.BlockSpec((2, rows, width), lambda c, k: (0, 0, c)),
        ),
        scratch_shapes=[
            pltpu.VMEM((3, rows, width), jnp.float32),
            pltpu.VMEM((3, rows, width), jnp.float32),
            pltpu.VMEM((3, pad + SEQ, LANES), jnp.float32),
            pltpu.VMEM((3, SEQ + pad, LANES), jnp.float32),
        ],
        name="gate",
        vmem=24,
    )


def relay_payload(order, place, first, inner):
    def body(place, first, inner, out, side):
        @pl.when(place[0] <= 1)
        def _():
            out[0] = inner[1]
            out[1] = first[0]

        @pl.when(place[0] > 1)
        def _():
            out[0] = first[0]
            out[1] = inner[0]

        level_own(place, inner, first, side)

    two = jax.ShapeDtypeStruct(inner.shape, inner.dtype)
    return order.call(
        body,
        (place, first, inner),
        [SMEM, VMEM, VMEM],
        out_shape=(two, two),
        out_specs=(VMEM, VMEM),
        name="relay_payload",
    )


def level_own(place, inner, ends, out):
    inside = jnp.logical_or(place[0] == 1, place[0] == 2)

    @pl.when(inside)
    def _():
        out[...] = inner[...]

    @pl.when(jnp.logical_not(inside))
    def _():
        out[jnp.where(place[0] == 0, 0, 1)] = ends[0]
        out[jnp.where(place[0] == 0, 1, 0)] = ends[0]


def side_payload(order, place, inner, ends):
    return order.call(
        level_own,
        (place, inner, ends),
        [SMEM, VMEM, VMEM],
        out_shape=jax.ShapeDtypeStruct(inner.shape, inner.dtype),
        out_specs=VMEM,
        name="side_payload",
    )


def part_of(order, place, array, step, count):
    def body(place, array, out):
        start = jnp.where(place[0] <= 1, 0, step)
        for i in range(count):
            out[i] = array[start + i]

    return order.call(
        body,
        (place, array),
        [SMEM, VMEM],
        out_shape=jax.ShapeDtypeStruct((count,) + array.shape[1:], array.dtype),
        out_specs=VMEM,
        name="part_of",
    )


def add(order, mine, other, scale=1.0):
    pair = mine.ndim == 3 and mine.shape[0] == 2

    def body(mine, other, out, again):
        if pair:
            out[...] = mine[1] + other[1]
            again[...] = mine[0] + other[0]
        else:
            total = (mine[...] + other[...]) * scale
            out[...] = total
            again[...] = total

    shape = jax.ShapeDtypeStruct(mine.shape[1:] if pair else mine.shape, mine.dtype)
    return order.call(
        body,
        (mine, other),
        [VMEM] * 2,
        out_shape=(shape, shape),
        out_specs=(VMEM,) * 2,
        name="add",
    )


def add_rounded(order, mine, other):
    def body(mine, other, out):
        out[...] = (mine[...] + other[...]).astype(jnp.bfloat16)

    return order.call(
        body,
        (mine, other),
        [VMEM] * 2,
        out_shape=jax.ShapeDtypeStruct(mine.shape, jnp.bfloat16),
        out_specs=VMEM,
        name="add_rounded",
    )


def arrange_tokens(order, place, own, slots):
    slab = BLOCK // 4
    rows = slots[0][0].shape[2]
    counts = [slot[0].shape[0] // HALF for slot in slots]
    total = (0 if own is None else 1) + sum(counts)

    def body(place, *refs):
        out = refs[-1]
        at = 0
        if own is not None:
            for i in range(HALF):
                block = device_block(place[0], place[1], i)
                columns = pl.ds(pl.multiple_of(block * BLOCK, BLOCK), BLOCK)
                out[i, :, 0:rows] = refs[0][:, columns].T
            refs = refs[1:]
            at = 1
        for n, count in enumerate(counts):
            for c in range(count):
                for i in range(HALF):
                    for k in range(4):
                        where = pl.multiple_of(jnp.bitwise_xor(place[2], k) * slab, slab)
                        out[i, pl.ds(where, slab), (at + c) * rows : (at + c + 1) * rows] = refs[
                            4 * n + k
                        ][HALF * c + i].astype(jnp.bfloat16)
            at += count

    arrays = [place] + ([] if own is None else [own]) + [piece for slot in slots for piece in slot]
    return order.call(
        body,
        arrays,
        [SMEM] + [VMEM] * (len(arrays) - 1),
        out_shape=jax.ShapeDtypeStruct((HALF, BLOCK, total * rows), jnp.bfloat16),
        out_specs=VMEM,
        name="arrange_tokens",
        vmem=20,
    )


def weight_part(order, place, tok, slots, scale=None, so_far=None):
    rows, chans = slots[0][0].shape[1:]
    count = len(slots)
    arrays = [a for slot in slots for a in slot if a is not None]

    def body(place, tok, *refs):
        out, held = refs[-2], refs[-1]
        level, column = place[0], place[1]
        i = pl.program_id(0)
        inside = jnp.logical_or(level == 1, level == 2)
        high = jnp.where(level <= 1, 0, 1)

        @pl.when(i == 0)
        def _():
            left = list(refs)
            for at, (streams, ends) in enumerate(slots):
                here = slice(at * rows, (at + 1) * rows)
                ref = left.pop(0)
                if streams.shape[0] == 3:
                    major = jnp.where(inside, level - 1 + column, 2 * high)
                    minor = 1
                else:
                    major = jnp.where(inside, column, high)
                    minor = 1 - high
                if ends is None:
                    held[0, here, :] = ref[major].astype(jnp.bfloat16)
                else:
                    end = left.pop(0)

                    @pl.when(inside)
                    def _():
                        held[0, here, :] = ref[major].astype(jnp.bfloat16)

                    @pl.when(jnp.logical_not(inside))
                    def _():
                        held[0, here, :] = end[0].astype(jnp.bfloat16)

                held[1, here, :] = ref[minor].astype(jnp.bfloat16)

        second = jnp.logical_or(
            jnp.logical_and(jnp.logical_and(level == 1, column == 0), i == 2),
            jnp.logical_and(jnp.logical_and(level == 2, column == 1), i == 0),
        )
        got = jnp.dot(
            tok[...], held[second.astype(jnp.int32)], preferred_element_type=jnp.float32
        )
        if so_far is not None:
            got = got + refs[-3][...]
        out[...] = got if scale is None else got * scale

    whole = lambda a: pl.BlockSpec(a.shape, lambda i: (0,) * a.ndim)
    more = [] if so_far is None else [so_far]
    part = pl.BlockSpec((BLOCK, chans), lambda i: (i, 0))
    return order.call(
        body,
        [place, tok] + arrays + more,
        [SMEM, pl.BlockSpec((None, BLOCK, count * rows), lambda i: (i, 0, 0))]
        + [whole(a) for a in arrays]
        + [part] * len(more),
        out_shape=jax.ShapeDtypeStruct((HALF * BLOCK, chans), jnp.float32),
        grid=(HALF,),
        out_specs=part,
        scratch_shapes=[pltpu.VMEM((2, count * rows, chans), jnp.bfloat16)],
        name="weight_part",
        vmem=56,
    )


def token_part(order, quarters, grads, weight):
    rows, chans = grads.shape[1:]
    wide = weight.shape[1] // 4
    count = quarters.shape[0]

    def body(quarters, grads, weight, out):
        now = lax.dot_general(
            grads[...], weight[...], (((1,), (1,)), ((), ())), preferred_element_type=jnp.float32
        )

        @pl.when(pl.program_id(1) == 0)
        def _():
            out[...] = now

        @pl.when(pl.program_id(1) > 0)
        def _():
            out[...] += now

    return order.call(
        body,
        (grads, weight),
        [
            pl.BlockSpec((None, rows, chans), lambda i, s, quarters: (s, 0, 0)),
            pl.BlockSpec((None, wide, chans), lambda i, s, quarters: (s, quarters[i], 0)),
        ],
        scalars=(quarters,),
        out_shape=jax.ShapeDtypeStruct((count, rows, wide), jnp.float32),
        grid=(count, 3),
        out_specs=pl.BlockSpec((None, rows, wide), lambda i, s, quarters: (i, 0, 0)),
        name="token_part",
        vmem=12,
    )


def lined(tokens, in_weight, kernel, out_grad):
    rows = tokens.shape[0]
    rep, quarter = lax.axis_index("rep"), lax.axis_index("shard")
    level, column = rep // 2, rep % 2
    place = jnp.stack([level, column, quarter]).astype(jnp.int32)
    scale = 1.0 / math.sqrt(rows * lax.axis_size("rep"))
    order = Order()
    quarters = [jnp.bitwise_xor(quarter, k).astype(jnp.int32) for k in (3, 1, 2, 0)]
    piece = turn_tokens(order, place, tokens)
    near = lines(piece, PAIRS)
    mid = lines(piece, MIDDLE)
    own, taps, first_out, inner_out, middle_out = gate(
        order, place, tokens, in_weight, kernel, out_grad
    )
    own_y = flipped(inner_out, "rep", 1)
    inner = lines(inner_out, INWARD)
    first = lines(first_out, PAIRS)
    middle = lines(middle_out, MIDDLE)
    taps1 = flipped(taps, "rep", 1)
    near = order.wait(near)
    far = lines(near, MIDDLE)
    over = column_blocks(order, place, [(piece, None), (near, None)], False)
    got1 = flipped(over, "rep", 1)
    mid = order.wait(mid)
    outer2 = lines(part_of(order, place, mid, BLOCKS - OWN, OWN), OUTWARD)
    send = token_part(order, jnp.stack(quarters[:2]), own, in_weight)
    summed = flipped(send, "shard", 1)
    inner, own_y, far = order.wait(inner, own_y, far)
    keep = token_part(order, jnp.stack(quarters[2:]), own, in_weight)
    outer3 = lines(part_of(order, place, far, BLOCKS - OWN, OWN), OUTWARD)
    outer2 = order.wait(outer2)
    over = column_blocks(order, place, [(mid, outer2)], False)
    got2 = flipped(over, "rep", 1)
    first = order.wait(first)
    relay, side1 = relay_payload(order, place, first, inner)
    relayed = lines(relay, MIDDLE)
    side1 = flipped(side1, "rep", 1)
    middle, got1 = order.wait(middle, got1)
    own1 = column_blocks(order, place, [(near, None)], True, got1, (0, OWN))
    across1 = flipped(own1, "shard", 2)
    beside1 = flipped(own1, "shard", 1)
    beside1, outer3, side1 = order.wait(beside1, outer3, side1)
    middle_end = lines(part_of(order, place, middle, 1, 1), OUTWARD)
    summed, got2 = order.wait(summed, got2)
    own2 = column_blocks(order, place, [(mid, outer2)], True, got2, (0, HALF))
    across2 = flipped(own2, "shard", 2)
    beside2 = flipped(own2, "shard", 1)
    relayed = order.wait(relayed)
    relayed_end = lines(part_of(order, place, relayed, 1, 1), OUTWARD)
    over = column_blocks(order, place, [(far, outer3)], False)
    got3 = flipped(over, "rep", 1)
    middle_end = order.wait(middle_end)
    side2 = flipped(side_payload(order, place, middle, middle_end), "rep", 1)
    across1 = order.wait(across1)
    both1 = flipped(across1, "shard", 1)
    token_grad, away = add(order, keep, summed)
    last = flipped(away, "shard", 2)
    beside2, across2, taps1 = order.wait(beside2, across2, taps1)
    both2 = flipped(across2, "shard", 1)
    taps, taps_out = add(order, taps, taps1)
    taps2 = flipped(taps_out, "rep", 2)
    relayed_end, got3 = order.wait(relayed_end, got3)
    own3 = column_blocks(order, place, [(far, outer3)], True, got3, (0, HALF))
    across3 = flipped(own3, "shard", 2)
    beside3 = flipped(own3, "shard", 1)
    both1 = order.wait(both1)
    side3 = flipped(side_payload(order, place, relayed, relayed_end), "rep", 1)
    side2, across3 = order.wait(side2, across3)
    both3 = flipped(across3, "shard", 1)
    both3, both2, taps2 = order.wait(both3, both2, taps2)
    taps, taps_out = add(order, taps, taps2)
    taps4 = flipped(taps_out, "rep", 4)
    beside3 = order.wait(beside3)
    tok3 = arrange_tokens(order, place, None, [(own3, beside3, across3, both3)])
    tok = arrange_tokens(
        order,
        place,
        tokens,
        [(own1, beside1, across1, both1), (own2, beside2, across2, both2)],
    )
    taps4 = order.wait(taps4)
    early = [(own, None), (inner, first), (own_y, None), (side1, None)]
    early += [(middle, middle_end), (side2, None)]
    so_far = weight_part(order, place, tok, early)
    last = order.wait(last)
    token_grad = add_rounded(order, token_grad, last)
    taps, _ = add(order, taps, taps4, scale=scale)
    side3 = order.wait(side3)
    late = [(relayed, relayed_end), (side3, None)]
    weight_grad = weight_part(order, place, tok3, late, scale, so_far)
    return (token_grad, weight_grad, taps)


def solution(mesh):
    placed = (P("rep", None), P(None, None, "shard"), P(None, None, "shard"), P("rep", "shard"))
    line = mesh.shape["rep"] == 2 * LEVELS and mesh.shape["shard"] == 4
    return jax.shard_map(
        lined if line else plain,
        mesh=mesh,
        in_specs=placed,
        out_specs=(P("rep", "shard"), P("rep", "shard"), P(None, None, "shard")),
        check_vma=False,
    )
```

```python
import functools
import math

import jax
import jax.numpy as jnp
from jax import lax
from jax.experimental import pallas as pl
from jax.experimental.pallas import tpu as pltpu
from jax.sharding import PartitionSpec as P

SEQ = 128


def causal_mix(values, kernel):
    width = kernel.shape[0]
    length = values.shape[1]
    padded = jnp.pad(values, ((0, 0), (width - 1, 0), (0, 0), (0, 0)))
    total = jnp.zeros_like(values)
    for offset in range(width):
        total = total + kernel[offset] * padded[:, width - 1 - offset : width - 1 - offset + length]
    return total


def causal_mix_back(grads, kernel):
    width = kernel.shape[0]
    length = grads.shape[1]
    padded = jnp.pad(grads, ((0, 0), (0, width - 1), (0, 0), (0, 0)))
    total = jnp.zeros_like(grads)
    for offset in range(width):
        total = total + kernel[offset] * padded[:, offset : offset + length]
    return total


def kernel_terms(values, grads, width):
    length = values.shape[1]
    padded = jnp.pad(values, ((0, 0), (width - 1, 0), (0, 0), (0, 0)))
    terms = []
    for offset in range(width):
        shifted = padded[:, width - 1 - offset : width - 1 - offset + length]
        terms.append(jnp.sum(shifted * grads, axis=(0, 1)))
    return jnp.stack(terms, axis=0)


def gated_grads(tokens, in_weight, kernel, out_grad):
    rows = tokens.shape[0]
    chans = in_weight.shape[2]
    mixed = jnp.einsum("td,sdc->tsc", tokens, in_weight, preferred_element_type=jnp.float32)
    stored = lax.optimization_barrier(mixed.astype(jnp.bfloat16))
    values = stored.astype(jnp.float32).reshape(rows // SEQ, SEQ, 3, chans)
    conv = causal_mix(values, kernel)
    query = conv[:, :, 0]
    keyed = conv[:, :, 1]
    valued = conv[:, :, 2]
    upstream = out_grad.astype(jnp.float32).reshape(rows // SEQ, SEQ, chans)
    conv_grad = jnp.stack(
        [upstream * keyed * valued, upstream * query * valued, upstream * query * keyed], axis=2
    )
    mixed_grad = causal_mix_back(conv_grad, kernel).reshape(rows, 3, chans)
    return mixed_grad, kernel_terms(values, conv_grad, kernel.shape[0])


def plain(tokens, in_weight, kernel, out_grad):
    features = tokens.shape[1]
    chans = in_weight.shape[2]
    scale = 1.0 / math.sqrt(tokens.shape[0] * lax.axis_size("rep"))
    wide_grad, taps = gated_grads(tokens, in_weight, kernel, out_grad)
    mixed_grad = wide_grad.astype(jnp.bfloat16)
    partial_grad = jnp.einsum(
        "tsc,sdc->td", mixed_grad, in_weight, preferred_element_type=jnp.float32
    )
    token_grad = lax.psum_scatter(partial_grad, "shard", scatter_dimension=1, tiled=True).astype(
        jnp.bfloat16
    )
    local_grad = (
        jnp.einsum("td,tsc->sdc", tokens, mixed_grad, preferred_element_type=jnp.float32) * scale
    )
    weight_grad = lax.psum_scatter(
        local_grad.reshape(3 * features, chans), "rep", scatter_dimension=0, tiled=True
    )
    kernel_grad = lax.psum(taps * scale, "rep")
    return (token_grad, weight_grad, kernel_grad)


LEVELS = 4
BLOCK = 512
BLOCKS = 8
OWN = 6
HALF = 3
LANES = 128
VMEM = pl.BlockSpec(memory_space=pltpu.VMEM)
SMEM = pl.BlockSpec(memory_space=pltpu.SMEM)
ANY = pl.BlockSpec(memory_space=pl.ANY)
NOTHING = pl.CostEstimate(flops=128, bytes_accessed=128, transcendentals=0)
PAIRS = ((0, 1), (1, 0), (2, 3), (3, 2))
INWARD = ((0, 1), (3, 2))
MIDDLE = ((1, 2), (2, 1))
OUTWARD = ((1, 0), (2, 3))


class Order:
    def __init__(self):
        self.after = []

    def call(self, body, arrays, in_specs, *, out_shape, out_specs, scalars=(), grid=(), scratch_shapes=(), name, vmem=10):
        held, count = len(scalars), len(arrays)
        after = [a for a in self.after if not any(a is b for b in arrays)]

        def short(*refs):
            body(*refs[: held + count], *refs[held + count + len(after) :])

        result = pl.pallas_call(
            short,
            out_shape=out_shape,
            grid_spec=pltpu.PrefetchScalarGridSpec(
                num_scalar_prefetch=held,
                grid=grid,
                in_specs=list(in_specs) + [ANY] * len(after),
                out_specs=out_specs,
                scratch_shapes=scratch_shapes,
            ),
            compiler_params=pltpu.CompilerParams(vmem_limit_bytes=vmem * 2**20),
            cost_estimate=NOTHING,
            name=name,
        )(*scalars, *arrays, *after)
        self.after = [result[0] if isinstance(result, (list, tuple)) else result]
        return result

    def wait(self, *arrays):
        self.after.extend(arrays)
        return arrays[0] if len(arrays) == 1 else arrays


def lines(array, hops):
    perm = [(2 * a + y, 2 * b + y) for a, b in hops for y in range(2)]
    return lax.ppermute(array, "rep", perm)


def flipped(array, axis, flip):
    return lax.ppermute(array, axis, [(r, r ^ flip) for r in range(lax.axis_size(axis))])


def device_block(level, column, i):
    return lax.rem(OWN * level + HALF * column + i, BLOCKS)


def turn_tokens(order, place, tokens):
    rows = tokens.shape[0]
    slab = BLOCK // 4

    def body(place, tokens, piece):
        start = pl.multiple_of(place[2] * slab, slab)
        for b in range(BLOCKS):
            piece[b] = tokens[:, pl.ds(pl.multiple_of(BLOCK * b + start, slab), slab)].astype(
                jnp.float32
            ).T

    return order.call(
        body,
        (place, tokens),
        [SMEM, VMEM],
        out_shape=jax.ShapeDtypeStruct((BLOCKS, slab, rows), jnp.float32),
        out_specs=VMEM,
        name="turn_tokens",
    )


def column_blocks(order, place, slots, own, got=None, part=(0, 0)):
    arrays = [a for slot in slots for a in slot if a is not None]
    begin, extra = part
    first = slots[0][0]
    count = HALF * len(slots)

    def body(place, *refs):
        out = refs[-1]
        left = list(refs)
        column = place[1] if own else 1 - place[1]
        inside = jnp.logical_or(place[0] == 1, place[0] == 2)
        for n, (_, ends) in enumerate(slots):
            inner = left.pop(0)
            end = None if ends is None else left.pop(0)
            for i in range(HALF):
                block = device_block(place[0], column, i)
                if end is None:
                    out[HALF * n + i] = inner[block]
                    continue

                @pl.when(inside)
                def _():
                    out[HALF * n + i] = inner[block]

                @pl.when(jnp.logical_not(inside))
                def _():
                    out[HALF * n + i] = end[HALF * column + i]

        for i in range(extra):
            out[count + i] = left[0][begin + i]

    return order.call(
        body,
        [place] + arrays + ([] if got is None else [got]),
        [SMEM] + [VMEM] * (len(arrays) + (extra > 0)),
        out_shape=jax.ShapeDtypeStruct((count + extra,) + first.shape[1:], first.dtype),
        out_specs=VMEM,
        name="own_blocks" if own else "other_blocks",
    )


def gate(order, place, tokens, in_weight, kernel, out_grad):
    rows, features = tokens.shape
    chans = in_weight.shape[2]
    taps = kernel.shape[0]
    steps = 4
    width = min(chans, 2 * LANES)
    deep = features // steps
    pad = 8

    def body(place, tokens, weight, kernel, out_grad, own, grad, first, inner, middle, total, held, pads, back):
        step = pl.program_id(1)
        for s in range(3):
            now = jnp.dot(tokens[...], weight[s], preferred_element_type=jnp.float32)

            @pl.when(step == 0)
            def _():
                total[s] = now

            @pl.when(step > 0)
            def _():
                total[s] += now

        @pl.when(step == steps - 1)
        def _():
            blank = jnp.zeros((pad, LANES), jnp.float32)
            for lane in range(0, width, LANES):
                lanes = slice(lane, lane + LANES)
                sums = [[None] * taps for _ in range(3)]
                for q in range(rows // SEQ):
                    here = slice(q * SEQ, (q + 1) * SEQ)
                    conv = []
                    for s in range(3):
                        values = total[s, here, lanes].astype(jnp.bfloat16).astype(jnp.float32)
                        pads[s, 0:pad, :] = blank
                        pads[s, pad : pad + SEQ, :] = values
                        mix = kernel[0, s : s + 1, lanes] * values
                        for j in range(1, taps):
                            mix += kernel[j, s : s + 1, lanes] * pads[s, pad - j : pad - j + SEQ, :]
                        conv.append(mix)
                    up = out_grad[here, lanes].astype(jnp.float32)
                    query, keyed, valued = conv
                    grads = (up * keyed * valued, up * query * valued, up * query * keyed)
                    for s in range(3):
                        back[s, 0:SEQ, :] = grads[s]
                        back[s, SEQ : SEQ + pad, :] = blank
                    for s in range(3):
                        values = pads[s, pad : pad + SEQ, :]
                        mixed = None
                        for j in range(taps):
                            moved = back[s, j : j + SEQ, :]
                            term = kernel[j, s : s + 1, lanes] * moved
                            mixed = term if mixed is None else mixed + term
                            folded = jnp.sum((values * moved).reshape(SEQ // 8, 8, LANES), axis=0)
                            sums[s][j] = folded if q == 0 else sums[s][j] + folded
                        held[s, here, lanes] = mixed
                for s in range(3):
                    for j in range(taps):
                        grad[j, s : s + 1, lanes] = jnp.sum(sums[s][j], axis=0, keepdims=True)
            for s in range(3):
                own[s] = held[s].astype(jnp.bfloat16)
            level = place[0]
            first[0] = held[2 - 2 * lax.rem(level, 2)]
            low = jnp.where(level <= 1, 0, 1)
            for i in range(2):
                inner[i] = held[low + i]
                middle[i] = held[1 - low + i]

    one = jax.ShapeDtypeStruct((1, rows, chans), jnp.float32)
    two = jax.ShapeDtypeStruct((2, rows, chans), jnp.float32)
    return order.call(
        body,
        (place, tokens, in_weight, kernel, out_grad),
        [
            SMEM,
            pl.BlockSpec((rows, deep), lambda c, k: (0, k)),
            pl.BlockSpec((3, deep, width), lambda c, k: (0, k, c)),
            pl.BlockSpec((taps, 3, width), lambda c, k: (0, 0, c)),
            pl.BlockSpec((rows, width), lambda c, k: (0, c)),
        ],
        out_shape=(
            jax.ShapeDtypeStruct((3, rows, chans), jnp.bfloat16),
            jax.ShapeDtypeStruct((taps, 3, chans), jnp.float32),
            one,
            two,
            two,
        ),
        grid=(chans // width, steps),
        out_specs=(
            pl.BlockSpec((3, rows, width), lambda c, k: (0, 0, c)),
            pl.BlockSpec((taps, 3, width), lambda c, k: (0, 0, c)),
            pl.BlockSpec((1, rows, width), lambda c, k: (0, 0, c)),
            pl.BlockSpec((2, rows, width), lambda c, k: (0, 0, c)),
            pl.BlockSpec((2, rows, width), lambda c, k: (0, 0, c)),
        ),
        scratch_shapes=[
            pltpu.VMEM((3, rows, width), jnp.float32),
            pltpu.VMEM((3, rows, width), jnp.float32),
            pltpu.VMEM((3, pad + SEQ, LANES), jnp.float32),
            pltpu.VMEM((3, SEQ + pad, LANES), jnp.float32),
        ],
        name="gate",
        vmem=50,
    )


def relay_payload(order, place, first, inner):
    def body(place, first, inner, out, side):
        @pl.when(place[0] <= 1)
        def _():
            out[0] = inner[1]
            out[1] = first[0]

        @pl.when(place[0] > 1)
        def _():
            out[0] = first[0]
            out[1] = inner[0]

        level_own(place, inner, first, side)

    two = jax.ShapeDtypeStruct(inner.shape, inner.dtype)
    return order.call(
        body,
        (place, first, inner),
        [SMEM, VMEM, VMEM],
        out_shape=(two, two),
        out_specs=(VMEM, VMEM),
        name="relay_payload",
    )


def level_own(place, inner, ends, out):
    inside = jnp.logical_or(place[0] == 1, place[0] == 2)

    @pl.when(inside)
    def _():
        out[...] = inner[...]

    @pl.when(jnp.logical_not(inside))
    def _():
        out[jnp.where(place[0] == 0, 0, 1)] = ends[0]
        out[jnp.where(place[0] == 0, 1, 0)] = ends[0]


def side_payload(order, place, inner, ends):
    return order.call(
        level_own,
        (place, inner, ends),
        [SMEM, VMEM, VMEM],
        out_shape=jax.ShapeDtypeStruct(inner.shape, inner.dtype),
        out_specs=VMEM,
        name="side_payload",
    )


def part_of(order, place, array, step, count):
    def body(place, array, out):
        start = jnp.where(place[0] <= 1, 0, step)
        for i in range(count):
            out[i] = array[start + i]

    return order.call(
        body,
        (place, array),
        [SMEM, VMEM],
        out_shape=jax.ShapeDtypeStruct((count,) + array.shape[1:], array.dtype),
        out_specs=VMEM,
        name="part_of",
    )


def add(order, mine, other, scale=1.0):
    pair = mine.ndim == 3 and mine.shape[0] == 2

    def body(mine, other, out, again):
        if pair:
            out[...] = mine[1] + other[1]
            again[...] = mine[0] + other[0]
        else:
            total = (mine[...] + other[...]) * scale
            out[...] = total
            again[...] = total

    shape = jax.ShapeDtypeStruct(mine.shape[1:] if pair else mine.shape, mine.dtype)
    return order.call(
        body,
        (mine, other),
        [VMEM] * 2,
        out_shape=(shape, shape),
        out_specs=(VMEM,) * 2,
        name="add",
    )


def add_rounded(order, mine, other):
    def body(mine, other, out):
        out[...] = (mine[...] + other[...]).astype(jnp.bfloat16)

    return order.call(
        body,
        (mine, other),
        [VMEM] * 2,
        out_shape=jax.ShapeDtypeStruct(mine.shape, jnp.bfloat16),
        out_specs=VMEM,
        name="add_rounded",
    )


def arrange_tokens(order, place, own, slots):
    slab = BLOCK // 4
    rows = slots[0][0].shape[2]
    counts = [slot[0].shape[0] // HALF for slot in slots]
    total = (0 if own is None else 1) + sum(counts)

    def body(place, *refs):
        out = refs[-1]
        at = 0
        if own is not None:
            for i in range(HALF):
                block = device_block(place[0], place[1], i)
                columns = pl.ds(pl.multiple_of(block * BLOCK, BLOCK), BLOCK)
                out[i, :, 0:rows] = refs[0][:, columns].T
            refs = refs[1:]
            at = 1
        for n, count in enumerate(counts):
            for c in range(count):
                for i in range(HALF):
                    for k in range(4):
                        where = pl.multiple_of(jnp.bitwise_xor(place[2], k) * slab, slab)
                        out[i, pl.ds(where, slab), (at + c) * rows : (at + c + 1) * rows] = refs[
                            4 * n + k
                        ][HALF * c + i].astype(jnp.bfloat16)
            at += count

    arrays = [place] + ([] if own is None else [own]) + [piece for slot in slots for piece in slot]
    return order.call(
        body,
        arrays,
        [SMEM] + [VMEM] * (len(arrays) - 1),
        out_shape=jax.ShapeDtypeStruct((HALF, BLOCK, total * rows), jnp.bfloat16),
        out_specs=VMEM,
        name="arrange_tokens",
        vmem=20,
    )


def weight_part(order, place, tok, slots, scale=None, so_far=None):
    rows, chans = slots[0][0].shape[1:]
    count = len(slots)
    arrays = [a for slot in slots for a in slot if a is not None]

    def body(place, tok, *refs):
        out, held = refs[-2], refs[-1]
        level, column = place[0], place[1]
        i = pl.program_id(0)
        inside = jnp.logical_or(level == 1, level == 2)
        high = jnp.where(level <= 1, 0, 1)

        @pl.when(i == 0)
        def _():
            left = list(refs)
            for at, (streams, ends) in enumerate(slots):
                here = slice(at * rows, (at + 1) * rows)
                ref = left.pop(0)
                if streams.shape[0] == 3:
                    major = jnp.where(inside, level - 1 + column, 2 * high)
                    minor = 1
                else:
                    major = jnp.where(inside, column, high)
                    minor = 1 - high
                if ends is None:
                    held[0, here, :] = ref[major].astype(jnp.bfloat16)
                else:
                    end = left.pop(0)

                    @pl.when(inside)
                    def _():
                        held[0, here, :] = ref[major].astype(jnp.bfloat16)

                    @pl.when(jnp.logical_not(inside))
                    def _():
                        held[0, here, :] = end[0].astype(jnp.bfloat16)

                held[1, here, :] = ref[minor].astype(jnp.bfloat16)

        second = jnp.logical_or(
            jnp.logical_and(jnp.logical_and(level == 1, column == 0), i == 2),
            jnp.logical_and(jnp.logical_and(level == 2, column == 1), i == 0),
        )
        got = jnp.dot(
            tok[...], held[second.astype(jnp.int32)], preferred_element_type=jnp.float32
        )
        if so_far is not None:
            got = got + refs[-3][...]
        out[...] = got if scale is None else got * scale

    whole = lambda a: pl.BlockSpec(a.shape, lambda i: (0,) * a.ndim)
    more = [] if so_far is None else [so_far]
    part = pl.BlockSpec((BLOCK, chans), lambda i: (i, 0))
    return order.call(
        body,
        [place, tok] + arrays + more,
        [SMEM, pl.BlockSpec((None, BLOCK, count * rows), lambda i: (i, 0, 0))]
        + [whole(a) for a in arrays]
        + [part] * len(more),
        out_shape=jax.ShapeDtypeStruct((HALF * BLOCK, chans), jnp.float32),
        grid=(HALF,),
        out_specs=part,
        scratch_shapes=[pltpu.VMEM((2, count * rows, chans), jnp.bfloat16)],
        name="weight_part",
        vmem=58,
    )


def token_part(order, quarters, grads, weight):
    rows, chans = grads.shape[1:]
    wide = weight.shape[1] // 4
    count = quarters.shape[0]

    def body(quarters, grads, weight, out):
        now = lax.dot_general(
            grads[...], weight[...], (((1,), (1,)), ((), ())), preferred_element_type=jnp.float32
        )

        @pl.when(pl.program_id(1) == 0)
        def _():
            out[...] = now

        @pl.when(pl.program_id(1) > 0)
        def _():
            out[...] += now

    return order.call(
        body,
        (grads, weight),
        [
            pl.BlockSpec((None, rows, chans), lambda i, s, quarters: (s, 0, 0)),
            pl.BlockSpec((None, wide, chans), lambda i, s, quarters: (s, quarters[i], 0)),
        ],
        scalars=(quarters,),
        out_shape=jax.ShapeDtypeStruct((count, rows, wide), jnp.float32),
        grid=(count, 3),
        out_specs=pl.BlockSpec((None, rows, wide), lambda i, s, quarters: (i, 0, 0)),
        name="token_part",
        vmem=50,
    )


def lined(tokens, in_weight, kernel, out_grad):
    rows = tokens.shape[0]
    rep, quarter = lax.axis_index("rep"), lax.axis_index("shard")
    level, column = rep // 2, rep % 2
    place = jnp.stack([level, column, quarter]).astype(jnp.int32)
    scale = 1.0 / math.sqrt(rows * lax.axis_size("rep"))
    order = Order()
    quarters = [jnp.bitwise_xor(quarter, k).astype(jnp.int32) for k in (3, 1, 2, 0)]
    piece = turn_tokens(order, place, tokens)
    near = lines(piece, PAIRS)
    mid = lines(piece, MIDDLE)
    own, taps, first_out, inner_out, middle_out = gate(
        order, place, tokens, in_weight, kernel, out_grad
    )
    own_y = flipped(inner_out, "rep", 1)
    inner = lines(inner_out, INWARD)
    first = lines(first_out, PAIRS)
    middle = lines(middle_out, MIDDLE)
    taps1 = flipped(taps, "rep", 1)
    near = order.wait(near)
    far = lines(near, MIDDLE)
    over = column_blocks(order, place, [(piece, None), (near, None)], False)
    got1 = flipped(over, "rep", 1)
    send = token_part(order, jnp.stack(quarters[:2]), own, in_weight)
    summed = flipped(send, "shard", 1)
    mid = order.wait(mid)
    outer2 = lines(part_of(order, place, mid, BLOCKS - OWN, OWN), OUTWARD)
    inner, own_y, far = order.wait(inner, own_y, far)
    keep = token_part(order, jnp.stack(quarters[2:]), own, in_weight)
    outer3 = lines(part_of(order, place, far, BLOCKS - OWN, OWN), OUTWARD)
    outer2 = order.wait(outer2)
    over = column_blocks(order, place, [(mid, outer2)], False)
    got2 = flipped(over, "rep", 1)
    first = order.wait(first)
    relay, side1 = relay_payload(order, place, first, inner)
    relayed = lines(relay, MIDDLE)
    side1 = flipped(side1, "rep", 1)
    middle, got1 = order.wait(middle, got1)
    middle_end = lines(part_of(order, place, middle, 1, 1), OUTWARD)
    own1 = column_blocks(order, place, [(near, None)], True, got1, (0, OWN))
    across1 = flipped(own1, "shard", 2)
    beside1 = flipped(own1, "shard", 1)
    outer3 = order.wait(outer3)
    over = column_blocks(order, place, [(far, outer3)], False)
    got3 = flipped(over, "rep", 1)
    summed, got2 = order.wait(summed, got2)
    own2 = column_blocks(order, place, [(mid, outer2)], True, got2, (0, HALF))
    across2 = flipped(own2, "shard", 2)
    beside2 = flipped(own2, "shard", 1)
    relayed = order.wait(relayed)
    relayed_end = lines(part_of(order, place, relayed, 1, 1), OUTWARD)
    middle_end = order.wait(middle_end)
    side2 = flipped(side_payload(order, place, middle, middle_end), "rep", 1)
    across1, relayed_end = order.wait(across1, relayed_end)
    both1 = flipped(across1, "shard", 1)
    token_grad, away = add(order, keep, summed)
    last = flipped(away, "shard", 2)
    beside2, beside1, side1, across2, got3, taps1 = order.wait(
        beside2, beside1, side1, across2, got3, taps1
    )
    both2 = flipped(across2, "shard", 1)
    taps, taps_out = add(order, taps, taps1)
    taps2 = flipped(taps_out, "rep", 2)
    own3 = column_blocks(order, place, [(far, outer3)], True, got3, (0, HALF))
    across3 = flipped(own3, "shard", 2)
    beside3 = flipped(own3, "shard", 1)
    both1 = order.wait(both1)
    tok = arrange_tokens(order, place, tokens, [(own1, beside1, across1, both1)])
    taps2 = order.wait(taps2)
    side3 = flipped(side_payload(order, place, relayed, relayed_end), "rep", 1)
    early = [(own, None), (inner, first), (own_y, None), (side1, None)]
    so_far = weight_part(order, place, tok, early)
    beside3, across3, side2, both2 = order.wait(beside3, across3, side2, both2)
    both3 = flipped(across3, "shard", 1)
    taps, taps_out = add(order, taps, taps2)
    taps4 = flipped(taps_out, "rep", 4)
    both3 = order.wait(both3)
    late = [(own2, beside2, across2, both2), (own3, beside3, across3, both3)]
    tok = arrange_tokens(order, place, None, late)
    side3 = order.wait(side3)
    late = [(middle, middle_end), (side2, None), (relayed, relayed_end), (side3, None)]
    weight_grad = weight_part(order, place, tok, late, scale, so_far)
    last = order.wait(last)
    token_grad = add_rounded(order, token_grad, last)
    taps4 = order.wait(taps4)
    taps, _ = add(order, taps, taps4, scale=scale)
    return (token_grad, weight_grad, taps)


def solution(mesh):
    placed = (P("rep", None), P(None, None, "shard"), P(None, None, "shard"), P("rep", "shard"))
    line = mesh.shape["rep"] == 2 * LEVELS and mesh.shape["shard"] == 4
    return jax.shard_map(
        lined if line else plain,
        mesh=mesh,
        in_specs=placed,
        out_specs=(P("rep", "shard"), P("rep", "shard"), P(None, None, "shard")),
        check_vma=False,
    )
```

```python
import functools
import math

import jax
import jax.numpy as jnp
from jax import lax
from jax.experimental import pallas as pl
from jax.experimental.pallas import tpu as pltpu
from jax.sharding import PartitionSpec as P

SEQ = 128


def causal_mix(values, kernel):
    width = kernel.shape[0]
    length = values.shape[1]
    padded = jnp.pad(values, ((0, 0), (width - 1, 0), (0, 0), (0, 0)))
    total = jnp.zeros_like(values)
    for offset in range(width):
        total = total + kernel[offset] * padded[:, width - 1 - offset : width - 1 - offset + length]
    return total


def causal_mix_back(grads, kernel):
    width = kernel.shape[0]
    length = grads.shape[1]
    padded = jnp.pad(grads, ((0, 0), (0, width - 1), (0, 0), (0, 0)))
    total = jnp.zeros_like(grads)
    for offset in range(width):
        total = total + kernel[offset] * padded[:, offset : offset + length]
    return total


def kernel_terms(values, grads, width):
    length = values.shape[1]
    padded = jnp.pad(values, ((0, 0), (width - 1, 0), (0, 0), (0, 0)))
    terms = []
    for offset in range(width):
        shifted = padded[:, width - 1 - offset : width - 1 - offset + length]
        terms.append(jnp.sum(shifted * grads, axis=(0, 1)))
    return jnp.stack(terms, axis=0)


def gated_grads(tokens, in_weight, kernel, out_grad):
    rows = tokens.shape[0]
    chans = in_weight.shape[2]
    mixed = jnp.einsum("td,sdc->tsc", tokens, in_weight, preferred_element_type=jnp.float32)
    stored = lax.optimization_barrier(mixed.astype(jnp.bfloat16))
    values = stored.astype(jnp.float32).reshape(rows // SEQ, SEQ, 3, chans)
    conv = causal_mix(values, kernel)
    query = conv[:, :, 0]
    keyed = conv[:, :, 1]
    valued = conv[:, :, 2]
    upstream = out_grad.astype(jnp.float32).reshape(rows // SEQ, SEQ, chans)
    conv_grad = jnp.stack(
        [upstream * keyed * valued, upstream * query * valued, upstream * query * keyed], axis=2
    )
    mixed_grad = causal_mix_back(conv_grad, kernel).reshape(rows, 3, chans)
    return mixed_grad, kernel_terms(values, conv_grad, kernel.shape[0])


def plain(tokens, in_weight, kernel, out_grad):
    features = tokens.shape[1]
    chans = in_weight.shape[2]
    scale = 1.0 / math.sqrt(tokens.shape[0] * lax.axis_size("rep"))
    wide_grad, taps = gated_grads(tokens, in_weight, kernel, out_grad)
    mixed_grad = wide_grad.astype(jnp.bfloat16)
    partial_grad = jnp.einsum(
        "tsc,sdc->td", mixed_grad, in_weight, preferred_element_type=jnp.float32
    )
    token_grad = lax.psum_scatter(partial_grad, "shard", scatter_dimension=1, tiled=True).astype(
        jnp.bfloat16
    )
    local_grad = (
        jnp.einsum("td,tsc->sdc", tokens, mixed_grad, preferred_element_type=jnp.float32) * scale
    )
    weight_grad = lax.psum_scatter(
        local_grad.reshape(3 * features, chans), "rep", scatter_dimension=0, tiled=True
    )
    kernel_grad = lax.psum(taps * scale, "rep")
    return (token_grad, weight_grad, kernel_grad)


LEVELS = 4
BLOCK = 512
BLOCKS = 8
OWN = 6
HALF = 3
LANES = 128
VMEM = pl.BlockSpec(memory_space=pltpu.VMEM)
SMEM = pl.BlockSpec(memory_space=pltpu.SMEM)
ANY = pl.BlockSpec(memory_space=pl.ANY)
NOTHING = pl.CostEstimate(flops=128, bytes_accessed=128, transcendentals=0)
PAIRS = ((0, 1), (1, 0), (2, 3), (3, 2))
INWARD = ((0, 1), (3, 2))
MIDDLE = ((1, 2), (2, 1))
OUTWARD = ((1, 0), (2, 3))


class Order:
    def __init__(self):
        self.after = []

    def call(self, body, arrays, in_specs, *, out_shape, out_specs, scalars=(), grid=(), scratch_shapes=(), name, vmem=10):
        held, count = len(scalars), len(arrays)
        after = [a for a in self.after if not any(a is b for b in arrays)]

        def short(*refs):
            body(*refs[: held + count], *refs[held + count + len(after) :])

        result = pl.pallas_call(
            short,
            out_shape=out_shape,
            grid_spec=pltpu.PrefetchScalarGridSpec(
                num_scalar_prefetch=held,
                grid=grid,
                in_specs=list(in_specs) + [ANY] * len(after),
                out_specs=out_specs,
                scratch_shapes=scratch_shapes,
            ),
            compiler_params=pltpu.CompilerParams(vmem_limit_bytes=vmem * 2**20),
            cost_estimate=NOTHING,
            name=name,
        )(*scalars, *arrays, *after)
        self.after = [result[0] if isinstance(result, (list, tuple)) else result]
        return result

    def wait(self, *arrays):
        self.after.extend(arrays)
        return arrays[0] if len(arrays) == 1 else arrays


def lines(array, hops):
    perm = [(2 * a + y, 2 * b + y) for a, b in hops for y in range(2)]
    return lax.ppermute(array, "rep", perm)


def flipped(array, axis, flip):
    return lax.ppermute(array, axis, [(r, r ^ flip) for r in range(lax.axis_size(axis))])


def device_block(level, column, i):
    return lax.rem(OWN * level + HALF * column + i, BLOCKS)


def turn_tokens(order, place, tokens):
    rows = tokens.shape[0]
    slab = BLOCK // 4

    def body(place, tokens, piece, theirs):
        start = pl.multiple_of(place[2] * slab, slab)
        for b in range(BLOCKS):
            piece[b] = tokens[:, pl.ds(pl.multiple_of(BLOCK * b + start, slab), slab)].astype(
                jnp.float32
            ).T
        for i in range(HALF):
            theirs[i] = piece[device_block(place[0], 1 - place[1], i)]

    return order.call(
        body,
        (place, tokens),
        [SMEM, VMEM],
        out_shape=(
            jax.ShapeDtypeStruct((BLOCKS, slab, rows), jnp.float32),
            jax.ShapeDtypeStruct((HALF, slab, rows), jnp.float32),
        ),
        out_specs=(VMEM, VMEM),
        name="turn_tokens",
    )


def column_blocks(order, place, slots, own, *got):
    arrays = [a for slot in slots for a in slot if a is not None]
    extra = sum(a.shape[0] for a in got)
    first = slots[0][0]
    count = HALF * len(slots)

    def body(place, *refs):
        out = refs[-1]
        left = list(refs)
        column = place[1] if own else 1 - place[1]
        inside = jnp.logical_or(place[0] == 1, place[0] == 2)
        for n, (_, ends) in enumerate(slots):
            inner = left.pop(0)
            end = None if ends is None else left.pop(0)
            for i in range(HALF):
                block = device_block(place[0], column, i)
                if end is None:
                    out[HALF * n + i] = inner[block]
                    continue

                @pl.when(inside)
                def _():
                    out[HALF * n + i] = inner[block]

                @pl.when(jnp.logical_not(inside))
                def _():
                    out[HALF * n + i] = end[HALF * column + i]

        at = count
        for ref in left[: len(got)]:
            out[at : at + ref.shape[0]] = ref[...]
            at += ref.shape[0]

    return order.call(
        body,
        [place] + arrays + list(got),
        [SMEM] + [VMEM] * (len(arrays) + len(got)),
        out_shape=jax.ShapeDtypeStruct((count + extra,) + first.shape[1:], first.dtype),
        out_specs=VMEM,
        name="own_blocks" if own else "other_blocks",
    )


def gate(order, place, tokens, in_weight, kernel, out_grad):
    rows, features = tokens.shape
    chans = in_weight.shape[2]
    taps = kernel.shape[0]
    steps = 4
    width = min(chans, 2 * LANES)
    deep = features // steps
    pad = 8

    def body(place, tokens, weight, kernel, out_grad, own, stored, grad, first, inner, middle, total, held, pads, back):
        step = pl.program_id(1)
        for s in range(3):
            now = jnp.dot(tokens[...], weight[s], preferred_element_type=jnp.float32)

            @pl.when(step == 0)
            def _():
                total[s] = now

            @pl.when(step > 0)
            def _():
                total[s] += now

        @pl.when(step == steps - 1)
        def _():
            blank = jnp.zeros((pad, LANES), jnp.float32)
            for lane in range(0, width, LANES):
                lanes = slice(lane, lane + LANES)
                for q in range(rows // SEQ):
                    here = slice(q * SEQ, (q + 1) * SEQ)
                    conv = []
                    for s in range(3):
                        stored[s, here, lanes] = total[s, here, lanes].astype(jnp.bfloat16)
                        values = stored[s, here, lanes].astype(jnp.float32)
                        pads[s, 0:pad, :] = blank
                        pads[s, pad : pad + SEQ, :] = values
                        mix = kernel[0, s : s + 1, lanes] * values
                        for j in range(1, taps):
                            mix += kernel[j, s : s + 1, lanes] * pads[s, pad - j : pad - j + SEQ, :]
                        conv.append(mix)
                    up = out_grad[here, lanes].astype(jnp.float32)
                    query, keyed, valued = conv
                    grads = (up * keyed * valued, up * query * valued, up * query * keyed)
                    for s in range(3):
                        back[s, 0:SEQ, :] = grads[s]
                        grad[s, here, lanes] = grads[s]
                        back[s, SEQ : SEQ + pad, :] = blank
                    for s in range(3):
                        mixed = None
                        for j in range(taps):
                            term = kernel[j, s : s + 1, lanes] * back[s, j : j + SEQ, :]
                            mixed = term if mixed is None else mixed + term
                        held[s, here, lanes] = mixed
            for s in range(3):
                own[s] = held[s].astype(jnp.bfloat16)
            level = place[0]
            first[0] = held[2 - 2 * lax.rem(level, 2)]
            low = jnp.where(level <= 1, 0, 1)
            for i in range(2):
                inner[i] = held[low + i]
                middle[i] = held[1 - low + i]

    one = jax.ShapeDtypeStruct((1, rows, chans), jnp.float32)
    two = jax.ShapeDtypeStruct((2, rows, chans), jnp.float32)
    return order.call(
        body,
        (place, tokens, in_weight, kernel, out_grad),
        [
            SMEM,
            pl.BlockSpec((rows, deep), lambda c, k: (0, k)),
            pl.BlockSpec((3, deep, width), lambda c, k: (0, k, c)),
            pl.BlockSpec((taps, 3, width), lambda c, k: (0, 0, c)),
            pl.BlockSpec((rows, width), lambda c, k: (0, c)),
        ],
        out_shape=(
            jax.ShapeDtypeStruct((3, rows, chans), jnp.bfloat16),
            jax.ShapeDtypeStruct((3, rows, chans), jnp.bfloat16),
            jax.ShapeDtypeStruct((3, rows, chans), jnp.float32),
            one,
            two,
            two,
        ),
        grid=(chans // width, steps),
        out_specs=(
            pl.BlockSpec((3, rows, width), lambda c, k: (0, 0, c)),
            pl.BlockSpec((3, rows, width), lambda c, k: (0, 0, c)),
            pl.BlockSpec((3, rows, width), lambda c, k: (0, 0, c)),
            pl.BlockSpec((1, rows, width), lambda c, k: (0, 0, c)),
            pl.BlockSpec((2, rows, width), lambda c, k: (0, 0, c)),
            pl.BlockSpec((2, rows, width), lambda c, k: (0, 0, c)),
        ),
        scratch_shapes=[
            pltpu.VMEM((3, rows, width), jnp.float32),
            pltpu.VMEM((3, rows, width), jnp.float32),
            pltpu.VMEM((3, pad + SEQ, LANES), jnp.float32),
            pltpu.VMEM((3, SEQ + pad, LANES), jnp.float32),
        ],
        name="gate",
        vmem=50,
    )


def tap_part(order, stored, grads, taps):
    rows, chans = grads.shape[1:]
    pad = 8

    def body(stored, grads, out, back):
        for s in range(3):
            sums = [None] * taps
            for q in range(rows // SEQ):
                here = slice(q * SEQ, (q + 1) * SEQ)
                values = stored[s, here, :].astype(jnp.float32)
                back[0:SEQ, :] = grads[s, here, :]
                back[SEQ : SEQ + pad, :] = jnp.zeros((pad, LANES), jnp.float32)
                for j in range(taps):
                    term = values * back[j : j + SEQ, :]
                    folded = jnp.sum(term.reshape(SEQ // 8, 8, LANES), axis=0)
                    sums[j] = folded if q == 0 else sums[j] + folded
            for j in range(taps):
                out[j, s : s + 1, :] = jnp.sum(sums[j], axis=0, keepdims=True)

    part = pl.BlockSpec((3, rows, LANES), lambda c: (0, 0, c))
    return order.call(
        body,
        (stored, grads),
        [part, part],
        out_shape=jax.ShapeDtypeStruct((taps, 3, chans), jnp.float32),
        grid=(chans // LANES,),
        out_specs=pl.BlockSpec((taps, 3, LANES), lambda c: (0, 0, c)),
        scratch_shapes=[pltpu.VMEM((SEQ + pad, LANES), jnp.float32)],
        name="tap_part",
    )


def relay_payload(order, place, first, inner):
    def body(place, first, inner, out, side):
        @pl.when(place[0] <= 1)
        def _():
            out[0] = inner[1]
            out[1] = first[0]

        @pl.when(place[0] > 1)
        def _():
            out[0] = first[0]
            out[1] = inner[0]

        level_own(place, inner, first, side)

    two = jax.ShapeDtypeStruct(inner.shape, inner.dtype)
    return order.call(
        body,
        (place, first, inner),
        [SMEM, VMEM, VMEM],
        out_shape=(two, two),
        out_specs=(VMEM, VMEM),
        name="relay_payload",
    )


def level_own(place, inner, ends, out):
    inside = jnp.logical_or(place[0] == 1, place[0] == 2)

    @pl.when(inside)
    def _():
        out[...] = inner[...]

    @pl.when(jnp.logical_not(inside))
    def _():
        out[jnp.where(place[0] == 0, 0, 1)] = ends[0]
        out[jnp.where(place[0] == 0, 1, 0)] = ends[0]


def side_payload(order, place, inner, ends):
    return order.call(
        level_own,
        (place, inner, ends),
        [SMEM, VMEM, VMEM],
        out_shape=jax.ShapeDtypeStruct(inner.shape, inner.dtype),
        out_specs=VMEM,
        name="side_payload",
    )


def part_of(order, place, array, step, count):
    def body(place, array, out):
        start = jnp.where(place[0] <= 1, 0, step)
        for i in range(count):
            out[i] = array[start + i]

    return order.call(
        body,
        (place, array),
        [SMEM, VMEM],
        out_shape=jax.ShapeDtypeStruct((count,) + array.shape[1:], array.dtype),
        out_specs=VMEM,
        name="part_of",
    )


def add(order, mine, other, scale=1.0):
    pair = mine.ndim == 3 and mine.shape[0] == 2

    def body(mine, other, out, again):
        if pair:
            out[...] = mine[1] + other[1]
            again[...] = mine[0] + other[0]
        else:
            total = (mine[...] + other[...]) * scale
            out[...] = total
            again[...] = total

    shape = jax.ShapeDtypeStruct(mine.shape[1:] if pair else mine.shape, mine.dtype)
    return order.call(
        body,
        (mine, other),
        [VMEM] * 2,
        out_shape=(shape, shape),
        out_specs=(VMEM,) * 2,
        name="add",
    )


def add_rounded(order, mine, other):
    def body(mine, other, out):
        out[...] = (mine[...] + other[...]).astype(jnp.bfloat16)

    return order.call(
        body,
        (mine, other),
        [VMEM] * 2,
        out_shape=jax.ShapeDtypeStruct(mine.shape, jnp.bfloat16),
        out_specs=VMEM,
        name="add_rounded",
    )


def arrange_tokens(order, place, own, slots):
    slab = BLOCK // 4
    rows = slots[0][0].shape[2]
    counts = [slot[0].shape[0] // HALF for slot in slots]
    total = (0 if own is None else 1) + sum(counts)

    def body(place, *refs):
        out = refs[-1]
        at = 0
        if own is not None:
            for i in range(HALF):
                block = device_block(place[0], place[1], i)
                columns = pl.ds(pl.multiple_of(block * BLOCK, BLOCK), BLOCK)
                out[i, :, 0:rows] = refs[0][:, columns].T
            refs = refs[1:]
            at = 1
        for n, count in enumerate(counts):
            for c in range(count):
                for i in range(HALF):
                    for k in range(4):
                        where = pl.multiple_of(jnp.bitwise_xor(place[2], k) * slab, slab)
                        out[i, pl.ds(where, slab), (at + c) * rows : (at + c + 1) * rows] = refs[
                            4 * n + k
                        ][HALF * c + i].astype(jnp.bfloat16)
            at += count

    arrays = [place] + ([] if own is None else [own]) + [piece for slot in slots for piece in slot]
    return order.call(
        body,
        arrays,
        [SMEM] + [VMEM] * (len(arrays) - 1),
        out_shape=jax.ShapeDtypeStruct((HALF, BLOCK, total * rows), jnp.bfloat16),
        out_specs=VMEM,
        name="arrange_tokens",
        vmem=20,
    )


def weight_part(order, place, tok, slots, scale=None, so_far=None):
    rows, chans = slots[0][0].shape[1:]
    count = len(slots)
    arrays = [a for slot in slots for a in slot if a is not None]

    def body(place, tok, *refs):
        out, held = refs[-2], refs[-1]
        level, column = place[0], place[1]
        i = pl.program_id(0)
        inside = jnp.logical_or(level == 1, level == 2)
        high = jnp.where(level <= 1, 0, 1)

        @pl.when(i == 0)
        def _():
            left = list(refs)
            for at, (streams, ends) in enumerate(slots):
                here = slice(at * rows, (at + 1) * rows)
                ref = left.pop(0)
                if streams.shape[0] == 3:
                    major = jnp.where(inside, level - 1 + column, 2 * high)
                    minor = 1
                else:
                    major = jnp.where(inside, column, high)
                    minor = 1 - high
                if ends is None:
                    held[0, here, :] = ref[major].astype(jnp.bfloat16)
                else:
                    end = left.pop(0)

                    @pl.when(inside)
                    def _():
                        held[0, here, :] = ref[major].astype(jnp.bfloat16)

                    @pl.when(jnp.logical_not(inside))
                    def _():
                        held[0, here, :] = end[0].astype(jnp.bfloat16)

                held[1, here, :] = ref[minor].astype(jnp.bfloat16)

        second = jnp.logical_or(
            jnp.logical_and(jnp.logical_and(level == 1, column == 0), i == 2),
            jnp.logical_and(jnp.logical_and(level == 2, column == 1), i == 0),
        )
        got = jnp.dot(
            tok[...], held[second.astype(jnp.int32)], preferred_element_type=jnp.float32
        )
        if so_far is not None:
            got = got + refs[-3][...]
        out[...] = got if scale is None else got * scale

    whole = lambda a: pl.BlockSpec(a.shape, lambda i: (0,) * a.ndim)
    more = [] if so_far is None else [so_far]
    part = pl.BlockSpec((BLOCK, chans), lambda i: (i, 0))
    return order.call(
        body,
        [place, tok] + arrays + more,
        [SMEM, pl.BlockSpec((None, BLOCK, count * rows), lambda i: (i, 0, 0))]
        + [whole(a) for a in arrays]
        + [part] * len(more),
        out_shape=jax.ShapeDtypeStruct((HALF * BLOCK, chans), jnp.float32),
        grid=(HALF,),
        out_specs=part,
        scratch_shapes=[pltpu.VMEM((2, count * rows, chans), jnp.bfloat16)],
        name="weight_part",
        vmem=58,
    )


def token_part(order, quarters, grads, weight):
    rows, chans = grads.shape[1:]
    wide = weight.shape[1] // 4
    count = quarters.shape[0]

    def body(quarters, grads, weight, out):
        now = lax.dot_general(
            grads[...], weight[...], (((1,), (1,)), ((), ())), preferred_element_type=jnp.float32
        )

        @pl.when(pl.program_id(1) == 0)
        def _():
            out[...] = now

        @pl.when(pl.program_id(1) > 0)
        def _():
            out[...] += now

    return order.call(
        body,
        (grads, weight),
        [
            pl.BlockSpec((None, rows, chans), lambda i, s, quarters: (s, 0, 0)),
            pl.BlockSpec((None, wide, chans), lambda i, s, quarters: (s, quarters[i], 0)),
        ],
        scalars=(quarters,),
        out_shape=jax.ShapeDtypeStruct((count, rows, wide), jnp.float32),
        grid=(count, 3),
        out_specs=pl.BlockSpec((None, rows, wide), lambda i, s, quarters: (i, 0, 0)),
        name="token_part",
        vmem=50,
    )


def lined(tokens, in_weight, kernel, out_grad):
    rows = tokens.shape[0]
    rep, quarter = lax.axis_index("rep"), lax.axis_index("shard")
    level, column = rep // 2, rep % 2
    place = jnp.stack([level, column, quarter]).astype(jnp.int32)
    scale = 1.0 / math.sqrt(rows * lax.axis_size("rep"))
    order = Order()
    quarters = [jnp.bitwise_xor(quarter, k).astype(jnp.int32) for k in (3, 1, 2, 0)]
    piece, theirs = turn_tokens(order, place, tokens)
    got0 = flipped(theirs, "rep", 1)
    near = lines(piece, PAIRS)
    mid = lines(piece, MIDDLE)
    own, stored, grads, first_out, inner_out, middle_out = gate(
        order, place, tokens, in_weight, kernel, out_grad
    )
    own_y = flipped(inner_out, "rep", 1)
    inner = lines(inner_out, INWARD)
    first = lines(first_out, PAIRS)
    middle = lines(middle_out, MIDDLE)
    near = order.wait(near)
    far = lines(near, MIDDLE)
    over = column_blocks(order, place, [(near, None)], False)
    got1 = flipped(over, "rep", 1)
    mid = order.wait(mid)
    outer2 = lines(part_of(order, place, mid, BLOCKS - OWN, OWN), OUTWARD)
    send = token_part(order, jnp.stack(quarters[:2]), own, in_weight)
    summed = flipped(send, "shard", 1)
    own_y, inner, far = order.wait(own_y, inner, far)
    keep = token_part(order, jnp.stack(quarters[2:]), own, in_weight)
    outer3 = lines(part_of(order, place, far, BLOCKS - OWN, OWN), OUTWARD)
    outer2 = order.wait(outer2)
    over = column_blocks(order, place, [(mid, outer2)], False)
    got2 = flipped(over, "rep", 1)
    first = order.wait(first)
    relay, side1 = relay_payload(order, place, first, inner)
    relayed = lines(relay, MIDDLE)
    side1 = flipped(side1, "rep", 1)
    middle = order.wait(middle)
    middle_end = lines(part_of(order, place, middle, 1, 1), OUTWARD)
    got0, got1 = order.wait(got0, got1)
    own1 = column_blocks(order, place, [(near, None)], True, got0, got1)
    across1 = flipped(own1, "shard", 2)
    beside1 = flipped(own1, "shard", 1)
    summed, got2 = order.wait(summed, got2)
    own2 = column_blocks(order, place, [(mid, outer2)], True, got2)
    across2 = flipped(own2, "shard", 2)
    beside2 = flipped(own2, "shard", 1)
    outer3 = order.wait(outer3)
    over = column_blocks(order, place, [(far, outer3)], False)
    got3 = flipped(over, "rep", 1)
    taps = tap_part(order, stored, grads, kernel.shape[0])
    taps1 = flipped(taps, "rep", 1)
    relayed = order.wait(relayed)
    relayed_end = lines(part_of(order, place, relayed, 1, 1), OUTWARD)
    relayed_end, middle_end = order.wait(relayed_end, middle_end)
    side2 = flipped(side_payload(order, place, middle, middle_end), "rep", 1)
    token_grad, away = add(order, keep, summed)
    last = flipped(away, "shard", 2)
    beside2, across1, beside1, side1, got3, taps1 = order.wait(
        beside2, across1, beside1, side1, got3, taps1
    )
    both1 = flipped(across1, "shard", 1)
    taps, taps_out = add(order, taps, taps1)
    taps2 = flipped(taps_out, "rep", 2)
    across2 = order.wait(across2)
    both2 = flipped(across2, "shard", 1)
    own3 = column_blocks(order, place, [(far, outer3)], True, got3)
    across3 = flipped(own3, "shard", 2)
    beside3 = flipped(own3, "shard", 1)
    both1 = order.wait(both1)
    tok = arrange_tokens(order, place, tokens, [(own1, beside1, across1, both1)])
    taps2 = order.wait(taps2)
    side3 = flipped(side_payload(order, place, relayed, relayed_end), "rep", 1)
    early = [(own, None), (inner, first), (own_y, None), (side1, None)]
    so_far = weight_part(order, place, tok, early)
    side2, beside3, across3, both2 = order.wait(side2, beside3, across3, both2)
    both3 = flipped(across3, "shard", 1)
    taps, taps_out = add(order, taps, taps2)
    taps4 = flipped(taps_out, "rep", 4)
    both3 = order.wait(both3)
    late = [(own2, beside2, across2, both2), (own3, beside3, across3, both3)]
    tok = arrange_tokens(order, place, None, late)
    taps4 = order.wait(taps4)
    taps, _ = add(order, taps, taps4, scale=scale)
    side3, last = order.wait(side3, last)
    token_grad = add_rounded(order, token_grad, last)
    late = [(middle, middle_end), (side2, None), (relayed, relayed_end), (side3, None)]
    weight_grad = weight_part(order, place, tok, late, scale, so_far)
    return (token_grad, weight_grad, taps)


def solution(mesh):
    placed = (P("rep", None), P(None, None, "shard"), P(None, None, "shard"), P("rep", "shard"))
    line = mesh.shape["rep"] == 2 * LEVELS and mesh.shape["shard"] == 4
    return jax.shard_map(
        lined if line else plain,
        mesh=mesh,
        in_specs=placed,
        out_specs=(P("rep", "shard"), P("rep", "shard"), P(None, None, "shard")),
        check_vma=False,
    )
```

```python
import functools
import math

import jax
import jax.numpy as jnp
from jax import lax
from jax.experimental import pallas as pl
from jax.experimental.pallas import tpu as pltpu
from jax.sharding import PartitionSpec as P

SEQ = 128


def causal_mix(values, kernel):
    width = kernel.shape[0]
    length = values.shape[1]
    padded = jnp.pad(values, ((0, 0), (width - 1, 0), (0, 0), (0, 0)))
    total = jnp.zeros_like(values)
    for offset in range(width):
        total = total + kernel[offset] * padded[:, width - 1 - offset : width - 1 - offset + length]
    return total


def causal_mix_back(grads, kernel):
    width = kernel.shape[0]
    length = grads.shape[1]
    padded = jnp.pad(grads, ((0, 0), (0, width - 1), (0, 0), (0, 0)))
    total = jnp.zeros_like(grads)
    for offset in range(width):
        total = total + kernel[offset] * padded[:, offset : offset + length]
    return total


def kernel_terms(values, grads, width):
    length = values.shape[1]
    padded = jnp.pad(values, ((0, 0), (width - 1, 0), (0, 0), (0, 0)))
    terms = []
    for offset in range(width):
        shifted = padded[:, width - 1 - offset : width - 1 - offset + length]
        terms.append(jnp.sum(shifted * grads, axis=(0, 1)))
    return jnp.stack(terms, axis=0)


def gated_grads(tokens, in_weight, kernel, out_grad):
    rows = tokens.shape[0]
    chans = in_weight.shape[2]
    mixed = jnp.einsum("td,sdc->tsc", tokens, in_weight, preferred_element_type=jnp.float32)
    stored = lax.optimization_barrier(mixed.astype(jnp.bfloat16))
    values = stored.astype(jnp.float32).reshape(rows // SEQ, SEQ, 3, chans)
    conv = causal_mix(values, kernel)
    query = conv[:, :, 0]
    keyed = conv[:, :, 1]
    valued = conv[:, :, 2]
    upstream = out_grad.astype(jnp.float32).reshape(rows // SEQ, SEQ, chans)
    conv_grad = jnp.stack(
        [upstream * keyed * valued, upstream * query * valued, upstream * query * keyed], axis=2
    )
    mixed_grad = causal_mix_back(conv_grad, kernel).reshape(rows, 3, chans)
    return mixed_grad, kernel_terms(values, conv_grad, kernel.shape[0])


def plain(tokens, in_weight, kernel, out_grad):
    features = tokens.shape[1]
    chans = in_weight.shape[2]
    scale = 1.0 / math.sqrt(tokens.shape[0] * lax.axis_size("rep"))
    wide_grad, taps = gated_grads(tokens, in_weight, kernel, out_grad)
    mixed_grad = wide_grad.astype(jnp.bfloat16)
    partial_grad = jnp.einsum(
        "tsc,sdc->td", mixed_grad, in_weight, preferred_element_type=jnp.float32
    )
    token_grad = lax.psum_scatter(partial_grad, "shard", scatter_dimension=1, tiled=True).astype(
        jnp.bfloat16
    )
    local_grad = (
        jnp.einsum("td,tsc->sdc", tokens, mixed_grad, preferred_element_type=jnp.float32) * scale
    )
    weight_grad = lax.psum_scatter(
        local_grad.reshape(3 * features, chans), "rep", scatter_dimension=0, tiled=True
    )
    kernel_grad = lax.psum(taps * scale, "rep")
    return (token_grad, weight_grad, kernel_grad)


LEVELS = 4
BLOCK = 512
BLOCKS = 8
OWN = 6
HALF = 3
LANES = 128
VMEM = pl.BlockSpec(memory_space=pltpu.VMEM)
SMEM = pl.BlockSpec(memory_space=pltpu.SMEM)
ANY = pl.BlockSpec(memory_space=pl.ANY)
NOTHING = pl.CostEstimate(flops=128, bytes_accessed=128, transcendentals=0)
PAIRS = ((0, 1), (1, 0), (2, 3), (3, 2))
INWARD = ((0, 1), (3, 2))
MIDDLE = ((1, 2), (2, 1))
OUTWARD = ((1, 0), (2, 3))


class Order:
    def __init__(self):
        self.after = []

    def call(self, body, arrays, in_specs, *, out_shape, out_specs, scalars=(), grid=(), scratch_shapes=(), name, vmem=10):
        held, count = len(scalars), len(arrays)
        after = [a for a in self.after if not any(a is b for b in arrays)]

        def short(*refs):
            body(*refs[: held + count], *refs[held + count + len(after) :])

        result = pl.pallas_call(
            short,
            out_shape=out_shape,
            grid_spec=pltpu.PrefetchScalarGridSpec(
                num_scalar_prefetch=held,
                grid=grid,
                in_specs=list(in_specs) + [ANY] * len(after),
                out_specs=out_specs,
                scratch_shapes=scratch_shapes,
            ),
            compiler_params=pltpu.CompilerParams(vmem_limit_bytes=vmem * 2**20),
            cost_estimate=NOTHING,
            name=name,
        )(*scalars, *arrays, *after)
        self.after = [result[0] if isinstance(result, (list, tuple)) else result]
        return result

    def wait(self, *arrays):
        self.after.extend(arrays)
        return arrays[0] if len(arrays) == 1 else arrays


def lines(array, hops):
    perm = [(2 * a + y, 2 * b + y) for a, b in hops for y in range(2)]
    return lax.ppermute(array, "rep", perm)


def flipped(array, axis, flip):
    return lax.ppermute(array, axis, [(r, r ^ flip) for r in range(lax.axis_size(axis))])


def device_block(level, column, i):
    return lax.rem(OWN * level + HALF * column + i, BLOCKS)


def turn_tokens(order, place, tokens):
    rows = tokens.shape[0]
    slab = BLOCK // 4

    def body(place, tokens, piece, theirs):
        start = pl.multiple_of(place[2] * slab, slab)
        for b in range(BLOCKS):
            piece[b] = tokens[:, pl.ds(pl.multiple_of(BLOCK * b + start, slab), slab)].astype(
                jnp.float32
            ).T
        for i in range(HALF):
            theirs[i] = piece[device_block(place[0], 1 - place[1], i)]

    return order.call(
        body,
        (place, tokens),
        [SMEM, VMEM],
        out_shape=(
            jax.ShapeDtypeStruct((BLOCKS, slab, rows), jnp.float32),
            jax.ShapeDtypeStruct((HALF, slab, rows), jnp.float32),
        ),
        out_specs=(VMEM, VMEM),
        name="turn_tokens",
    )


def column_blocks(order, place, slots, own, *got):
    arrays = [a for slot in slots for a in slot if a is not None]
    extra = sum(a.shape[0] for a in got)
    first = slots[0][0]
    count = HALF * len(slots)

    def body(place, *refs):
        out = refs[-1]
        left = list(refs)
        column = place[1] if own else 1 - place[1]
        inside = jnp.logical_or(place[0] == 1, place[0] == 2)
        for n, (_, ends) in enumerate(slots):
            inner = left.pop(0)
            end = None if ends is None else left.pop(0)
            for i in range(HALF):
                block = device_block(place[0], column, i)
                if end is None:
                    out[HALF * n + i] = inner[block]
                    continue

                @pl.when(inside)
                def _():
                    out[HALF * n + i] = inner[block]

                @pl.when(jnp.logical_not(inside))
                def _():
                    out[HALF * n + i] = end[HALF * column + i]

        at = count
        for ref in left[: len(got)]:
            out[at : at + ref.shape[0]] = ref[...]
            at += ref.shape[0]

    return order.call(
        body,
        [place] + arrays + list(got),
        [SMEM] + [VMEM] * (len(arrays) + len(got)),
        out_shape=jax.ShapeDtypeStruct((count + extra,) + first.shape[1:], first.dtype),
        out_specs=VMEM,
        name="own_blocks" if own else "other_blocks",
    )


def gate(order, place, tokens, in_weight, kernel, out_grad):
    rows, features = tokens.shape
    chans = in_weight.shape[2]
    taps = kernel.shape[0]
    steps = 2
    width = min(chans, 2 * LANES)
    deep = features // steps
    pad = 8

    def body(place, tokens, weight, kernel, out_grad, own, stored, grad, first, inner, middle, total, held, pads, back):
        step = pl.program_id(1)
        for s in range(3):
            now = jnp.dot(tokens[...], weight[s], preferred_element_type=jnp.float32)

            @pl.when(step == 0)
            def _():
                total[s] = now

            @pl.when(step > 0)
            def _():
                total[s] += now

        @pl.when(step == steps - 1)
        def _():
            blank = jnp.zeros((pad, LANES), jnp.float32)
            for lane in range(0, width, LANES):
                lanes = slice(lane, lane + LANES)
                for q in range(rows // SEQ):
                    here = slice(q * SEQ, (q + 1) * SEQ)
                    conv = []
                    for s in range(3):
                        stored[s, here, lanes] = total[s, here, lanes].astype(jnp.bfloat16)
                        values = stored[s, here, lanes].astype(jnp.float32)
                        pads[s, 0:pad, :] = blank
                        pads[s, pad : pad + SEQ, :] = values
                        mix = kernel[0, s : s + 1, lanes] * values
                        for j in range(1, taps):
                            mix += kernel[j, s : s + 1, lanes] * pads[s, pad - j : pad - j + SEQ, :]
                        conv.append(mix)
                    up = out_grad[here, lanes].astype(jnp.float32)
                    query, keyed, valued = conv
                    grads = (up * keyed * valued, up * query * valued, up * query * keyed)
                    for s in range(3):
                        back[s, 0:SEQ, :] = grads[s]
                        grad[s, here, lanes] = grads[s]
                        back[s, SEQ : SEQ + pad, :] = blank
                    for s in range(3):
                        mixed = None
                        for j in range(taps):
                            term = kernel[j, s : s + 1, lanes] * back[s, j : j + SEQ, :]
                            mixed = term if mixed is None else mixed + term
                        held[s, here, lanes] = mixed
            for s in range(3):
                own[s] = held[s].astype(jnp.bfloat16)
            level = place[0]
            first[0] = held[2 - 2 * lax.rem(level, 2)]
            low = jnp.where(level <= 1, 0, 1)
            for i in range(2):
                inner[i] = held[low + i]
                middle[i] = held[1 - low + i]

    one = jax.ShapeDtypeStruct((1, rows, chans), jnp.float32)
    two = jax.ShapeDtypeStruct((2, rows, chans), jnp.float32)
    return order.call(
        body,
        (place, tokens, in_weight, kernel, out_grad),
        [
            SMEM,
            pl.BlockSpec((rows, deep), lambda c, k: (0, k)),
            pl.BlockSpec((3, deep, width), lambda c, k: (0, k, c)),
            pl.BlockSpec((taps, 3, width), lambda c, k: (0, 0, c)),
            pl.BlockSpec((rows, width), lambda c, k: (0, c)),
        ],
        out_shape=(
            jax.ShapeDtypeStruct((3, rows, chans), jnp.bfloat16),
            jax.ShapeDtypeStruct((3, rows, chans), jnp.bfloat16),
            jax.ShapeDtypeStruct((3, rows, chans), jnp.float32),
            one,
            two,
            two,
        ),
        grid=(chans // width, steps),
        out_specs=(
            pl.BlockSpec((3, rows, width), lambda c, k: (0, 0, c)),
            pl.BlockSpec((3, rows, width), lambda c, k: (0, 0, c)),
            pl.BlockSpec((3, rows, width), lambda c, k: (0, 0, c)),
            pl.BlockSpec((1, rows, width), lambda c, k: (0, 0, c)),
            pl.BlockSpec((2, rows, width), lambda c, k: (0, 0, c)),
            pl.BlockSpec((2, rows, width), lambda c, k: (0, 0, c)),
        ),
        scratch_shapes=[
            pltpu.VMEM((3, rows, width), jnp.float32),
            pltpu.VMEM((3, rows, width), jnp.float32),
            pltpu.VMEM((3, pad + SEQ, LANES), jnp.float32),
            pltpu.VMEM((3, SEQ + pad, LANES), jnp.float32),
        ],
        name="gate",
        vmem=50,
    )


def tap_part(order, stored, grads, taps):
    rows, chans = grads.shape[1:]
    pad = 8

    def body(stored, grads, out, back):
        for s in range(3):
            sums = [None] * taps
            for q in range(rows // SEQ):
                here = slice(q * SEQ, (q + 1) * SEQ)
                values = stored[s, here, :].astype(jnp.float32)
                back[0:SEQ, :] = grads[s, here, :]
                back[SEQ : SEQ + pad, :] = jnp.zeros((pad, LANES), jnp.float32)
                for j in range(taps):
                    term = values * back[j : j + SEQ, :]
                    folded = jnp.sum(term.reshape(SEQ // 8, 8, LANES), axis=0)
                    sums[j] = folded if q == 0 else sums[j] + folded
            for j in range(taps):
                out[j, s : s + 1, :] = jnp.sum(sums[j], axis=0, keepdims=True)

    part = pl.BlockSpec((3, rows, LANES), lambda c: (0, 0, c))
    return order.call(
        body,
        (stored, grads),
        [part, part],
        out_shape=jax.ShapeDtypeStruct((taps, 3, chans), jnp.float32),
        grid=(chans // LANES,),
        out_specs=pl.BlockSpec((taps, 3, LANES), lambda c: (0, 0, c)),
        scratch_shapes=[pltpu.VMEM((SEQ + pad, LANES), jnp.float32)],
        name="tap_part",
    )


def relay_payload(order, place, first, inner):
    def body(place, first, inner, out, side):
        @pl.when(place[0] <= 1)
        def _():
            out[0] = inner[1]
            out[1] = first[0]

        @pl.when(place[0] > 1)
        def _():
            out[0] = first[0]
            out[1] = inner[0]

        level_own(place, inner, first, side)

    two = jax.ShapeDtypeStruct(inner.shape, inner.dtype)
    return order.call(
        body,
        (place, first, inner),
        [SMEM, VMEM, VMEM],
        out_shape=(two, two),
        out_specs=(VMEM, VMEM),
        name="relay_payload",
    )


def level_own(place, inner, ends, out):
    inside = jnp.logical_or(place[0] == 1, place[0] == 2)

    @pl.when(inside)
    def _():
        out[...] = inner[...]

    @pl.when(jnp.logical_not(inside))
    def _():
        out[jnp.where(place[0] == 0, 0, 1)] = ends[0]
        out[jnp.where(place[0] == 0, 1, 0)] = ends[0]


def side_payload(order, place, inner, ends):
    return order.call(
        level_own,
        (place, inner, ends),
        [SMEM, VMEM, VMEM],
        out_shape=jax.ShapeDtypeStruct(inner.shape, inner.dtype),
        out_specs=VMEM,
        name="side_payload",
    )


def part_of(order, place, array, step, count):
    def body(place, array, out):
        start = jnp.where(place[0] <= 1, 0, step)
        for i in range(count):
            out[i] = array[start + i]

    return order.call(
        body,
        (place, array),
        [SMEM, VMEM],
        out_shape=jax.ShapeDtypeStruct((count,) + array.shape[1:], array.dtype),
        out_specs=VMEM,
        name="part_of",
    )


def add(order, mine, other, scale=1.0):
    pair = mine.ndim == 3 and mine.shape[0] == 2

    def body(mine, other, out, again):
        if pair:
            out[...] = mine[1] + other[1]
            again[...] = mine[0] + other[0]
        else:
            total = (mine[...] + other[...]) * scale
            out[...] = total
            again[...] = total

    shape = jax.ShapeDtypeStruct(mine.shape[1:] if pair else mine.shape, mine.dtype)
    return order.call(
        body,
        (mine, other),
        [VMEM] * 2,
        out_shape=(shape, shape),
        out_specs=(VMEM,) * 2,
        name="add",
    )


def add_rounded(order, mine, other):
    def body(mine, other, out):
        out[...] = (mine[...] + other[...]).astype(jnp.bfloat16)

    return order.call(
        body,
        (mine, other),
        [VMEM] * 2,
        out_shape=jax.ShapeDtypeStruct(mine.shape, jnp.bfloat16),
        out_specs=VMEM,
        name="add_rounded",
    )


def arrange_tokens(order, place, own, slots):
    slab = BLOCK // 4
    rows = slots[0][0].shape[2]
    counts = [slot[0].shape[0] // HALF for slot in slots]
    total = (0 if own is None else 1) + sum(counts)

    def body(place, *refs):
        out = refs[-1]
        at = 0
        if own is not None:
            for i in range(HALF):
                block = device_block(place[0], place[1], i)
                columns = pl.ds(pl.multiple_of(block * BLOCK, BLOCK), BLOCK)
                out[i, :, 0:rows] = refs[0][:, columns].T
            refs = refs[1:]
            at = 1
        for n, count in enumerate(counts):
            for c in range(count):
                for i in range(HALF):
                    for k in range(4):
                        where = pl.multiple_of(jnp.bitwise_xor(place[2], k) * slab, slab)
                        out[i, pl.ds(where, slab), (at + c) * rows : (at + c + 1) * rows] = refs[
                            4 * n + k
                        ][HALF * c + i].astype(jnp.bfloat16)
            at += count

    arrays = [place] + ([] if own is None else [own]) + [piece for slot in slots for piece in slot]
    return order.call(
        body,
        arrays,
        [SMEM] + [VMEM] * (len(arrays) - 1),
        out_shape=jax.ShapeDtypeStruct((HALF, BLOCK, total * rows), jnp.bfloat16),
        out_specs=VMEM,
        name="arrange_tokens",
        vmem=20,
    )


def weight_part(order, place, tok, slots, scale=None, so_far=None):
    rows, chans = slots[0][0].shape[1:]
    count = len(slots)
    arrays = [a for slot in slots for a in slot if a is not None]

    def body(place, tok, *refs):
        out, held = refs[-2], refs[-1]
        level, column = place[0], place[1]
        i = pl.program_id(0)
        inside = jnp.logical_or(level == 1, level == 2)
        high = jnp.where(level <= 1, 0, 1)

        @pl.when(i == 0)
        def _():
            left = list(refs)
            for at, (streams, ends) in enumerate(slots):
                here = slice(at * rows, (at + 1) * rows)
                ref = left.pop(0)
                if streams.shape[0] == 3:
                    major = jnp.where(inside, level - 1 + column, 2 * high)
                    minor = 1
                else:
                    major = jnp.where(inside, column, high)
                    minor = 1 - high
                if ends is None:
                    held[0, here, :] = ref[major].astype(jnp.bfloat16)
                else:
                    end = left.pop(0)

                    @pl.when(inside)
                    def _():
                        held[0, here, :] = ref[major].astype(jnp.bfloat16)

                    @pl.when(jnp.logical_not(inside))
                    def _():
                        held[0, here, :] = end[0].astype(jnp.bfloat16)

                held[1, here, :] = ref[minor].astype(jnp.bfloat16)

        second = jnp.logical_or(
            jnp.logical_and(jnp.logical_and(level == 1, column == 0), i == 2),
            jnp.logical_and(jnp.logical_and(level == 2, column == 1), i == 0),
        )
        got = jnp.dot(
            tok[...], held[second.astype(jnp.int32)], preferred_element_type=jnp.float32
        )
        if so_far is not None:
            got = got + refs[-3][...]
        out[...] = got if scale is None else got * scale

    whole = lambda a: pl.BlockSpec(a.shape, lambda i: (0,) * a.ndim)
    more = [] if so_far is None else [so_far]
    part = pl.BlockSpec((BLOCK, chans), lambda i: (i, 0))
    return order.call(
        body,
        [place, tok] + arrays + more,
        [SMEM, pl.BlockSpec((None, BLOCK, count * rows), lambda i: (i, 0, 0))]
        + [whole(a) for a in arrays]
        + [part] * len(more),
        out_shape=jax.ShapeDtypeStruct((HALF * BLOCK, chans), jnp.float32),
        grid=(HALF,),
        out_specs=part,
        scratch_shapes=[pltpu.VMEM((2, count * rows, chans), jnp.bfloat16)],
        name="weight_part",
        vmem=58,
    )


def token_part(order, quarters, grads, weight):
    rows, chans = grads.shape[1:]
    wide = weight.shape[1] // 4
    count = quarters.shape[0]

    def body(quarters, grads, weight, out):
        now = lax.dot_general(
            grads[...], weight[...], (((1,), (1,)), ((), ())), preferred_element_type=jnp.float32
        )

        @pl.when(pl.program_id(1) == 0)
        def _():
            out[...] = now

        @pl.when(pl.program_id(1) > 0)
        def _():
            out[...] += now

    return order.call(
        body,
        (grads, weight),
        [
            pl.BlockSpec((None, rows, chans), lambda i, s, quarters: (s, 0, 0)),
            pl.BlockSpec((None, wide, chans), lambda i, s, quarters: (s, quarters[i], 0)),
        ],
        scalars=(quarters,),
        out_shape=jax.ShapeDtypeStruct((count, rows, wide), jnp.float32),
        grid=(count, 3),
        out_specs=pl.BlockSpec((None, rows, wide), lambda i, s, quarters: (i, 0, 0)),
        name="token_part",
        vmem=50,
    )


def lined(tokens, in_weight, kernel, out_grad):
    rows = tokens.shape[0]
    rep, quarter = lax.axis_index("rep"), lax.axis_index("shard")
    level, column = rep // 2, rep % 2
    place = jnp.stack([level, column, quarter]).astype(jnp.int32)
    scale = 1.0 / math.sqrt(rows * lax.axis_size("rep"))
    order = Order()
    quarters = [jnp.bitwise_xor(quarter, k).astype(jnp.int32) for k in (3, 1, 2, 0)]
    piece, theirs = turn_tokens(order, place, tokens)
    got0 = flipped(theirs, "rep", 1)
    near = lines(piece, PAIRS)
    mid = lines(piece, MIDDLE)
    own, stored, grads, first_out, inner_out, middle_out = gate(
        order, place, tokens, in_weight, kernel, out_grad
    )
    own_y = flipped(inner_out, "rep", 1)
    inner = lines(inner_out, INWARD)
    first = lines(first_out, PAIRS)
    middle = lines(middle_out, MIDDLE)
    near, mid = order.wait(near, mid)
    far = lines(near, MIDDLE)
    send = token_part(order, jnp.stack(quarters[:2]), own, in_weight)
    summed = flipped(send, "shard", 1)
    outer2 = lines(part_of(order, place, mid, BLOCKS - OWN, OWN), OUTWARD)
    own_y, inner = order.wait(own_y, inner)
    over = column_blocks(order, place, [(near, None)], False)
    got1 = flipped(over, "rep", 1)
    far = order.wait(far)
    keep = token_part(order, jnp.stack(quarters[2:]), own, in_weight)
    outer3 = lines(part_of(order, place, far, BLOCKS - OWN, OWN), OUTWARD)
    outer2 = order.wait(outer2)
    over = column_blocks(order, place, [(mid, outer2)], False)
    got2 = flipped(over, "rep", 1)
    first = order.wait(first)
    relay, side1 = relay_payload(order, place, first, inner)
    relayed = lines(relay, MIDDLE)
    side1 = flipped(side1, "rep", 1)
    middle = order.wait(middle)
    middle_end = lines(part_of(order, place, middle, 1, 1), OUTWARD)
    got0, got1 = order.wait(got0, got1)
    own1 = column_blocks(order, place, [(near, None)], True, got0, got1)
    across1 = flipped(own1, "shard", 2)
    beside1 = flipped(own1, "shard", 1)
    summed, outer3, got2 = order.wait(summed, outer3, got2)
    own2 = column_blocks(order, place, [(mid, outer2)], True, got2)
    across2 = flipped(own2, "shard", 2)
    beside2 = flipped(own2, "shard", 1)
    over = column_blocks(order, place, [(far, outer3)], False)
    got3 = flipped(over, "rep", 1)
    taps = tap_part(order, stored, grads, kernel.shape[0])
    taps1 = flipped(taps, "rep", 1)
    relayed = order.wait(relayed)
    relayed_end = lines(part_of(order, place, relayed, 1, 1), OUTWARD)
    across1, relayed_end, middle_end = order.wait(across1, relayed_end, middle_end)
    both1 = flipped(across1, "shard", 1)
    side2 = flipped(side_payload(order, place, middle, middle_end), "rep", 1)
    token_grad, away = add(order, keep, summed)
    last = flipped(away, "shard", 2)
    beside2, beside1, side1, got3, taps1, across2 = order.wait(
        beside2, beside1, side1, got3, taps1, across2
    )
    both2 = flipped(across2, "shard", 1)
    own3 = column_blocks(order, place, [(far, outer3)], True, got3)
    across3 = flipped(own3, "shard", 2)
    beside3 = flipped(own3, "shard", 1)
    both1 = order.wait(both1)
    tok = arrange_tokens(order, place, tokens, [(own1, beside1, across1, both1)])
    taps, taps_out = add(order, taps, taps1)
    taps2 = flipped(taps_out, "rep", 2)
    taps2 = order.wait(taps2)
    side3 = flipped(side_payload(order, place, relayed, relayed_end), "rep", 1)
    early = [(own, None), (inner, first), (own_y, None), (side1, None)]
    so_far = weight_part(order, place, tok, early)
    side2, beside3, across3, both2 = order.wait(side2, beside3, across3, both2)
    both3 = flipped(across3, "shard", 1)
    taps, taps_out = add(order, taps, taps2)
    taps4 = flipped(taps_out, "rep", 4)
    both3 = order.wait(both3)
    late = [(own2, beside2, across2, both2), (own3, beside3, across3, both3)]
    tok = arrange_tokens(order, place, None, late)
    side3, taps4 = order.wait(side3, taps4)
    taps, _ = add(order, taps, taps4, scale=scale)
    last = order.wait(last)
    token_grad = add_rounded(order, token_grad, last)
    late = [(middle, middle_end), (side2, None), (relayed, relayed_end), (side3, None)]
    weight_grad = weight_part(order, place, tok, late, scale, so_far)
    return (token_grad, weight_grad, taps)


def solution(mesh):
    placed = (P("rep", None), P(None, None, "shard"), P(None, None, "shard"), P("rep", "shard"))
    line = mesh.shape["rep"] == 2 * LEVELS and mesh.shape["shard"] == 4
    return jax.shard_map(
        lined if line else plain,
        mesh=mesh,
        in_specs=placed,
        out_specs=(P("rep", "shard"), P("rep", "shard"), P(None, None, "shard")),
        check_vma=False,
    )
```

```python
import functools
import math

import jax
import jax.numpy as jnp
from jax import lax
from jax.experimental import pallas as pl
from jax.experimental.pallas import tpu as pltpu
from jax.sharding import PartitionSpec as P

SEQ = 128


def causal_mix(values, kernel):
    width = kernel.shape[0]
    length = values.shape[1]
    padded = jnp.pad(values, ((0, 0), (width - 1, 0), (0, 0), (0, 0)))
    total = jnp.zeros_like(values)
    for offset in range(width):
        total = total + kernel[offset] * padded[:, width - 1 - offset : width - 1 - offset + length]
    return total


def causal_mix_back(grads, kernel):
    width = kernel.shape[0]
    length = grads.shape[1]
    padded = jnp.pad(grads, ((0, 0), (0, width - 1), (0, 0), (0, 0)))
    total = jnp.zeros_like(grads)
    for offset in range(width):
        total = total + kernel[offset] * padded[:, offset : offset + length]
    return total


def kernel_terms(values, grads, width):
    length = values.shape[1]
    padded = jnp.pad(values, ((0, 0), (width - 1, 0), (0, 0), (0, 0)))
    terms = []
    for offset in range(width):
        shifted = padded[:, width - 1 - offset : width - 1 - offset + length]
        terms.append(jnp.sum(shifted * grads, axis=(0, 1)))
    return jnp.stack(terms, axis=0)


def gated_grads(tokens, in_weight, kernel, out_grad):
    rows = tokens.shape[0]
    chans = in_weight.shape[2]
    mixed = jnp.einsum("td,sdc->tsc", tokens, in_weight, preferred_element_type=jnp.float32)
    stored = lax.optimization_barrier(mixed.astype(jnp.bfloat16))
    values = stored.astype(jnp.float32).reshape(rows // SEQ, SEQ, 3, chans)
    conv = causal_mix(values, kernel)
    query = conv[:, :, 0]
    keyed = conv[:, :, 1]
    valued = conv[:, :, 2]
    upstream = out_grad.astype(jnp.float32).reshape(rows // SEQ, SEQ, chans)
    conv_grad = jnp.stack(
        [upstream * keyed * valued, upstream * query * valued, upstream * query * keyed], axis=2
    )
    mixed_grad = causal_mix_back(conv_grad, kernel).reshape(rows, 3, chans)
    return mixed_grad, kernel_terms(values, conv_grad, kernel.shape[0])


def plain(tokens, in_weight, kernel, out_grad):
    features = tokens.shape[1]
    chans = in_weight.shape[2]
    scale = 1.0 / math.sqrt(tokens.shape[0] * lax.axis_size("rep"))
    wide_grad, taps = gated_grads(tokens, in_weight, kernel, out_grad)
    mixed_grad = wide_grad.astype(jnp.bfloat16)
    partial_grad = jnp.einsum(
        "tsc,sdc->td", mixed_grad, in_weight, preferred_element_type=jnp.float32
    )
    token_grad = lax.psum_scatter(partial_grad, "shard", scatter_dimension=1, tiled=True).astype(
        jnp.bfloat16
    )
    local_grad = (
        jnp.einsum("td,tsc->sdc", tokens, mixed_grad, preferred_element_type=jnp.float32) * scale
    )
    weight_grad = lax.psum_scatter(
        local_grad.reshape(3 * features, chans), "rep", scatter_dimension=0, tiled=True
    )
    kernel_grad = lax.psum(taps * scale, "rep")
    return (token_grad, weight_grad, kernel_grad)


LEVELS = 4
BLOCK = 512
BLOCKS = 8
OWN = 6
HALF = 3
LANES = 128
VMEM = pl.BlockSpec(memory_space=pltpu.VMEM)
SMEM = pl.BlockSpec(memory_space=pltpu.SMEM)
ANY = pl.BlockSpec(memory_space=pl.ANY)
NOTHING = pl.CostEstimate(flops=128, bytes_accessed=128, transcendentals=0)
PAIRS = ((0, 1), (1, 0), (2, 3), (3, 2))
INWARD = ((0, 1), (3, 2))
MIDDLE = ((1, 2), (2, 1))
OUTWARD = ((1, 0), (2, 3))


class Order:
    def __init__(self):
        self.after = []

    def call(self, body, arrays, in_specs, *, out_shape, out_specs, scalars=(), grid=(), scratch_shapes=(), name, vmem=10):
        held, count = len(scalars), len(arrays)
        after = [a for a in self.after if not any(a is b for b in arrays)]

        def short(*refs):
            body(*refs[: held + count], *refs[held + count + len(after) :])

        result = pl.pallas_call(
            short,
            out_shape=out_shape,
            grid_spec=pltpu.PrefetchScalarGridSpec(
                num_scalar_prefetch=held,
                grid=grid,
                in_specs=list(in_specs) + [ANY] * len(after),
                out_specs=out_specs,
                scratch_shapes=scratch_shapes,
            ),
            compiler_params=pltpu.CompilerParams(vmem_limit_bytes=vmem * 2**20),
            cost_estimate=NOTHING,
            name=name,
        )(*scalars, *arrays, *after)
        self.after = [result[0] if isinstance(result, (list, tuple)) else result]
        return result

    def wait(self, *arrays):
        self.after.extend(arrays)
        return arrays[0] if len(arrays) == 1 else arrays


def lines(array, hops):
    perm = [(2 * a + y, 2 * b + y) for a, b in hops for y in range(2)]
    return lax.ppermute(array, "rep", perm)


def flipped(array, axis, flip):
    return lax.ppermute(array, axis, [(r, r ^ flip) for r in range(lax.axis_size(axis))])


def device_block(level, column, i):
    return lax.rem(OWN * level + HALF * column + i, BLOCKS)


def turn_tokens(order, place, tokens):
    rows = tokens.shape[0]
    slab = BLOCK // 4

    def body(place, tokens, piece):
        start = pl.multiple_of(place[2] * slab, slab)
        for b in range(BLOCKS):
            piece[b] = tokens[:, pl.ds(pl.multiple_of(BLOCK * b + start, slab), slab)].astype(
                jnp.float32
            ).T

    return order.call(
        body,
        (place, tokens),
        [SMEM, VMEM],
        out_shape=jax.ShapeDtypeStruct((BLOCKS, slab, rows), jnp.float32),
        out_specs=VMEM,
        name="turn_tokens",
    )


def column_blocks(order, place, slots, own, got=None, part=(0, 0)):
    arrays = [a for slot in slots for a in slot if a is not None]
    begin, extra = part
    first = slots[0][0]
    count = HALF * len(slots)

    def body(place, *refs):
        out = refs[-1]
        left = list(refs)
        column = place[1] if own else 1 - place[1]
        inside = jnp.logical_or(place[0] == 1, place[0] == 2)
        for n, (_, ends) in enumerate(slots):
            inner = left.pop(0)
            end = None if ends is None else left.pop(0)
            for i in range(HALF):
                block = device_block(place[0], column, i)
                if end is None:
                    out[HALF * n + i] = inner[block]
                    continue

                @pl.when(inside)
                def _():
                    out[HALF * n + i] = inner[block]

                @pl.when(jnp.logical_not(inside))
                def _():
                    out[HALF * n + i] = end[HALF * column + i]

        for i in range(extra):
            out[count + i] = left[0][begin + i]

    return order.call(
        body,
        [place] + arrays + ([] if got is None else [got]),
        [SMEM] + [VMEM] * (len(arrays) + (extra > 0)),
        out_shape=jax.ShapeDtypeStruct((count + extra,) + first.shape[1:], first.dtype),
        out_specs=VMEM,
        name="own_blocks" if own else "other_blocks",
    )


def gate(order, place, tokens, in_weight, kernel, out_grad):
    rows, features = tokens.shape
    chans = in_weight.shape[2]
    taps = kernel.shape[0]
    steps = 2
    width = min(chans, 2 * LANES)
    deep = features // steps
    pad = 8

    def body(place, tokens, weight, kernel, out_grad, own, grad, first, inner, middle, total, held, pads, back):
        step = pl.program_id(1)
        for s in range(3):
            now = jnp.dot(tokens[...], weight[s], preferred_element_type=jnp.float32)

            @pl.when(step == 0)
            def _():
                total[s] = now

            @pl.when(step > 0)
            def _():
                total[s] += now

        @pl.when(step == steps - 1)
        def _():
            blank = jnp.zeros((pad, LANES), jnp.float32)
            for lane in range(0, width, LANES):
                lanes = slice(lane, lane + LANES)
                sums = [[None] * taps for _ in range(3)]
                for q in range(rows // SEQ):
                    here = slice(q * SEQ, (q + 1) * SEQ)
                    conv = []
                    for s in range(3):
                        values = total[s, here, lanes].astype(jnp.bfloat16).astype(jnp.float32)
                        pads[s, 0:pad, :] = blank
                        pads[s, pad : pad + SEQ, :] = values
                        mix = kernel[0, s : s + 1, lanes] * values
                        for j in range(1, taps):
                            mix += kernel[j, s : s + 1, lanes] * pads[s, pad - j : pad - j + SEQ, :]
                        conv.append(mix)
                    up = out_grad[here, lanes].astype(jnp.float32)
                    query, keyed, valued = conv
                    grads = (up * keyed * valued, up * query * valued, up * query * keyed)
                    for s in range(3):
                        back[s, 0:SEQ, :] = grads[s]
                        back[s, SEQ : SEQ + pad, :] = blank
                    for s in range(3):
                        values = pads[s, pad : pad + SEQ, :]
                        mixed = None
                        for j in range(taps):
                            moved = back[s, j : j + SEQ, :]
                            term = kernel[j, s : s + 1, lanes] * moved
                            mixed = term if mixed is None else mixed + term
                            folded = jnp.sum((values * moved).reshape(SEQ // 8, 8, LANES), axis=0)
                            sums[s][j] = folded if q == 0 else sums[s][j] + folded
                        held[s, here, lanes] = mixed
                for s in range(3):
                    for j in range(taps):
                        grad[j, s : s + 1, lanes] = jnp.sum(sums[s][j], axis=0, keepdims=True)
            for s in range(3):
                own[s] = held[s].astype(jnp.bfloat16)
            level = place[0]
            first[0] = held[2 - 2 * lax.rem(level, 2)]
            low = jnp.where(level <= 1, 0, 1)
            for i in range(2):
                inner[i] = held[low + i]
                middle[i] = held[1 - low + i]

    one = jax.ShapeDtypeStruct((1, rows, chans), jnp.float32)
    two = jax.ShapeDtypeStruct((2, rows, chans), jnp.float32)
    return order.call(
        body,
        (place, tokens, in_weight, kernel, out_grad),
        [
            SMEM,
            pl.BlockSpec((rows, deep), lambda c, k: (0, k)),
            pl.BlockSpec((3, deep, width), lambda c, k: (0, k, c)),
            pl.BlockSpec((taps, 3, width), lambda c, k: (0, 0, c)),
            pl.BlockSpec((rows, width), lambda c, k: (0, c)),
        ],
        out_shape=(
            jax.ShapeDtypeStruct((3, rows, chans), jnp.bfloat16),
            jax.ShapeDtypeStruct((taps, 3, chans), jnp.float32),
            one,
            two,
            two,
        ),
        grid=(chans // width, steps),
        out_specs=(
            pl.BlockSpec((3, rows, width), lambda c, k: (0, 0, c)),
            pl.BlockSpec((taps, 3, width), lambda c, k: (0, 0, c)),
            pl.BlockSpec((1, rows, width), lambda c, k: (0, 0, c)),
            pl.BlockSpec((2, rows, width), lambda c, k: (0, 0, c)),
            pl.BlockSpec((2, rows, width), lambda c, k: (0, 0, c)),
        ),
        scratch_shapes=[
            pltpu.VMEM((3, rows, width), jnp.float32),
            pltpu.VMEM((3, rows, width), jnp.float32),
            pltpu.VMEM((3, pad + SEQ, LANES), jnp.float32),
            pltpu.VMEM((3, SEQ + pad, LANES), jnp.float32),
        ],
        name="gate",
        vmem=50,
    )


def relay_payload(order, place, first, inner):
    def body(place, first, inner, out, side):
        @pl.when(place[0] <= 1)
        def _():
            out[0] = inner[1]
            out[1] = first[0]

        @pl.when(place[0] > 1)
        def _():
            out[0] = first[0]
            out[1] = inner[0]

        level_own(place, inner, first, side)

    two = jax.ShapeDtypeStruct(inner.shape, inner.dtype)
    return order.call(
        body,
        (place, first, inner),
        [SMEM, VMEM, VMEM],
        out_shape=(two, two),
        out_specs=(VMEM, VMEM),
        name="relay_payload",
    )


def level_own(place, inner, ends, out):
    inside = jnp.logical_or(place[0] == 1, place[0] == 2)

    @pl.when(inside)
    def _():
        out[...] = inner[...]

    @pl.when(jnp.logical_not(inside))
    def _():
        out[jnp.where(place[0] == 0, 0, 1)] = ends[0]
        out[jnp.where(place[0] == 0, 1, 0)] = ends[0]


def side_payload(order, place, inner, ends):
    return order.call(
        level_own,
        (place, inner, ends),
        [SMEM, VMEM, VMEM],
        out_shape=jax.ShapeDtypeStruct(inner.shape, inner.dtype),
        out_specs=VMEM,
        name="side_payload",
    )


def part_of(order, place, array, step, count):
    def body(place, array, out):
        start = jnp.where(place[0] <= 1, 0, step)
        for i in range(count):
            out[i] = array[start + i]

    return order.call(
        body,
        (place, array),
        [SMEM, VMEM],
        out_shape=jax.ShapeDtypeStruct((count,) + array.shape[1:], array.dtype),
        out_specs=VMEM,
        name="part_of",
    )


def add(order, mine, other, scale=1.0):
    pair = mine.ndim == 3 and mine.shape[0] == 2

    def body(mine, other, out, again):
        if pair:
            out[...] = mine[1] + other[1]
            again[...] = mine[0] + other[0]
        else:
            total = (mine[...] + other[...]) * scale
            out[...] = total
            again[...] = total

    shape = jax.ShapeDtypeStruct(mine.shape[1:] if pair else mine.shape, mine.dtype)
    return order.call(
        body,
        (mine, other),
        [VMEM] * 2,
        out_shape=(shape, shape),
        out_specs=(VMEM,) * 2,
        name="add",
    )


def add_rounded(order, mine, other):
    def body(mine, other, out):
        out[...] = (mine[...] + other[...]).astype(jnp.bfloat16)

    return order.call(
        body,
        (mine, other),
        [VMEM] * 2,
        out_shape=jax.ShapeDtypeStruct(mine.shape, jnp.bfloat16),
        out_specs=VMEM,
        name="add_rounded",
    )


def arrange_tokens(order, place, own, slots):
    slab = BLOCK // 4
    rows = slots[0][0].shape[2]
    counts = [slot[0].shape[0] // HALF for slot in slots]
    total = (0 if own is None else 1) + sum(counts)

    def body(place, *refs):
        out = refs[-1]
        at = 0
        if own is not None:
            for i in range(HALF):
                block = device_block(place[0], place[1], i)
                columns = pl.ds(pl.multiple_of(block * BLOCK, BLOCK), BLOCK)
                out[i, :, 0:rows] = refs[0][:, columns].T
            refs = refs[1:]
            at = 1
        for n, count in enumerate(counts):
            for c in range(count):
                for i in range(HALF):
                    for k in range(4):
                        where = pl.multiple_of(jnp.bitwise_xor(place[2], k) * slab, slab)
                        out[i, pl.ds(where, slab), (at + c) * rows : (at + c + 1) * rows] = refs[
                            4 * n + k
                        ][HALF * c + i].astype(jnp.bfloat16)
            at += count

    arrays = [place] + ([] if own is None else [own]) + [piece for slot in slots for piece in slot]
    return order.call(
        body,
        arrays,
        [SMEM] + [VMEM] * (len(arrays) - 1),
        out_shape=jax.ShapeDtypeStruct((HALF, BLOCK, total * rows), jnp.bfloat16),
        out_specs=VMEM,
        name="arrange_tokens",
        vmem=20,
    )


def weight_part(order, place, tok, slots, scale=None, so_far=None):
    rows, chans = slots[0][0].shape[1:]
    count = len(slots)
    arrays = [a for slot in slots for a in slot if a is not None]

    def body(place, tok, *refs):
        out, held = refs[-2], refs[-1]
        level, column = place[0], place[1]
        i = pl.program_id(0)
        inside = jnp.logical_or(level == 1, level == 2)
        high = jnp.where(level <= 1, 0, 1)

        @pl.when(i == 0)
        def _():
            left = list(refs)
            for at, (streams, ends) in enumerate(slots):
                here = slice(at * rows, (at + 1) * rows)
                ref = left.pop(0)
                if streams.shape[0] == 3:
                    major = jnp.where(inside, level - 1 + column, 2 * high)
                    minor = 1
                else:
                    major = jnp.where(inside, column, high)
                    minor = 1 - high
                if ends is None:
                    held[0, here, :] = ref[major].astype(jnp.bfloat16)
                else:
                    end = left.pop(0)

                    @pl.when(inside)
                    def _():
                        held[0, here, :] = ref[major].astype(jnp.bfloat16)

                    @pl.when(jnp.logical_not(inside))
                    def _():
                        held[0, here, :] = end[0].astype(jnp.bfloat16)

                held[1, here, :] = ref[minor].astype(jnp.bfloat16)

        second = jnp.logical_or(
            jnp.logical_and(jnp.logical_and(level == 1, column == 0), i == 2),
            jnp.logical_and(jnp.logical_and(level == 2, column == 1), i == 0),
        )
        got = jnp.dot(
            tok[...], held[second.astype(jnp.int32)], preferred_element_type=jnp.float32
        )
        if so_far is not None:
            got = got + refs[-3][...]
        out[...] = got if scale is None else got * scale

    whole = lambda a: pl.BlockSpec(a.shape, lambda i: (0,) * a.ndim)
    more = [] if so_far is None else [so_far]
    part = pl.BlockSpec((BLOCK, chans), lambda i: (i, 0))
    return order.call(
        body,
        [place, tok] + arrays + more,
        [SMEM, pl.BlockSpec((None, BLOCK, count * rows), lambda i: (i, 0, 0))]
        + [whole(a) for a in arrays]
        + [part] * len(more),
        out_shape=jax.ShapeDtypeStruct((HALF * BLOCK, chans), jnp.float32),
        grid=(HALF,),
        out_specs=part,
        scratch_shapes=[pltpu.VMEM((2, count * rows, chans), jnp.bfloat16)],
        name="weight_part",
        vmem=61,
    )


def token_part(order, quarters, grads, weight):
    rows, chans = grads.shape[1:]
    wide = weight.shape[1] // 4
    count = quarters.shape[0]

    def body(quarters, grads, weight, out):
        now = lax.dot_general(
            grads[...], weight[...], (((1,), (1,)), ((), ())), preferred_element_type=jnp.float32
        )

        @pl.when(pl.program_id(1) == 0)
        def _():
            out[...] = now

        @pl.when(pl.program_id(1) > 0)
        def _():
            out[...] += now

    return order.call(
        body,
        (grads, weight),
        [
            pl.BlockSpec((None, rows, chans), lambda i, s, quarters: (s, 0, 0)),
            pl.BlockSpec((None, wide, chans), lambda i, s, quarters: (s, quarters[i], 0)),
        ],
        scalars=(quarters,),
        out_shape=jax.ShapeDtypeStruct((count, rows, wide), jnp.float32),
        grid=(count, 3),
        out_specs=pl.BlockSpec((None, rows, wide), lambda i, s, quarters: (i, 0, 0)),
        name="token_part",
        vmem=50,
    )


def lined(tokens, in_weight, kernel, out_grad):
    rows = tokens.shape[0]
    rep, quarter = lax.axis_index("rep"), lax.axis_index("shard")
    level, column = rep // 2, rep % 2
    place = jnp.stack([level, column, quarter]).astype(jnp.int32)
    scale = 1.0 / math.sqrt(rows * lax.axis_size("rep"))
    order = Order()
    quarters = [jnp.bitwise_xor(quarter, k).astype(jnp.int32) for k in (3, 1, 2, 0)]
    piece = turn_tokens(order, place, tokens)
    near = lines(piece, PAIRS)
    mid = lines(piece, MIDDLE)
    own, taps, first_out, inner_out, middle_out = gate(
        order, place, tokens, in_weight, kernel, out_grad
    )
    own_y = flipped(inner_out, "rep", 1)
    inner = lines(inner_out, INWARD)
    first = lines(first_out, PAIRS)
    middle = lines(middle_out, MIDDLE)
    taps1 = flipped(taps, "rep", 1)
    near = order.wait(near)
    far = lines(near, MIDDLE)
    over = column_blocks(order, place, [(piece, None), (near, None)], False)
    got1 = flipped(over, "rep", 1)
    send = token_part(order, jnp.stack(quarters[:2]), own, in_weight)
    summed = flipped(send, "shard", 1)
    mid = order.wait(mid)
    outer2 = lines(part_of(order, place, mid, BLOCKS - OWN, OWN), OUTWARD)
    inner, own_y, far = order.wait(inner, own_y, far)
    keep = token_part(order, jnp.stack(quarters[2:]), own, in_weight)
    outer3 = lines(part_of(order, place, far, BLOCKS - OWN, OWN), OUTWARD)
    outer2 = order.wait(outer2)
    over = column_blocks(order, place, [(mid, outer2)], False)
    got2 = flipped(over, "rep", 1)
    first = order.wait(first)
    relay, side1 = relay_payload(order, place, first, inner)
    relayed = lines(relay, MIDDLE)
    side1 = flipped(side1, "rep", 1)
    middle, got1 = order.wait(middle, got1)
    middle_end = lines(part_of(order, place, middle, 1, 1), OUTWARD)
    own1 = column_blocks(order, place, [(near, None)], True, got1, (0, OWN))
    across1 = flipped(own1, "shard", 2)
    beside1 = flipped(own1, "shard", 1)
    outer3 = order.wait(outer3)
    over = column_blocks(order, place, [(far, outer3)], False)
    got3 = flipped(over, "rep", 1)
    summed, got2 = order.wait(summed, got2)
    own2 = column_blocks(order, place, [(mid, outer2)], True, got2, (0, HALF))
    across2 = flipped(own2, "shard", 2)
    beside2 = flipped(own2, "shard", 1)
    relayed = order.wait(relayed)
    relayed_end = lines(part_of(order, place, relayed, 1, 1), OUTWARD)
    middle_end = order.wait(middle_end)
    side2 = flipped(side_payload(order, place, middle, middle_end), "rep", 1)
    across1, relayed_end = order.wait(across1, relayed_end)
    both1 = flipped(across1, "shard", 1)
    token_grad, away = add(order, keep, summed)
    last = flipped(away, "shard", 2)
    beside2, beside1, side1, across2, got3, taps1 = order.wait(
        beside2, beside1, side1, across2, got3, taps1
    )
    both2 = flipped(across2, "shard", 1)
    taps, taps_out = add(order, taps, taps1)
    taps2 = flipped(taps_out, "rep", 2)
    own3 = column_blocks(order, place, [(far, outer3)], True, got3, (0, HALF))
    across3 = flipped(own3, "shard", 2)
    beside3 = flipped(own3, "shard", 1)
    both1 = order.wait(both1)
    tok = arrange_tokens(order, place, tokens, [(own1, beside1, across1, both1)])
    taps2 = order.wait(taps2)
    side3 = flipped(side_payload(order, place, relayed, relayed_end), "rep", 1)
    early = [(own, None), (inner, first), (own_y, None), (side1, None)]
    so_far = weight_part(order, place, tok, early)
    beside3, across3, side2, both2 = order.wait(beside3, across3, side2, both2)
    both3 = flipped(across3, "shard", 1)
    taps, taps_out = add(order, taps, taps2)
    taps4 = flipped(taps_out, "rep", 4)
    both3 = order.wait(both3)
    late = [(own2, beside2, across2, both2), (own3, beside3, across3, both3)]
    tok = arrange_tokens(order, place, None, late)
    side3 = order.wait(side3)
    late = [(middle, middle_end), (side2, None), (relayed, relayed_end), (side3, None)]
    weight_grad = weight_part(order, place, tok, late, scale, so_far)
    last = order.wait(last)
    token_grad = add_rounded(order, token_grad, last)
    taps4 = order.wait(taps4)
    taps, _ = add(order, taps, taps4, scale=scale)
    return (token_grad, weight_grad, taps)


def solution(mesh):
    placed = (P("rep", None), P(None, None, "shard"), P(None, None, "shard"), P("rep", "shard"))
    line = mesh.shape["rep"] == 2 * LEVELS and mesh.shape["shard"] == 4
    return jax.shard_map(
        lined if line else plain,
        mesh=mesh,
        in_specs=placed,
        out_specs=(P("rep", "shard"), P("rep", "shard"), P(None, None, "shard")),
        check_vma=False,
    )
```

```python
import functools
import math

import jax
import jax.numpy as jnp
from jax import lax
from jax.experimental import pallas as pl
from jax.experimental.pallas import tpu as pltpu
from jax.sharding import PartitionSpec as P

SEQ = 128


def causal_mix(values, kernel):
    width = kernel.shape[0]
    length = values.shape[1]
    padded = jnp.pad(values, ((0, 0), (width - 1, 0), (0, 0), (0, 0)))
    total = jnp.zeros_like(values)
    for offset in range(width):
        total = total + kernel[offset] * padded[:, width - 1 - offset : width - 1 - offset + length]
    return total


def causal_mix_back(grads, kernel):
    width = kernel.shape[0]
    length = grads.shape[1]
    padded = jnp.pad(grads, ((0, 0), (0, width - 1), (0, 0), (0, 0)))
    total = jnp.zeros_like(grads)
    for offset in range(width):
        total = total + kernel[offset] * padded[:, offset : offset + length]
    return total


def kernel_terms(values, grads, width):
    length = values.shape[1]
    padded = jnp.pad(values, ((0, 0), (width - 1, 0), (0, 0), (0, 0)))
    terms = []
    for offset in range(width):
        shifted = padded[:, width - 1 - offset : width - 1 - offset + length]
        terms.append(jnp.sum(shifted * grads, axis=(0, 1)))
    return jnp.stack(terms, axis=0)


def gated_grads(tokens, in_weight, kernel, out_grad):
    rows = tokens.shape[0]
    chans = in_weight.shape[2]
    mixed = jnp.einsum("td,sdc->tsc", tokens, in_weight, preferred_element_type=jnp.float32)
    stored = lax.optimization_barrier(mixed.astype(jnp.bfloat16))
    values = stored.astype(jnp.float32).reshape(rows // SEQ, SEQ, 3, chans)
    conv = causal_mix(values, kernel)
    query = conv[:, :, 0]
    keyed = conv[:, :, 1]
    valued = conv[:, :, 2]
    upstream = out_grad.astype(jnp.float32).reshape(rows // SEQ, SEQ, chans)
    conv_grad = jnp.stack(
        [upstream * keyed * valued, upstream * query * valued, upstream * query * keyed], axis=2
    )
    mixed_grad = causal_mix_back(conv_grad, kernel).reshape(rows, 3, chans)
    return mixed_grad, kernel_terms(values, conv_grad, kernel.shape[0])


def plain(tokens, in_weight, kernel, out_grad):
    features = tokens.shape[1]
    chans = in_weight.shape[2]
    scale = 1.0 / math.sqrt(tokens.shape[0] * lax.axis_size("rep"))
    wide_grad, taps = gated_grads(tokens, in_weight, kernel, out_grad)
    mixed_grad = wide_grad.astype(jnp.bfloat16)
    partial_grad = jnp.einsum(
        "tsc,sdc->td", mixed_grad, in_weight, preferred_element_type=jnp.float32
    )
    token_grad = lax.psum_scatter(partial_grad, "shard", scatter_dimension=1, tiled=True).astype(
        jnp.bfloat16
    )
    local_grad = (
        jnp.einsum("td,tsc->sdc", tokens, mixed_grad, preferred_element_type=jnp.float32) * scale
    )
    weight_grad = lax.psum_scatter(
        local_grad.reshape(3 * features, chans), "rep", scatter_dimension=0, tiled=True
    )
    kernel_grad = lax.psum(taps * scale, "rep")
    return (token_grad, weight_grad, kernel_grad)


LEVELS = 4
BLOCK = 512
BLOCKS = 8
OWN = 6
HALF = 3
LANES = 128
VMEM = pl.BlockSpec(memory_space=pltpu.VMEM)
SMEM = pl.BlockSpec(memory_space=pltpu.SMEM)
ANY = pl.BlockSpec(memory_space=pl.ANY)
NOTHING = pl.CostEstimate(flops=128, bytes_accessed=128, transcendentals=0)
PAIRS = ((0, 1), (1, 0), (2, 3), (3, 2))
INWARD = ((0, 1), (3, 2))
MIDDLE = ((1, 2), (2, 1))
OUTWARD = ((1, 0), (2, 3))


class Order:
    def __init__(self):
        self.after = []

    def call(self, body, arrays, in_specs, *, out_shape, out_specs, scalars=(), grid=(), scratch_shapes=(), name, vmem=10):
        held, count = len(scalars), len(arrays)
        after = [a for a in self.after if not any(a is b for b in arrays)]

        def short(*refs):
            body(*refs[: held + count], *refs[held + count + len(after) :])

        result = pl.pallas_call(
            short,
            out_shape=out_shape,
            grid_spec=pltpu.PrefetchScalarGridSpec(
                num_scalar_prefetch=held,
                grid=grid,
                in_specs=list(in_specs) + [ANY] * len(after),
                out_specs=out_specs,
                scratch_shapes=scratch_shapes,
            ),
            compiler_params=pltpu.CompilerParams(vmem_limit_bytes=vmem * 2**20),
            cost_estimate=NOTHING,
            name=name,
        )(*scalars, *arrays, *after)
        self.after = [result[0] if isinstance(result, (list, tuple)) else result]
        return result

    def wait(self, *arrays):
        self.after.extend(arrays)
        return arrays[0] if len(arrays) == 1 else arrays


def lines(array, hops):
    perm = [(2 * a + y, 2 * b + y) for a, b in hops for y in range(2)]
    return lax.ppermute(array, "rep", perm)


def flipped(array, axis, flip):
    return lax.ppermute(array, axis, [(r, r ^ flip) for r in range(lax.axis_size(axis))])


def device_block(level, column, i):
    return lax.rem(OWN * level + HALF * column + i, BLOCKS)


def turn_tokens(order, place, tokens):
    rows = tokens.shape[0]
    slab = BLOCK // 4

    def body(place, tokens, piece):
        piece[...] = tokens[...].astype(jnp.float32).T

    return order.call(
        body,
        (tokens,),
        [pl.BlockSpec((rows, slab), lambda b, place: (0, 4 * b + place[2]))],
        scalars=(place,),
        out_shape=jax.ShapeDtypeStruct((BLOCKS, slab, rows), jnp.float32),
        grid=(BLOCKS,),
        out_specs=pl.BlockSpec((None, slab, rows), lambda b, place: (b, 0, 0)),
        name="turn_tokens",
        vmem=62,
    )


def column_blocks(order, place, slots, own, got=None, part=(0, 0)):
    arrays = [a for slot in slots for a in slot if a is not None]
    begin, extra = part
    first = slots[0][0]
    count = HALF * len(slots)

    def body(place, *refs):
        out = refs[-1]
        left = list(refs)
        column = place[1] if own else 1 - place[1]
        inside = jnp.logical_or(place[0] == 1, place[0] == 2)
        for n, (_, ends) in enumerate(slots):
            inner = left.pop(0)
            end = None if ends is None else left.pop(0)
            for i in range(HALF):
                block = device_block(place[0], column, i)
                if end is None:
                    out[HALF * n + i] = inner[block]
                    continue

                @pl.when(inside)
                def _():
                    out[HALF * n + i] = inner[block]

                @pl.when(jnp.logical_not(inside))
                def _():
                    out[HALF * n + i] = end[HALF * column + i]

        for i in range(extra):
            out[count + i] = left[0][begin + i]

    return order.call(
        body,
        [place] + arrays + ([] if got is None else [got]),
        [SMEM] + [VMEM] * (len(arrays) + (extra > 0)),
        out_shape=jax.ShapeDtypeStruct((count + extra,) + first.shape[1:], first.dtype),
        out_specs=VMEM,
        name="own_blocks" if own else "other_blocks",
    )


def gate(order, place, tokens, in_weight, kernel, out_grad):
    rows, features = tokens.shape
    chans = in_weight.shape[2]
    taps = kernel.shape[0]
    steps = 4
    width = min(chans, 2 * LANES)
    deep = features // steps
    pad = 8

    def body(place, tokens, weight, kernel, out_grad, own, grad, first, inner, middle, total, held, pads, back):
        step = pl.program_id(1)
        for s in range(3):
            now = jnp.dot(tokens[...], weight[s], preferred_element_type=jnp.float32)

            @pl.when(step == 0)
            def _():
                total[s] = now

            @pl.when(step > 0)
            def _():
                total[s] += now

        @pl.when(step == steps - 1)
        def _():
            blank = jnp.zeros((pad, LANES), jnp.float32)
            for lane in range(0, width, LANES):
                lanes = slice(lane, lane + LANES)
                sums = [[None] * taps for _ in range(3)]
                for q in range(rows // SEQ):
                    here = slice(q * SEQ, (q + 1) * SEQ)
                    conv = []
                    for s in range(3):
                        values = total[s, here, lanes].astype(jnp.bfloat16).astype(jnp.float32)
                        pads[s, 0:pad, :] = blank
                        pads[s, pad : pad + SEQ, :] = values
                        mix = kernel[0, s : s + 1, lanes] * values
                        for j in range(1, taps):
                            mix += kernel[j, s : s + 1, lanes] * pads[s, pad - j : pad - j + SEQ, :]
                        conv.append(mix)
                    up = out_grad[here, lanes].astype(jnp.float32)
                    query, keyed, valued = conv
                    grads = (up * keyed * valued, up * query * valued, up * query * keyed)
                    for s in range(3):
                        back[s, 0:SEQ, :] = grads[s]
                        back[s, SEQ : SEQ + pad, :] = blank
                    for s in range(3):
                        values = pads[s, pad : pad + SEQ, :]
                        mixed = None
                        for j in range(taps):
                            moved = back[s, j : j + SEQ, :]
                            term = kernel[j, s : s + 1, lanes] * moved
                            mixed = term if mixed is None else mixed + term
                            folded = jnp.sum((values * moved).reshape(SEQ // 8, 8, LANES), axis=0)
                            sums[s][j] = folded if q == 0 else sums[s][j] + folded
                        held[s, here, lanes] = mixed
                for s in range(3):
                    for j in range(taps):
                        grad[j, s : s + 1, lanes] = jnp.sum(sums[s][j], axis=0, keepdims=True)
            for s in range(3):
                own[s] = held[s].astype(jnp.bfloat16)
            level = place[0]
            first[0] = held[2 - 2 * lax.rem(level, 2)]
            low = jnp.where(level <= 1, 0, 1)
            for i in range(2):
                inner[i] = held[low + i]
                middle[i] = held[1 - low + i]

    one = jax.ShapeDtypeStruct((1, rows, chans), jnp.float32)
    two = jax.ShapeDtypeStruct((2, rows, chans), jnp.float32)
    return order.call(
        body,
        (place, tokens, in_weight, kernel, out_grad),
        [
            SMEM,
            pl.BlockSpec((rows, deep), lambda c, k: (0, k)),
            pl.BlockSpec((3, deep, width), lambda c, k: (0, k, c)),
            pl.BlockSpec((taps, 3, width), lambda c, k: (0, 0, c)),
            pl.BlockSpec((rows, width), lambda c, k: (0, c)),
        ],
        out_shape=(
            jax.ShapeDtypeStruct((3, rows, chans), jnp.bfloat16),
            jax.ShapeDtypeStruct((taps, 3, chans), jnp.float32),
            one,
            two,
            two,
        ),
        grid=(chans // width, steps),
        out_specs=(
            pl.BlockSpec((3, rows, width), lambda c, k: (0, 0, c)),
            pl.BlockSpec((taps, 3, width), lambda c, k: (0, 0, c)),
            pl.BlockSpec((1, rows, width), lambda c, k: (0, 0, c)),
            pl.BlockSpec((2, rows, width), lambda c, k: (0, 0, c)),
            pl.BlockSpec((2, rows, width), lambda c, k: (0, 0, c)),
        ),
        scratch_shapes=[
            pltpu.VMEM((3, rows, width), jnp.float32),
            pltpu.VMEM((3, rows, width), jnp.float32),
            pltpu.VMEM((3, pad + SEQ, LANES), jnp.float32),
            pltpu.VMEM((3, SEQ + pad, LANES), jnp.float32),
        ],
        name="gate",
        vmem=50,
    )


def relay_payload(order, place, first, inner):
    def body(place, first, inner, out, side):
        @pl.when(place[0] <= 1)
        def _():
            out[0] = inner[1]
            out[1] = first[0]

        @pl.when(place[0] > 1)
        def _():
            out[0] = first[0]
            out[1] = inner[0]

        level_own(place, inner, first, side)

    two = jax.ShapeDtypeStruct(inner.shape, inner.dtype)
    return order.call(
        body,
        (place, first, inner),
        [SMEM, VMEM, VMEM],
        out_shape=(two, two),
        out_specs=(VMEM, VMEM),
        name="relay_payload",
    )


def level_own(place, inner, ends, out):
    inside = jnp.logical_or(place[0] == 1, place[0] == 2)

    @pl.when(inside)
    def _():
        out[...] = inner[...]

    @pl.when(jnp.logical_not(inside))
    def _():
        out[jnp.where(place[0] == 0, 0, 1)] = ends[0]
        out[jnp.where(place[0] == 0, 1, 0)] = ends[0]


def side_payload(order, place, inner, ends):
    return order.call(
        level_own,
        (place, inner, ends),
        [SMEM, VMEM, VMEM],
        out_shape=jax.ShapeDtypeStruct(inner.shape, inner.dtype),
        out_specs=VMEM,
        name="side_payload",
    )


def part_of(order, place, array, step, count):
    def body(place, array, out):
        start = jnp.where(place[0] <= 1, 0, step)
        for i in range(count):
            out[i] = array[start + i]

    return order.call(
        body,
        (place, array),
        [SMEM, VMEM],
        out_shape=jax.ShapeDtypeStruct((count,) + array.shape[1:], array.dtype),
        out_specs=VMEM,
        name="part_of",
    )


def add(order, mine, other, scale=1.0):
    pair = mine.ndim == 3 and mine.shape[0] == 2

    def body(mine, other, out, again):
        if pair:
            out[...] = mine[1] + other[1]
            again[...] = mine[0] + other[0]
        else:
            total = (mine[...] + other[...]) * scale
            out[...] = total
            again[...] = total

    shape = jax.ShapeDtypeStruct(mine.shape[1:] if pair else mine.shape, mine.dtype)
    return order.call(
        body,
        (mine, other),
        [VMEM] * 2,
        out_shape=(shape, shape),
        out_specs=(VMEM,) * 2,
        name="add",
    )


def add_rounded(order, mine, other):
    def body(mine, other, out):
        out[...] = (mine[...] + other[...]).astype(jnp.bfloat16)

    return order.call(
        body,
        (mine, other),
        [VMEM] * 2,
        out_shape=jax.ShapeDtypeStruct(mine.shape, jnp.bfloat16),
        out_specs=VMEM,
        name="add_rounded",
    )


def arrange_tokens(order, place, own, slots):
    slab = BLOCK // 4
    rows = slots[0][0].shape[2]
    counts = [slot[0].shape[0] // HALF for slot in slots]
    total = (0 if own is None else 1) + sum(counts)

    def body(place, *refs):
        out = refs[-1]
        at = 0
        if own is not None:
            for i in range(HALF):
                block = device_block(place[0], place[1], i)
                columns = pl.ds(pl.multiple_of(block * BLOCK, BLOCK), BLOCK)
                out[i, :, 0:rows] = refs[0][:, columns].T
            refs = refs[1:]
            at = 1
        for n, count in enumerate(counts):
            for c in range(count):
                for i in range(HALF):
                    for k in range(4):
                        where = pl.multiple_of(jnp.bitwise_xor(place[2], k) * slab, slab)
                        out[i, pl.ds(where, slab), (at + c) * rows : (at + c + 1) * rows] = refs[
                            4 * n + k
                        ][HALF * c + i].astype(jnp.bfloat16)
            at += count

    arrays = [place] + ([] if own is None else [own]) + [piece for slot in slots for piece in slot]
    return order.call(
        body,
        arrays,
        [SMEM] + [VMEM] * (len(arrays) - 1),
        out_shape=jax.ShapeDtypeStruct((HALF, BLOCK, total * rows), jnp.bfloat16),
        out_specs=VMEM,
        name="arrange_tokens",
        vmem=20,
    )


def weight_part(order, place, tok, slots, scale=None, so_far=None):
    rows, chans = slots[0][0].shape[1:]
    count = len(slots)
    arrays = [a for slot in slots for a in slot if a is not None]

    def body(place, tok, *refs):
        out, held = refs[-2], refs[-1]
        level, column = place[0], place[1]
        i = pl.program_id(0)
        inside = jnp.logical_or(level == 1, level == 2)
        high = jnp.where(level <= 1, 0, 1)

        @pl.when(i == 0)
        def _():
            left = list(refs)
            for at, (streams, ends) in enumerate(slots):
                here = slice(at * rows, (at + 1) * rows)
                ref = left.pop(0)
                if streams.shape[0] == 3:
                    major = jnp.where(inside, level - 1 + column, 2 * high)
                    minor = 1
                else:
                    major = jnp.where(inside, column, high)
                    minor = 1 - high
                if ends is None:
                    held[0, here, :] = ref[major].astype(jnp.bfloat16)
                else:
                    end = left.pop(0)

                    @pl.when(inside)
                    def _():
                        held[0, here, :] = ref[major].astype(jnp.bfloat16)

                    @pl.when(jnp.logical_not(inside))
                    def _():
                        held[0, here, :] = end[0].astype(jnp.bfloat16)

                held[1, here, :] = ref[minor].astype(jnp.bfloat16)

        second = jnp.logical_or(
            jnp.logical_and(jnp.logical_and(level == 1, column == 0), i == 2),
            jnp.logical_and(jnp.logical_and(level == 2, column == 1), i == 0),
        )
        got = jnp.dot(
            tok[...], held[second.astype(jnp.int32)], preferred_element_type=jnp.float32
        )
        if so_far is not None:
            got = got + refs[-3][...]
        out[...] = got if scale is None else got * scale

    whole = lambda a: pl.BlockSpec(a.shape, lambda i: (0,) * a.ndim)
    more = [] if so_far is None else [so_far]
    part = pl.BlockSpec((BLOCK, chans), lambda i: (i, 0))
    return order.call(
        body,
        [place, tok] + arrays + more,
        [SMEM, pl.BlockSpec((None, BLOCK, count * rows), lambda i: (i, 0, 0))]
        + [whole(a) for a in arrays]
        + [part] * len(more),
        out_shape=jax.ShapeDtypeStruct((HALF * BLOCK, chans), jnp.float32),
        grid=(HALF,),
        out_specs=part,
        scratch_shapes=[pltpu.VMEM((2, count * rows, chans), jnp.bfloat16)],
        name="weight_part",
        vmem=58,
    )


def token_part(order, quarters, grads, weight):
    rows, chans = grads.shape[1:]
    wide = weight.shape[1] // 4
    count = quarters.shape[0]

    def body(quarters, grads, weight, out):
        now = lax.dot_general(
            grads[...], weight[...], (((1,), (1,)), ((), ())), preferred_element_type=jnp.float32
        )

        @pl.when(pl.program_id(1) == 0)
        def _():
            out[...] = now

        @pl.when(pl.program_id(1) > 0)
        def _():
            out[...] += now

    return order.call(
        body,
        (grads, weight),
        [
            pl.BlockSpec((None, rows, chans), lambda i, s, quarters: (s, 0, 0)),
            pl.BlockSpec((None, wide, chans), lambda i, s, quarters: (s, quarters[i], 0)),
        ],
        scalars=(quarters,),
        out_shape=jax.ShapeDtypeStruct((count, rows, wide), jnp.float32),
        grid=(count, 3),
        out_specs=pl.BlockSpec((None, rows, wide), lambda i, s, quarters: (i, 0, 0)),
        name="token_part",
        vmem=50,
    )


def lined(tokens, in_weight, kernel, out_grad):
    rows = tokens.shape[0]
    rep, quarter = lax.axis_index("rep"), lax.axis_index("shard")
    level, column = rep // 2, rep % 2
    place = jnp.stack([level, column, quarter]).astype(jnp.int32)
    scale = 1.0 / math.sqrt(rows * lax.axis_size("rep"))
    order = Order()
    quarters = [jnp.bitwise_xor(quarter, k).astype(jnp.int32) for k in (3, 1, 2, 0)]
    piece = turn_tokens(order, place, tokens)
    near = lines(piece, PAIRS)
    mid = lines(piece, MIDDLE)
    own, taps, first_out, inner_out, middle_out = gate(
        order, place, tokens, in_weight, kernel, out_grad
    )
    own_y = flipped(inner_out, "rep", 1)
    inner = lines(inner_out, INWARD)
    first = lines(first_out, PAIRS)
    middle = lines(middle_out, MIDDLE)
    taps1 = flipped(taps, "rep", 1)
    near = order.wait(near)
    far = lines(near, MIDDLE)
    over = column_blocks(order, place, [(piece, None), (near, None)], False)
    got1 = flipped(over, "rep", 1)
    send = token_part(order, jnp.stack(quarters[:2]), own, in_weight)
    summed = flipped(send, "shard", 1)
    mid = order.wait(mid)
    outer2 = lines(part_of(order, place, mid, BLOCKS - OWN, OWN), OUTWARD)
    inner, own_y, far = order.wait(inner, own_y, far)
    keep = token_part(order, jnp.stack(quarters[2:]), own, in_weight)
    outer3 = lines(part_of(order, place, far, BLOCKS - OWN, OWN), OUTWARD)
    outer2 = order.wait(outer2)
    over = column_blocks(order, place, [(mid, outer2)], False)
    got2 = flipped(over, "rep", 1)
    first = order.wait(first)
    relay, side1 = relay_payload(order, place, first, inner)
    relayed = lines(relay, MIDDLE)
    side1 = flipped(side1, "rep", 1)
    middle, got1 = order.wait(middle, got1)
    middle_end = lines(part_of(order, place, middle, 1, 1), OUTWARD)
    own1 = column_blocks(order, place, [(near, None)], True, got1, (0, OWN))
    across1 = flipped(own1, "shard", 2)
    beside1 = flipped(own1, "shard", 1)
    outer3 = order.wait(outer3)
    over = column_blocks(order, place, [(far, outer3)], False)
    got3 = flipped(over, "rep", 1)
    summed, got2 = order.wait(summed, got2)
    own2 = column_blocks(order, place, [(mid, outer2)], True, got2, (0, HALF))
    across2 = flipped(own2, "shard", 2)
    beside2 = flipped(own2, "shard", 1)
    relayed = order.wait(relayed)
    relayed_end = lines(part_of(order, place, relayed, 1, 1), OUTWARD)
    middle_end = order.wait(middle_end)
    side2 = flipped(side_payload(order, place, middle, middle_end), "rep", 1)
    across1, relayed_end = order.wait(across1, relayed_end)
    both1 = flipped(across1, "shard", 1)
    token_grad, away = add(order, keep, summed)
    last = flipped(away, "shard", 2)
    beside2, beside1, side1, across2, got3, taps1 = order.wait(
        beside2, beside1, side1, across2, got3, taps1
    )
    both2 = flipped(across2, "shard", 1)
    taps, taps_out = add(order, taps, taps1)
    taps2 = flipped(taps_out, "rep", 2)
    own3 = column_blocks(order, place, [(far, outer3)], True, got3, (0, HALF))
    across3 = flipped(own3, "shard", 2)
    beside3 = flipped(own3, "shard", 1)
    both1 = order.wait(both1)
    tok = arrange_tokens(order, place, tokens, [(own1, beside1, across1, both1)])
    taps2 = order.wait(taps2)
    side3 = flipped(side_payload(order, place, relayed, relayed_end), "rep", 1)
    early = [(own, None), (inner, first), (own_y, None), (side1, None)]
    so_far = weight_part(order, place, tok, early)
    beside3, across3, side2, both2 = order.wait(beside3, across3, side2, both2)
    both3 = flipped(across3, "shard", 1)
    taps, taps_out = add(order, taps, taps2)
    taps4 = flipped(taps_out, "rep", 4)
    both3 = order.wait(both3)
    late = [(own2, beside2, across2, both2), (own3, beside3, across3, both3)]
    tok = arrange_tokens(order, place, None, late)
    side3 = order.wait(side3)
    late = [(middle, middle_end), (side2, None), (relayed, relayed_end), (side3, None)]
    weight_grad = weight_part(order, place, tok, late, scale, so_far)
    last = order.wait(last)
    token_grad = add_rounded(order, token_grad, last)
    taps4 = order.wait(taps4)
    taps, _ = add(order, taps, taps4, scale=scale)
    return (token_grad, weight_grad, taps)


def solution(mesh):
    placed = (P("rep", None), P(None, None, "shard"), P(None, None, "shard"), P("rep", "shard"))
    line = mesh.shape["rep"] == 2 * LEVELS and mesh.shape["shard"] == 4
    return jax.shard_map(
        lined if line else plain,
        mesh=mesh,
        in_specs=placed,
        out_specs=(P("rep", "shard"), P("rep", "shard"), P(None, None, "shard")),
        check_vma=False,
    )
```
